128 devices in a mesh: rows: 128 (over x, y, z, core).
Axes of the slice: x: 4, y: 4, z: 4, core: 2. Of those that a mesh axis runs over, the one named last changes fastest.
Arguments:
- vectors: bfloat16 [64, 131072], P(None, 'rows'), may hold values from -6 to 6
- diag_blocks: bfloat16 [512, 256, 256], P('rows')
- near_blocks: bfloat16 [16384, 256, 256], P('rows'), may hold values from -0.0625 to 0.0625
- near_rows: int32 [16384], P('rows'), may hold values from 0 to 511, as said below
- near_cols: int32 [16384], P('rows'), may hold values from 0 to 511, as said below
- far_left: bfloat16 [16384, 32, 256], P('rows'), may hold values from -1 to 1
- far_right: bfloat16 [16384, 32, 256], P('rows'), may hold values from -0.0625 to 0.0625
- far_rows: int32 [16384], P('rows'), may hold values from 0 to 511, as said below
- far_cols: int32 [16384], P('rows'), may hold values from 0 to 511, as said below
- counts: int32 [128, 2], P('rows'), may hold values from 16 to 128, as said below
Outputs:
- first_image: float32 [64, 131072], P(None, 'rows')
- second_image: float32 [64, 131072], P(None, 'rows')
The draws below stay inside these ranges and needn't reach their ends.
Inputs may be any that keep to these rules, and one draw needn't show every extreme that they name: `near_rows`: slot s belongs to device d = s // 128, and its row cluster lies on d: it is one of d * 4 to d * 4 + 3. `near_cols`: the column cluster of a slot of device d lies on device (d + e) mod 128, with e one of -6 to -1 and 1 to 6; all slots of device d, near and far, whose column clusters lie on one device name the same cluster. `far_rows`: as for near_rows, with device d = s // 128. `far_cols`: as for near_cols, and consistent with it: one cluster per pair of devices. counts[d, 0] is at most 128 and counts[d, 1] at most 128; some device uses all 128 near slots and some device all 128 far slots.
All inputs are finite; a program needn't handle non-finite values.
Results may differ from the reference program's by a relative error of at most 0.0024.
Values may be sent and summed in bfloat16 or wider, within the bound.
No kernel may reach another device: no remote copies, remote signals or barrier semaphores. Data moves between devices by JAX's collectives and lax.ppermute only.
A program may use at most 128 MiB of HBM per device.

```python
import jax
import jax.numpy as jnp
from jax import lax

B = 256
K = 32
RHS = 64
REACH = 6
CL_DEV = 4
NEAR_CAP = 128
FAR_CAP = 128
CLUSTERS = 512
PANELS = 131072
NEAR_TOTAL = 16384
FAR_TOTAL = 16384


def block_pairs(key, slot_cap, salt_value):
    shard_count = CLUSTERS // CL_DEV
    base_key = jax.random.fold_in(key, salt_value)
    row_key, peer_key = jax.random.split(base_key)
    slot_total = shard_count * slot_cap
    device_ids = jnp.arange(slot_total, dtype=jnp.int32) // slot_cap
    row_ids = device_ids * CL_DEV + jax.random.randint(row_key, (slot_total,), 0, CL_DEV, dtype=jnp.int32)
    step_pick = jax.random.randint(peer_key, (slot_total,), 0, 2 * REACH, dtype=jnp.int32)
    offsets = jnp.where(step_pick < REACH, step_pick + 1, REACH - 1 - step_pick)
    peer_ids = (device_ids + offsets) % shard_count
    partner = jax.random.randint(jax.random.fold_in(key, 7), (shard_count, 2 * REACH), 0, CL_DEV, dtype=jnp.int32)
    part_ids = partner[device_ids, step_pick]
    col_ids = peer_ids * CL_DEV + part_ids
    return (row_ids.astype(jnp.int32), col_ids.astype(jnp.int32))


def draw_near_rows(key, part):
    row_ids, col_ids = block_pairs(key, NEAR_CAP, 11)
    return row_ids


def draw_near_cols(key, part):
    row_ids, col_ids = block_pairs(key, NEAR_CAP, 11)
    return col_ids


def draw_far_rows(key, part):
    row_ids, col_ids = block_pairs(key, FAR_CAP, 13)
    return row_ids


def draw_far_cols(key, part):
    row_ids, col_ids = block_pairs(key, FAR_CAP, 13)
    return col_ids


def draw_counts(key, part):
    key = jax.random.fold_in(key, 21)
    shard_count = CLUSTERS // CL_DEV
    near_key, near_top, far_key, far_top = jax.random.split(key, 4)
    device_ids = jnp.arange(shard_count, dtype=jnp.int32)
    near_fill = jax.random.randint(near_key, (shard_count,), max(1, NEAR_CAP // 8), 7 * NEAR_CAP // 10 + 1, dtype=jnp.int32)
    near_fill = jnp.where(device_ids == jax.random.randint(near_top, (), 0, shard_count, dtype=jnp.int32), NEAR_CAP, near_fill)
    far_fill = jax.random.randint(far_key, (shard_count,), max(1, FAR_CAP // 8), 7 * FAR_CAP // 10 + 1, dtype=jnp.int32)
    far_fill = jnp.where(device_ids == jax.random.randint(far_top, (), 0, shard_count, dtype=jnp.int32), FAR_CAP, far_fill)
    return jnp.stack([near_fill, far_fill], axis=1).astype(jnp.int32)


def draw_diag_blocks(key, part):
    key = jax.random.fold_in(key, 31)
    noise_key, center_key = jax.random.split(key)
    noise_part = jax.random.normal(noise_key, (CLUSTERS, B, B), jnp.float32)
    center = jax.random.uniform(center_key, (CLUSTERS, B), jnp.float32, 1.0, 2.0)
    symmetric = (noise_part + jnp.swapaxes(noise_part, 1, 2)) * (0.5 / B ** 0.5)
    identity = jnp.eye(B, dtype=jnp.float32)
    return (symmetric * (1.0 - identity) + identity[None] * center[:, :, None]).astype(jnp.bfloat16)


def block_levels(key, extent, cuts, smallest, largest):
    def one(dim, shards_of):
        draws = jax.random.uniform(jax.random.fold_in(jax.random.fold_in(key, 6), dim), (shards_of,), jnp.float32, smallest / len(cuts), largest / len(cuts))
        return jnp.repeat(jnp.exp(draws), extent[dim] // shards_of).reshape((-1,) + (1,) * (len(extent) - dim - 1))

    factor_of = one(*cuts[0])
    for cut in cuts[1:]:
        factor_of = factor_of * one(*cut)
    return factor_of


def gaussian(own_key, shape, scale, most, cuts=(), kind=jnp.bfloat16):
    values = jax.random.normal(own_key, shape, jnp.float32) * scale
    if len(cuts) > 0:
        values = block_levels(own_key, shape, cuts, -0.22, 0.18) * values
    return jnp.clip(values, min=-most, max=most).astype(kind)


def setup_inputs(seed: int = 0) -> dict:
    streams_of = jax.random.split(jax.random.key(seed), 11)
    return {
        "vectors": gaussian(streams_of[0], (RHS, PANELS), 1.0, 6.0, ((1, 128),)),
        "diag_blocks": draw_diag_blocks(jax.random.fold_in(streams_of[10], 71), 0),
        "near_blocks": gaussian(streams_of[2], (NEAR_TOTAL, B, B), (32 * B) ** -0.5, 0.0625, ((0, 128),)),
        "near_rows": draw_near_rows(jax.random.fold_in(streams_of[10], 71), 0),
        "near_cols": draw_near_cols(jax.random.fold_in(streams_of[10], 71), 0),
        "far_left": gaussian(streams_of[5], (FAR_TOTAL, K, B), K ** -0.5, 1.0, ((0, 128),)),
        "far_right": gaussian(streams_of[6], (FAR_TOTAL, K, B), (32 * B) ** -0.5, 0.0625, ((0, 128),)),
        "far_rows": draw_far_rows(jax.random.fold_in(streams_of[10], 71), 0),
        "far_cols": draw_far_cols(jax.random.fold_in(streams_of[10], 71), 0),
        "counts": draw_counts(jax.random.fold_in(streams_of[10], 71), 0),
    }


def round_trip(value):
    rounded = lax.optimization_barrier(value.astype(jnp.bfloat16))
    return rounded.astype(jnp.float32)


def apply_operator(vector_in, diag_blocks, near_blocks, near_rows, near_cols, far_left, far_right, far_rows, far_cols, counts):
    shard_count = counts.shape[0]
    columns = vector_in.astype(jnp.float32).reshape(RHS, CLUSTERS, B).transpose(1, 0, 2)
    result = jnp.einsum("cab,crb->cra", diag_blocks.astype(jnp.float32), columns)

    def near_step(result, pieces):
        blocks, rows_ids, cols_ids, live_count = pieces
        live_mask = (jnp.arange(NEAR_CAP) < live_count).astype(jnp.float32)[:, None, None]
        blocks = blocks.astype(jnp.float32)
        forward = jnp.einsum("gab,grb->gra", blocks, columns[cols_ids]) * live_mask
        transposed = jnp.einsum("gab,gra->grb", blocks, columns[rows_ids]) * live_mask
        result = result.at[rows_ids].add(forward).at[cols_ids].add(transposed)
        return result, None

    def far_step(result, pieces):
        left_part, right_part, rows_ids, cols_ids, live_count = pieces
        live_mask = (jnp.arange(FAR_CAP) < live_count).astype(jnp.float32)[:, None, None]
        left_part = left_part.astype(jnp.float32)
        right_part = right_part.astype(jnp.float32)
        coefficient = round_trip(jnp.einsum("gkb,grb->grk", right_part, columns[cols_ids]))
        forward = jnp.einsum("gka,grk->gra", left_part, coefficient) * live_mask
        back_coefficient = round_trip(jnp.einsum("gka,gra->grk", left_part, columns[rows_ids]))
        transposed = jnp.einsum("gkb,grk->grb", right_part, back_coefficient) * live_mask
        result = result.at[rows_ids].add(forward).at[cols_ids].add(transposed)
        return result, None

    result, unused = lax.scan(near_step, result, (
        near_blocks.reshape(shard_count, NEAR_CAP, B, B),
        near_rows.reshape(shard_count, NEAR_CAP),
        near_cols.reshape(shard_count, NEAR_CAP),
        counts[:, 0]))
    result, unused = lax.scan(far_step, result, (
        far_left.reshape(shard_count, FAR_CAP, K, B),
        far_right.reshape(shard_count, FAR_CAP, K, B),
        far_rows.reshape(shard_count, FAR_CAP),
        far_cols.reshape(shard_count, FAR_CAP),
        counts[:, 1]))
    return result.transpose(1, 0, 2).reshape(RHS, CLUSTERS * B)


def reference(vectors, diag_blocks, near_blocks, near_rows, near_cols, far_left, far_right, far_rows, far_cols, counts):
    first_image = apply_operator(vectors, diag_blocks, near_blocks, near_rows, near_cols, far_left, far_right, far_rows, far_cols, counts)
    second_image = apply_operator(first_image.astype(jnp.bfloat16), diag_blocks, near_blocks, near_rows, near_cols, far_left, far_right, far_rows, far_cols, counts)
    return first_image, second_image
```

```python
import functools

import jax
import jax.numpy as jnp
from jax import lax
from jax.experimental import pallas as pl
from jax.experimental.pallas import tpu as pltpu
from jax.sharding import PartitionSpec as P

RHS, B, K = 64, 256, 32
CL, SLOTS, CHUNK = 4, 128, 16
CHUNKS = SLOTS // CHUNK
GROUP = B // K
PEERS = 12
DEAD = 12
EXTRA = 8
VMEM_BYTES = 44 * 2**20
F32, BF16 = jnp.float32, jnp.bfloat16


def dot(x, y):
    return lax.dot_general(x, y, (((1,), (0,)), ((), ())), preferred_element_type=F32)


def dot_t(x, y):
    return lax.dot_general(x, y, (((1,), (1,)), ((), ())), preferred_element_type=F32)


def peer_number(delta, core):
    kappa, other = delta // 2 - 3, delta % 2
    step = kappa * (1 - 2 * core)
    same = int(other != core)
    if step == 0:
        return 11 if same else DEAD
    if step < 0:
        return 2 * (-step - 1) + same
    return 6 + 2 * (step - 1) + same if step < 3 or not same else DEAD


class Stream:
    def __init__(self, counts, near, left, right, near_buf, left_buf, right_buf, near_sem, left_sem, right_sem):
        self.near_chunks = (counts[0, 0] + (CHUNK - 1)) // CHUNK
        self.far_chunks = (counts[0, 1] + (CHUNK - 1)) // CHUNK
        self.near = (near, near_buf, near_sem)
        self.far = ((left, left_buf, left_sem), (right, right_buf, right_sem))

    @staticmethod
    def copy(triple, chunk):
        source, target, sem = triple
        place = pl.ds(chunk * CHUNK, CHUNK)
        return pltpu.make_async_copy(source.at[place], target.at[place], sem.at[chunk])

    def start(self):
        def far_start(chunk, carry):
            for triple in self.far:
                self.copy(triple, chunk).start()
            return carry

        def near_start(chunk, carry):
            self.copy(self.near, chunk).start()
            return carry

        lax.fori_loop(0, self.far_chunks, far_start, 0)
        lax.fori_loop(0, self.near_chunks, near_start, 0)

    def far_loop(self, body):
        def step(chunk, carry):
            for triple in self.far:
                self.copy(triple, chunk).wait()
            for part in range(CHUNK // GROUP):
                body(chunk * CHUNK + part * GROUP)
            return carry

        lax.fori_loop(0, self.far_chunks, step, 0)

    def near_loop(self, body):
        def step(chunk, carry):
            self.copy(self.near, chunk).wait()
            for part in range(CHUNK):
                body(chunk * CHUNK + part)
            return carry

        lax.fori_loop(0, self.near_chunks, step, 0)


def lane_ids(table, row, first):
    lane = lax.broadcasted_iota(jnp.int32, (1, B), 1) // K
    ids = jnp.zeros((1, B), jnp.int32)
    for k in range(GROUP):
        ids = jnp.where(lane == k, table[row, first + k], ids)
    return jnp.broadcast_to(ids, (RHS, B))


def spread(value, ids, number):
    return jnp.concatenate([jnp.where(ids == n, value, 0.0).astype(BF16) for n in range(number)], axis=0)


def gathered(values, ids, number):
    out = jnp.zeros((RHS, B), F32)
    for n in range(number):
        out = jnp.where(ids == n, values[n * RHS : (n + 1) * RHS], out)
    return out.astype(BF16)


def back_products(stream, table, own, acc, near_buf, left_buf, right_buf):
    acc[...] = jnp.zeros_like(acc)

    def far(first):
        left = left_buf[pl.ds(first, GROUP)].reshape(B, B)
        right = right_buf[pl.ds(first, GROUP)].reshape(B, B)
        coef = gathered(dot_t(own[...].reshape(CL * RHS, B), left), lane_ids(table, 2, first), CL)
        terms = dot(spread(coef.astype(F32), lane_ids(table, 3, first), PEERS), right)
        acc[0:PEERS] += terms.reshape(PEERS, RHS, B)

    def near(slot):
        rho = table[1, slot]
        acc[rho] += dot(own[jnp.minimum(table[0, slot], CL - 1)], near_buf[slot])

    stream.far_loop(far)
    stream.near_loop(near)


def forward_products(stream, table, fetched, acc, near_buf, left_buf, right_buf):
    def far(first):
        left = left_buf[pl.ds(first, GROUP)].reshape(B, B)
        right = right_buf[pl.ds(first, GROUP)].reshape(B, B)
        columns = fetched[0:PEERS].reshape(PEERS * RHS, B)
        coef = gathered(dot_t(columns, right), lane_ids(table, 3, first), PEERS)
        terms = dot(spread(coef.astype(F32), lane_ids(table, 2, first), CL), left)
        acc[0:CL] += terms.reshape(CL, RHS, B)

    def near(slot):
        row = table[0, slot]
        acc[row] += dot_t(fetched[table[1, slot]], near_buf[slot])

    stream.far_loop(far)
    stream.near_loop(near)


def place_out(rho):
    if rho == 11:
        return 3, 6
    if rho < 6:
        return 3, rho ^ 1
    k, same = divmod(rho - 6, 2)
    return k, 3 * same


def place_in(rho):
    if rho == 11:
        return 4, 6
    if rho < 6:
        return rho // 2, rho % 2
    return 3, rho - 6


MESSAGE = (4, 4, 3)


def back_first(
    me, near_rows, near_cols, far_rows, far_cols, counts, own, near, left, right,
    m1, m2, m3, give, table, parts,
    near_buf, left_buf, right_buf, acc, lut, near_sem, left_sem, right_sem,
):
    stream = Stream(counts, near, left, right, near_buf, left_buf, right_buf, near_sem, left_sem, right_sem)
    stream.start()
    core = me[0] % 2
    base = me[0] - core - 6
    for delta in range(16):
        pair = [peer_number(delta, a) if delta < 14 else DEAD for a in (0, 1)]
        lut[delta] = jnp.where(core == 0, pair[0], pair[1])
    for rho in range(16):
        parts[rho] = 0
    for kind, (rows, cols, chunks) in enumerate(
        ((near_rows, near_cols, stream.near_chunks), (far_rows, far_cols, stream.far_chunks))
    ):

        def note(index, carry, kind=kind, rows=rows, cols=cols):
            for part in range(8):
                slot = index * 8 + part
                live = slot < counts[0, kind]
                col = cols[slot]
                rho = jnp.where(live, lut[((col // CL) - base) & 15], DEAD)
                table[2 * kind, slot] = jnp.where(live, rows[slot] & (CL - 1), CL)
                table[2 * kind + 1, slot] = rho
                parts[rho] = col & (CL - 1)
            return carry

        lax.fori_loop(0, chunks * (CHUNK // 8), note, 0)
    back_products(stream, table, own, acc, near_buf, left_buf, right_buf)
    outs = (m1, m2, m3, give)
    for rho in range(PEERS):
        message, index = place_out(rho)
        outs[message][index, 0:RHS] = acc[rho]
        outs[message][index, RHS:] = jnp.full((EXTRA, B), parts[rho].astype(F32), F32)


def forward_first(
    counts, table, parts, own, sib, h1, h2, h3, post, diag, near, left, right,
    out,
    near_buf, left_buf, right_buf, fetched, acc, near_sem, left_sem, right_sem, fetch_sem,
):
    stream = Stream(counts, near, left, right, near_buf, left_buf, right_buf, near_sem, left_sem, right_sem)
    halo = (h1, h2, h3)
    copies = []
    for rho in range(PEERS):
        if rho == 11:
            source, first = sib, 0
        elif rho < 6:
            source, first = halo[rho // 2], CL * (rho % 2)
        else:
            k, same = divmod(rho - 6, 2)
            source, first = post, 2 * CL * k + (CL * (1 - same) if k < 2 else 0)
        copies.append(pltpu.make_async_copy(source.at[first + parts[rho]], fetched.at[rho], fetch_sem.at[rho]))
    for copy in copies:
        copy.start()
    stream.start()
    fetched[DEAD] = jnp.zeros((RHS, B), BF16)
    acc[CL] = jnp.zeros((RHS, B), F32)
    for cluster in range(CL):
        acc[cluster] = dot_t(own[cluster], diag[cluster])
    for copy in copies:
        copy.wait()
    forward_products(stream, table, fetched, acc, near_buf, left_buf, right_buf)
    out[...] = acc[0:CL]


def back_second(
    counts, table, partial, r1, r2, r3, post, got, near, left, right,
    image, rounded, wanted, m1, m2, m3, give,
    near_buf, left_buf, right_buf, arrived, acc, near_sem, left_sem, right_sem, arrived_sem,
):
    stream = Stream(counts, near, left, right, near_buf, left_buf, right_buf, near_sem, left_sem, right_sem)
    ins = (r1, r2, r3, post, got)
    copies = []
    for rho in range(PEERS):
        message, index = place_in(rho)
        copies.append(pltpu.make_async_copy(ins[message].at[index], arrived.at[rho], arrived_sem.at[rho]))
    for copy in copies:
        copy.start()
    stream.start()
    for copy in copies:
        copy.wait()
    for rho in range(PEERS):
        wanted[rho] = arrived[rho, RHS:]
    for cluster in range(CL):
        total = partial[cluster]
        for rho in range(PEERS):
            mine = arrived[rho, RHS : RHS + 1] == float(cluster)
            total += jnp.where(jnp.broadcast_to(mine, (RHS, B)), arrived[rho, 0:RHS], 0.0)
        image[:, cluster * B : (cluster + 1) * B] = total
        rounded[cluster] = total.astype(BF16)
    back_products(stream, table, rounded, acc, near_buf, left_buf, right_buf)
    outs = (m1, m2, m3, give)
    for rho in range(PEERS):
        message, index = place_out(rho)
        outs[message][index, 0:RHS] = acc[rho].astype(BF16)
        pick = jnp.broadcast_to(wanted[rho, 0:1], (RHS, B))
        chosen = jnp.zeros((RHS, B), F32)
        for cluster in range(CL):
            chosen = jnp.where(pick == float(cluster), rounded[cluster].astype(F32), chosen)
        outs[message][index, RHS:] = chosen.astype(BF16)


def forward_second(
    counts, table, own, wanted, r1, r2, r3, post, got, diag, near, left, right,
    image,
    near_buf, left_buf, right_buf, arrived, fetched, acc, near_sem, left_sem, right_sem, arrived_sem,
):
    stream = Stream(counts, near, left, right, near_buf, left_buf, right_buf, near_sem, left_sem, right_sem)
    ins = (r1, r2, r3, post, got)
    copies = []
    for rho in range(PEERS):
        message, index = place_in(rho)
        source = ins[message].at[index]
        copies.append(pltpu.make_async_copy(source, arrived.at[rho], arrived_sem.at[rho]))
    for copy in copies:
        copy.start()
    stream.start()
    fetched[DEAD] = jnp.zeros((RHS, B), BF16)
    acc[CL] = jnp.zeros((RHS, B), F32)
    for cluster in range(CL):
        acc[cluster] = dot_t(own[cluster], diag[cluster])
    for copy in copies:
        copy.wait()
    for rho in range(PEERS):
        fetched[rho] = arrived[rho, RHS:]
    for cluster in range(CL):
        total = acc[cluster]
        for rho in range(PEERS):
            mine = wanted[rho, 0:1] == float(cluster)
            total += jnp.where(jnp.broadcast_to(mine, (RHS, B)), arrived[rho, 0:RHS].astype(F32), 0.0)
        acc[cluster] = total
    forward_products(stream, table, fetched, acc, near_buf, left_buf, right_buf)
    for cluster in range(CL):
        image[:, cluster * B : (cluster + 1) * B] = acc[cluster]


SMEM = pl.BlockSpec(memory_space=pltpu.SMEM)
VMEM = pl.BlockSpec(memory_space=pltpu.VMEM)
ANY = pl.BlockSpec(memory_space=pl.ANY)


def blocks_scratch():
    return [
        pltpu.VMEM((SLOTS, B, B), BF16),
        pltpu.VMEM((SLOTS, K, B), BF16),
        pltpu.VMEM((SLOTS, K, B), BF16),
    ]


def sems(*more):
    return [pltpu.SemaphoreType.DMA((CHUNKS,))] * 3 + [pltpu.SemaphoreType.DMA((n,)) for n in more]


def call(kernel, name, outs, out_specs, in_specs, scratch):
    return pl.pallas_call(
        kernel,
        name=name,
        out_shape=outs,
        in_specs=in_specs,
        out_specs=out_specs,
        scratch_shapes=scratch,
        compiler_params=pltpu.CompilerParams(vmem_limit_bytes=VMEM_BYTES),
        cost_estimate=pl.CostEstimate(flops=2 * 10**9, bytes_accessed=22 * 10**6, transcendentals=0),
    )


def shaped(shape, dtype):
    return jax.ShapeDtypeStruct(shape, dtype)


def carriers(size, k):
    pairs = []
    for chip in range(size // 2):
        for core in range(2):
            step = k if core == 0 else -k
            pairs.append((2 * chip + core, (2 * (chip + step) + core) % size))
    return pairs


def per_device(
    vectors, diag_blocks, near_blocks, near_rows, near_cols, far_left, far_right, far_rows, far_cols, counts
):
    size = lax.axis_size("rows")
    me = lax.axis_index("rows").reshape(1)

    def swap(block):
        return lax.ppermute(block, "rows", [(i, i ^ 1) for i in range(size)])

    def carry(block, k):
        return lax.ppermute(block, "rows", carriers(size, k))

    def exchange(m1, m2, m3, give):
        got = swap(give)
        messages = []
        for k, message in enumerate((m1, m2, m3)):
            messages.append(lax.dynamic_update_slice(message, got[2 * k : 2 * k + 2], (1, 0, 0)))
        return [carry(message, k + 1) for k, message in enumerate(messages)] + [got]

    def passed_on(r1, r2, r3):
        return swap(jnp.concatenate([r1[2:4], r2[2:4], r3[2:3]]))

    own = vectors.reshape(RHS, CL, B).transpose(1, 0, 2)
    sib = swap(own)
    both = jnp.concatenate([own, sib])
    halo = [carry(both, k) for k in (1, 2, 3)]

    def message_shapes(rows, dtype):
        return [shaped((n, rows, B), dtype) for n in MESSAGE + (7,)]

    m1, m2, m3, give, table, parts = call(
        back_first, "transposed_products",
        message_shapes(RHS + EXTRA, F32) + [shaped((4, SLOTS), jnp.int32), shaped((16,), jnp.int32)],
        [VMEM] * 4 + [SMEM] * 2,
        [SMEM] * 6 + [VMEM] + [ANY] * 3,
        blocks_scratch() + [pltpu.VMEM((PEERS + 1, RHS, B), F32), pltpu.SMEM((16,), jnp.int32)] + sems(),
    )(me, near_rows, near_cols, far_rows, far_cols, counts, own, near_blocks, far_left, far_right)
    halo_post = swap(jnp.concatenate([halo[0], halo[1], halo[2][CL:]]))
    r1, r2, r3, got = exchange(m1, m2, m3, give)
    partial = call(
        forward_first, "forward_products",
        shaped((CL, RHS, B), F32), VMEM,
        [SMEM] * 3 + [VMEM] + [ANY] * 5 + [VMEM] + [ANY] * 3,
        blocks_scratch()
        + [pltpu.VMEM((PEERS + 1, RHS, B), BF16), pltpu.VMEM((CL + 1, RHS, B), F32)]
        + sems(PEERS),
    )(counts, table, parts, own, sib, *halo, halo_post, diag_blocks, near_blocks, far_left, far_right)
    post = passed_on(r1, r2, r3)
    first_image, rounded, wanted, m1, m2, m3, give = call(
        back_second, "image_and_transposed_products",
        [
            shaped((RHS, CL * B), F32),
            shaped((CL, RHS, B), BF16),
            shaped((PEERS, EXTRA, B), F32),
        ]
        + message_shapes(2 * RHS, BF16),
        [VMEM] * 7,
        [SMEM] * 2 + [VMEM] + [ANY] * 8,
        blocks_scratch()
        + [pltpu.VMEM((PEERS, RHS + EXTRA, B), F32), pltpu.VMEM((PEERS + 1, RHS, B), F32)]
        + sems(PEERS),
    )(counts, table, partial, r1, r2, r3, post, got, near_blocks, far_left, far_right)
    r1, r2, r3, got = exchange(m1, m2, m3, give)
    post = passed_on(r1, r2, r3)
    second_image = call(
        forward_second, "second_image",
        shaped((RHS, CL * B), F32), VMEM,
        [SMEM] * 2 + [VMEM] * 2 + [ANY] * 5 + [VMEM] + [ANY] * 3,
        blocks_scratch()
        + [
            pltpu.VMEM((PEERS, 2 * RHS, B), BF16),
            pltpu.VMEM((PEERS + 1, RHS, B), BF16),
            pltpu.VMEM((CL + 1, RHS, B), F32),
        ]
        + sems(PEERS),
    )(counts, table, rounded, wanted, r1, r2, r3, post, got, diag_blocks, near_blocks, far_left, far_right)
    return first_image, second_image


def solution(mesh):
    return jax.shard_map(
        per_device,
        mesh=mesh,
        in_specs=(
            P(None, "rows"),
            P("rows", None, None),
            P("rows", None, None),
            P("rows"),
            P("rows"),
            P("rows", None, None),
            P("rows", None, None),
            P("rows"),
            P("rows"),
            P("rows", None),
        ),
        out_specs=(P(None, "rows"), P(None, "rows")),
        check_vma=False,
    )
```

```python
import functools

import jax
import jax.numpy as jnp
from jax import lax
from jax.experimental import pallas as pl
from jax.experimental.pallas import tpu as pltpu
from jax.sharding import PartitionSpec as P

RHS, B, K = 64, 256, 32
CL, SLOTS, CHUNK = 4, 128, 16
CHUNKS = SLOTS // CHUNK
GROUP = B // K
PEERS = 12
DEAD = 12
EXTRA = 8
QUAD = 4
LISTED = SLOTS + PEERS * (QUAD - 1) + 12
VMEM_BYTES = 44 * 2**20
F32, BF16 = jnp.float32, jnp.bfloat16


def dot(x, y):
    return lax.dot_general(x, y, (((1,), (0,)), ((), ())), preferred_element_type=F32)


def dot_t(x, y):
    return lax.dot_general(x, y, (((1,), (1,)), ((), ())), preferred_element_type=F32)


def peer_number(delta, core):
    kappa, other = delta // 2 - 3, delta % 2
    step = kappa * (1 - 2 * core)
    same = int(other != core)
    if step == 0:
        return 11 if same else DEAD
    if step < 0:
        return 2 * (-step - 1) + same
    return 6 + 2 * (step - 1) + same if step < 3 or not same else DEAD


class Stream:
    def __init__(self, plan, near, left, right, near_buf, left_buf, right_buf, near_sem, left_sem, right_sem):
        self.plan = plan
        self.near = (near, near_buf, near_sem)
        self.far = ((left, left_buf, left_sem), (right, right_buf, right_sem))

    @staticmethod
    def copy(triple, chunk):
        source, target, sem = triple
        place = pl.ds(chunk * CHUNK, CHUNK)
        return pltpu.make_async_copy(source.at[place], target.at[place], sem.at[chunk])

    def start(self, near_chunks, far_chunks):
        def far_start(chunk, carry):
            for triple in self.far:
                self.copy(triple, chunk).start()
            return carry

        def near_start(chunk, carry):
            self.copy(self.near, chunk).start()
            return carry

        lax.fori_loop(0, far_chunks, far_start, 0)
        lax.fori_loop(0, near_chunks, near_start, 0)

    def start_planned(self):
        self.start(self.plan[4, 16], self.plan[4, 17])

    def far_loop(self, body):
        def arrived(chunk, carry):
            for triple in self.far:
                self.copy(triple, chunk).wait()
            return carry

        lax.fori_loop(0, self.plan[4, 17], arrived, 0)

        def step(index, carry):
            for part in range(2):
                first = index * 2 + part
                entries = [self.plan[2, first * GROUP + k] for k in range(GROUP)]
                slots = [entry & 255 for entry in entries]
                left = jnp.concatenate([self.far[0][1][slot] for slot in slots], axis=0)
                right = jnp.concatenate([self.far[1][1][slot] for slot in slots], axis=0)
                lane = lax.broadcasted_iota(jnp.int32, (1, B), 1) // K
                rows = jnp.zeros((1, B), jnp.int32)
                for k in range(GROUP):
                    rows = jnp.where(lane == k, entries[k] >> 8, rows)
                rows = jnp.broadcast_to(rows, (RHS, B))
                body(left, right, rows, [self.plan[3, 2 * first + half] for half in (0, 1)])
            return carry

        lax.fori_loop(0, self.plan[4, 18], step, 0)

    def near_loop(self, body):
        def step(chunk, carry):
            self.copy(self.near, chunk).wait()
            for part in range(CHUNK):
                body(chunk * CHUNK + part)
            return carry

        lax.fori_loop(0, self.plan[4, 16], step, 0)


HALF = B // 2


def back_products(stream, own, acc, near_buf):
    plan = stream.plan
    acc[...] = jnp.zeros_like(acc)

    def far(left, right, rows, partners):
        every = dot_t(own[0:CL].reshape(CL * RHS, B), left)
        coef = jnp.zeros((RHS, B), F32)
        for cluster in range(CL):
            coef = jnp.where(rows == cluster, every[cluster * RHS : (cluster + 1) * RHS], coef)
        coef = coef.astype(BF16)
        for half, partner in enumerate(partners):
            part = slice(half * HALF, (half + 1) * HALF)
            acc[partner] += dot(coef[:, part], right[part])

    def near(slot):
        acc[plan[1, slot]] += dot(own[plan[0, slot]], near_buf[slot])

    stream.far_loop(far)
    stream.near_loop(near)


def forward_products(stream, fetched, acc, near_buf):
    plan = stream.plan

    def far(left, right, rows, partners):
        coef = [
            dot_t(fetched[partner], right[half * HALF : (half + 1) * HALF])
            for half, partner in enumerate(partners)
        ]
        coef = jnp.concatenate(coef, axis=1).astype(BF16).astype(F32)
        spread = [jnp.where(rows == cluster, coef, 0.0).astype(BF16) for cluster in range(CL)]
        acc[0:CL] += dot(jnp.concatenate(spread, axis=0), left).reshape(CL, RHS, B)

    def near(slot):
        acc[plan[0, slot]] += dot_t(fetched[plan[1, slot]], near_buf[slot])

    stream.far_loop(far)
    stream.near_loop(near)


def make_plan(me, near_rows, near_cols, far_rows, far_cols, counts, plan, lut, fill, rank):
    core = me % 2
    base = me - core - 6
    for delta in range(16):
        pair = [peer_number(delta, a) if delta < 14 else DEAD for a in (0, 1)]
        lut[delta] = jnp.where(core == 0, pair[0], pair[1])
        plan[4, delta] = 0
        fill[delta] = 0
    near_chunks = (counts[0, 0] + (CHUNK - 1)) // CHUNK
    far_chunks = (counts[0, 1] + (CHUNK - 1)) // CHUNK

    def near_note(index, carry):
        for part in range(8):
            slot = index * 8 + part
            live = slot < counts[0, 0]
            col = near_cols[slot]
            rho = jnp.where(live, lut[((col // CL) - base) & 15], DEAD)
            plan[0, slot] = jnp.where(live, near_rows[slot] & (CL - 1), CL)
            plan[1, slot] = rho
            plan[4, rho] = col & (CL - 1)
        return carry

    def far_note(slot, carry):
        col = far_cols[slot]
        rho = lut[((col // CL) - base) & 15]
        plan[4, rho] = col & (CL - 1)
        before = fill[rho]
        rank[slot] = before + 256 * rho
        fill[rho] = before + 1
        return carry

    def far_place(slot, carry):
        noted = rank[slot]
        plan[2, fill[noted >> 8] + (noted & 255)] = slot + 256 * (far_rows[slot] & (CL - 1))
        return carry

    lax.fori_loop(0, counts[0, 1], far_note, 0)
    quads = 0
    for rho in range(PEERS):
        number = fill[rho]
        first = quads
        fill[rho] = first * QUAD
        wanted = (number + (QUAD - 1)) // QUAD

        def own_quad(index, carry, rho=rho):
            plan[3, index] = rho
            return carry

        quads = first + wanted
        lax.fori_loop(first, quads, own_quad, 0)
        for pad in range(1, QUAD):

            @pl.when(quads * QUAD - pad >= first * QUAD + number)
            def _(pad=pad, quads=quads):
                plan[2, quads * QUAD - pad] = 256 * CL

    fours = (quads + 3) // 4

    def dead_quad(index, carry):
        plan[3, index] = DEAD
        for k in range(QUAD):
            plan[2, index * QUAD + k] = 256 * CL
        return carry

    lax.fori_loop(quads, fours * 4, dead_quad, 0)
    lax.fori_loop(0, counts[0, 1], far_place, 0)
    lax.fori_loop(0, near_chunks * (CHUNK // 8), near_note, 0)
    plan[4, 16] = near_chunks
    plan[4, 17] = far_chunks
    plan[4, 18] = fours


def place_out(rho):
    if rho == 11:
        return 3, 6
    if rho < 6:
        return 3, rho ^ 1
    k, same = divmod(rho - 6, 2)
    return k, 3 * same


def place_in(rho):
    if rho == 11:
        return 4, 6
    if rho < 6:
        return rho // 2, rho % 2
    return 3, rho - 6


MESSAGE = (4, 4, 3)


def back_first(
    me, near_rows, near_cols, far_rows, far_cols, counts, vectors, near, left, right,
    m1, m2, m3, give, plan,
    near_buf, left_buf, right_buf, own, acc, lists, few, lut, fill, rank, near_sem, left_sem, right_sem, list_sem,
):
    copies = [pltpu.make_async_copy(counts, few, list_sem.at[4])]
    for index, source in enumerate((near_rows, near_cols, far_rows, far_cols)):
        copies.append(pltpu.make_async_copy(source, lists[index], list_sem.at[index]))
    for copy in copies:
        copy.start()
    for cluster in range(CL):
        own[cluster] = vectors[:, cluster * B : (cluster + 1) * B]
    own[CL] = jnp.zeros((RHS, B), BF16)
    for copy in copies:
        copy.wait()
    stream = Stream(plan, near, left, right, near_buf, left_buf, right_buf, near_sem, left_sem, right_sem)
    stream.start((few[0, 0] + (CHUNK - 1)) // CHUNK, (few[0, 1] + (CHUNK - 1)) // CHUNK)
    make_plan(me[0], *lists, few, plan, lut, fill, rank)
    back_products(stream, own, acc, near_buf)
    outs = (m1, m2, m3, give)
    for rho in range(PEERS):
        message, index = place_out(rho)
        outs[message][index, 0:RHS] = acc[rho]
        outs[message][index, RHS:] = jnp.full((EXTRA, B), plan[4, rho].astype(F32), F32)


def forward_first(
    plan, vectors, sib, h1, h2, h3, post, diag, near, left, right,
    out,
    near_buf, left_buf, right_buf, fetched, acc, near_sem, left_sem, right_sem, fetch_sem,
):
    stream = Stream(plan, near, left, right, near_buf, left_buf, right_buf, near_sem, left_sem, right_sem)
    halo = (h1, h2, h3)
    copies = []
    for rho in range(PEERS):
        lanes = pl.ds(pl.multiple_of(plan[4, rho] * B, B), B)
        if rho == 11:
            source = sib.at[:, lanes]
        elif rho < 6:
            source = halo[rho // 2].at[rho % 2, :, lanes]
        else:
            k, same = divmod(rho - 6, 2)
            source = post.at[2 * k + (1 - same if k < 2 else 0), :, lanes]
        copies.append(pltpu.make_async_copy(source, fetched.at[rho], fetch_sem.at[rho]))
    for copy in copies:
        copy.start()
    stream.start_planned()
    fetched[DEAD] = jnp.zeros((RHS, B), BF16)
    acc[CL] = jnp.zeros((RHS, B), F32)
    for cluster in range(CL):
        acc[cluster] = dot_t(vectors[:, cluster * B : (cluster + 1) * B], diag[cluster])
    for copy in copies:
        copy.wait()
    forward_products(stream, fetched, acc, near_buf)
    out[...] = acc[0:CL]


def back_second(
    plan, partial, r1, r2, r3, post, got, near, left, right,
    image, rounded, wanted, m1, m2, m3, give,
    near_buf, left_buf, right_buf, own, arrived, acc, near_sem, left_sem, right_sem, arrived_sem,
):
    stream = Stream(plan, near, left, right, near_buf, left_buf, right_buf, near_sem, left_sem, right_sem)
    ins = (r1, r2, r3, post, got)
    copies = []
    for rho in range(PEERS):
        message, index = place_in(rho)
        copies.append(pltpu.make_async_copy(ins[message].at[index], arrived.at[rho], arrived_sem.at[rho]))
    for copy in copies:
        copy.start()
    stream.start_planned()
    own[CL] = jnp.zeros((RHS, B), BF16)
    for copy in copies:
        copy.wait()
    for rho in range(PEERS):
        wanted[rho] = arrived[rho, RHS:]
    for cluster in range(CL):
        total = partial[cluster]
        for rho in range(PEERS):
            mine = arrived[rho, RHS : RHS + 1] == float(cluster)
            total += jnp.where(jnp.broadcast_to(mine, (RHS, B)), arrived[rho, 0:RHS], 0.0)
        image[:, cluster * B : (cluster + 1) * B] = total
        own[cluster] = total.astype(BF16)
        rounded[cluster] = total.astype(BF16)
    back_products(stream, own, acc, near_buf)
    outs = (m1, m2, m3, give)
    for rho in range(PEERS):
        message, index = place_out(rho)
        outs[message][index, 0:RHS] = acc[rho].astype(BF16)
        pick = jnp.broadcast_to(wanted[rho, 0:1], (RHS, B))
        chosen = jnp.zeros((RHS, B), F32)
        for cluster in range(CL):
            chosen = jnp.where(pick == float(cluster), own[cluster].astype(F32), chosen)
        outs[message][index, RHS:] = chosen.astype(BF16)


def forward_second(
    plan, own, wanted, r1, r2, r3, post, got, diag, near, left, right,
    image,
    near_buf, left_buf, right_buf, arrived, fetched, acc, near_sem, left_sem, right_sem, arrived_sem,
):
    stream = Stream(plan, near, left, right, near_buf, left_buf, right_buf, near_sem, left_sem, right_sem)
    ins = (r1, r2, r3, post, got)
    copies = []
    for rho in range(PEERS):
        message, index = place_in(rho)
        source = ins[message].at[index]
        copies.append(pltpu.make_async_copy(source, arrived.at[rho], arrived_sem.at[rho]))
    for copy in copies:
        copy.start()
    stream.start_planned()
    fetched[DEAD] = jnp.zeros((RHS, B), BF16)
    acc[CL] = jnp.zeros((RHS, B), F32)
    for cluster in range(CL):
        acc[cluster] = dot_t(own[cluster], diag[cluster])
    for copy in copies:
        copy.wait()
    for rho in range(PEERS):
        fetched[rho] = arrived[rho, RHS:]
    for cluster in range(CL):
        total = acc[cluster]
        for rho in range(PEERS):
            mine = wanted[rho, 0:1] == float(cluster)
            total += jnp.where(jnp.broadcast_to(mine, (RHS, B)), arrived[rho, 0:RHS].astype(F32), 0.0)
        acc[cluster] = total
    forward_products(stream, fetched, acc, near_buf)
    for cluster in range(CL):
        image[:, cluster * B : (cluster + 1) * B] = acc[cluster]


SMEM = pl.BlockSpec(memory_space=pltpu.SMEM)
VMEM = pl.BlockSpec(memory_space=pltpu.VMEM)
ANY = pl.BlockSpec(memory_space=pl.ANY)
HBM = pl.BlockSpec(memory_space=pltpu.HBM)


def blocks_scratch():
    return [
        pltpu.VMEM((SLOTS, B, B), BF16),
        pltpu.VMEM((SLOTS, K, B), BF16),
        pltpu.VMEM((SLOTS, K, B), BF16),
    ]


def sems(*more):
    return [pltpu.SemaphoreType.DMA((CHUNKS,))] * 3 + [pltpu.SemaphoreType.DMA((n,)) for n in more]


def call(kernel, name, outs, out_specs, in_specs, scratch):
    return pl.pallas_call(
        kernel,
        name=name,
        out_shape=outs,
        in_specs=in_specs,
        out_specs=out_specs,
        scratch_shapes=scratch,
        compiler_params=pltpu.CompilerParams(vmem_limit_bytes=VMEM_BYTES),
        cost_estimate=pl.CostEstimate(flops=2 * 10**9, bytes_accessed=22 * 10**6, transcendentals=0),
    )


def shaped(shape, dtype):
    return jax.ShapeDtypeStruct(shape, dtype)


def message_shapes(rows, dtype):
    return [shaped((n, rows, B), dtype) for n in MESSAGE + (7,)]


def k1(*args):
    return call(
        back_first, "transposed_products",
        message_shapes(RHS + EXTRA, F32) + [shaped((5, LISTED), jnp.int32)],
        [VMEM] * 4 + [SMEM],
        [SMEM] + [HBM] * 5 + [VMEM] + [HBM] * 3,
        blocks_scratch()
        + [
            pltpu.VMEM((CL + 1, RHS, B), BF16),
            pltpu.VMEM((PEERS + 1, RHS, B), F32),
            [pltpu.SMEM((SLOTS,), jnp.int32)] * 4,
            pltpu.SMEM((1, 2), jnp.int32),
            pltpu.SMEM((16,), jnp.int32),
            pltpu.SMEM((16,), jnp.int32),
            pltpu.SMEM((SLOTS,), jnp.int32),
        ]
        + sems(5),
    )(*args)


def k2(*args):
    return call(
        forward_first, "forward_products",
        shaped((CL, RHS, B), F32), VMEM,
        [SMEM] + [VMEM] + [ANY] * 5 + [VMEM] + [HBM] * 3,
        blocks_scratch()
        + [pltpu.VMEM((PEERS + 1, RHS, B), BF16), pltpu.VMEM((CL + 1, RHS, B), F32)]
        + sems(PEERS),
    )(*args)


def k3(*args):
    return call(
        back_second, "image_and_transposed_products",
        [
            shaped((RHS, CL * B), F32),
            shaped((CL, RHS, B), BF16),
            shaped((PEERS, EXTRA, B), F32),
        ]
        + message_shapes(2 * RHS, BF16),
        [VMEM] * 7,
        [SMEM] + [VMEM] + [ANY] * 5 + [HBM] * 3,
        blocks_scratch()
        + [
            pltpu.VMEM((CL + 1, RHS, B), BF16),
            pltpu.VMEM((PEERS, RHS + EXTRA, B), F32),
            pltpu.VMEM((PEERS + 1, RHS, B), F32),
        ]
        + sems(PEERS),
    )(*args)


def k4(*args):
    return call(
        forward_second, "second_image",
        shaped((RHS, CL * B), F32), VMEM,
        [SMEM] + [VMEM] * 2 + [ANY] * 5 + [VMEM] + [HBM] * 3,
        blocks_scratch()
        + [
            pltpu.VMEM((PEERS, 2 * RHS, B), BF16),
            pltpu.VMEM((PEERS + 1, RHS, B), BF16),
            pltpu.VMEM((CL + 1, RHS, B), F32),
        ]
        + sems(PEERS),
    )(*args)


def carriers(size, k):
    pairs = []
    for chip in range(size // 2):
        for core in range(2):
            step = k if core == 0 else -k
            pairs.append((2 * chip + core, (2 * (chip + step) + core) % size))
    return pairs


def per_device(
    vectors, diag_blocks, near_blocks, near_rows, near_cols, far_left, far_right, far_rows, far_cols, counts
):
    size = lax.axis_size("rows")
    me = lax.axis_index("rows").reshape(1)

    def swap(block):
        return lax.ppermute(block, "rows", [(i, i ^ 1) for i in range(size)])

    def carry(block, k):
        return lax.ppermute(block, "rows", carriers(size, k))

    def exchange(m1, m2, m3, give):
        got = swap(give)
        messages = []
        for k, message in enumerate((m1, m2, m3)):
            messages.append(lax.dynamic_update_slice(message, got[2 * k : 2 * k + 2], (1, 0, 0)))
        return [carry(message, k + 1) for k, message in enumerate(messages)] + [got, messages]

    def passed_on(r1, r2, r3):
        return swap(jnp.concatenate([r1[2:4], r2[2:4], r3[2:3]]))

    sib = swap(vectors)
    both = jnp.stack([vectors, sib])
    halo = [carry(both, k) for k in (1, 2, 3)]
    own, both = lax.optimization_barrier((vectors, both))
    m1, m2, m3, give, plan = k1(
        me, near_rows, near_cols, far_rows, far_cols, counts, own, near_blocks, far_left, far_right
    )
    r1, r2, r3, got, messages = exchange(m1, m2, m3, give)
    halo_post = swap(jnp.concatenate([halo[0], halo[1], halo[2][1:]]))
    halo_post, messages = lax.optimization_barrier((halo_post, messages))
    partial = k2(plan, vectors, sib, *halo, halo_post, diag_blocks, near_blocks, far_left, far_right)
    partial, r1, r2, r3 = lax.optimization_barrier((partial, r1, r2, r3))
    post = passed_on(r1, r2, r3)
    first_image, rounded, wanted, m1, m2, m3, give = k3(
        plan, partial, r1, r2, r3, post, got, near_blocks, far_left, far_right
    )
    r1, r2, r3, got, messages = exchange(m1, m2, m3, give)
    post = passed_on(r1, r2, r3)
    second_image = k4(
        plan, rounded, wanted, r1, r2, r3, post, got, diag_blocks, near_blocks, far_left, far_right
    )
    return first_image, second_image


def solution(mesh):
    return jax.shard_map(
        per_device,
        mesh=mesh,
        in_specs=(
            P(None, "rows"),
            P("rows", None, None),
            P("rows", None, None),
            P("rows"),
            P("rows"),
            P("rows", None, None),
            P("rows", None, None),
            P("rows"),
            P("rows"),
            P("rows", None),
        ),
        out_specs=(P(None, "rows"), P(None, "rows")),
        check_vma=False,
    )
```

```python
import functools

import jax
import jax.numpy as jnp
from jax import lax
from jax.experimental import pallas as pl
from jax.experimental.pallas import tpu as pltpu
from jax.sharding import PartitionSpec as P

RHS, B, K = 64, 256, 32
CL, SLOTS, CHUNK = 4, 128, 16
CHUNKS = SLOTS // CHUNK
GROUP = B // K
HALF = B // 2
PEERS = 12
DEAD = 12
EXTRA = 8
QUAD = 4
VMEM_BYTES = 16 * 2**20
F32, BF16 = jnp.float32, jnp.bfloat16


def dot(x, y):
    return lax.dot_general(x, y, (((1,), (0,)), ((), ())), preferred_element_type=F32)


def dot_t(x, y):
    return lax.dot_general(x, y, (((1,), (1,)), ((), ())), preferred_element_type=F32)


def peer_number(delta, core):
    kappa, other = delta // 2 - 3, delta % 2
    step = kappa * (1 - 2 * core)
    same = int(other != core)
    if step == 0:
        return 11 if same else DEAD
    if step < 0:
        return 2 * (-step - 1) + same
    return 6 + 2 * (step - 1) + same if step < 3 or not same else DEAD


PLAN = (24, 2 * SLOTS)
COUNTS, WANTED = 4, 8


class Blocks:
    def __init__(self, plan, near, left, right, sources=None):
        self.plan, self.near, self.left, self.right = plan, near, left, right
        self.sources = sources

    def copy(self, which, chunk):
        source, sem = self.sources[which]
        place = pl.ds(chunk * CHUNK, CHUNK)
        target = (self.near, self.left, self.right)[which]
        return pltpu.make_async_copy(source.at[place], target.at[place], sem.at[chunk])

    def start(self, near_chunks, far_chunks):
        def far_start(chunk, carry):
            self.copy(1, chunk).start()
            self.copy(2, chunk).start()
            return carry

        def near_start(chunk, carry):
            self.copy(0, chunk).start()
            return carry

        lax.fori_loop(0, far_chunks, far_start, 0)
        lax.fori_loop(0, near_chunks, near_start, 0)

    def far_loop(self, body):
        def arrived(chunk, carry):
            self.copy(1, chunk).wait()
            self.copy(2, chunk).wait()
            return carry

        if self.sources is not None:
            lax.fori_loop(0, self.plan[COUNTS, 1], arrived, 0)

        def step(index, carry):
            for part in range(2):
                first = index * 2 + part
                entries = [self.plan[2, first * GROUP + k] for k in range(GROUP)]
                slots = [entry & 255 for entry in entries]
                left = jnp.concatenate([self.left[slot] for slot in slots], axis=0)
                right = jnp.concatenate([self.right[slot] for slot in slots], axis=0)
                lane = lax.broadcasted_iota(jnp.int32, (1, B), 1) // K
                rows = jnp.zeros((1, B), jnp.int32)
                for k in range(GROUP):
                    rows = jnp.where(lane == k, entries[k] >> 8, rows)
                rows = jnp.broadcast_to(rows, (RHS, B))
                body(left, right, rows, [self.plan[3, 2 * first + half] for half in (0, 1)])
            return carry

        lax.fori_loop(0, self.plan[COUNTS, 2], step, 0)

    def near_loop(self, body):
        def step(chunk, carry):
            if self.sources is not None:
                self.copy(0, chunk).wait()
            for part in range(CHUNK):
                body(chunk * CHUNK + part)
            return carry

        lax.fori_loop(0, self.plan[COUNTS, 0], step, 0)


def back_products(blocks, own, acc):
    plan = blocks.plan

    def far(left, right, rows, partners):
        every = dot_t(own[0:CL].reshape(CL * RHS, B), left)
        coef = jnp.zeros((RHS, B), F32)
        for cluster in range(CL):
            coef = jnp.where(rows == cluster, every[cluster * RHS : (cluster + 1) * RHS], coef)
        coef = coef.astype(BF16)
        for half, partner in enumerate(partners):
            part = slice(half * HALF, (half + 1) * HALF)
            acc[partner] += dot(coef[:, part], right[part])

    def near(slot):
        acc[plan[1, slot]] += dot(own[plan[0, slot]], blocks.near[slot])

    blocks.far_loop(far)
    blocks.near_loop(near)


def forward_products(blocks, fetched, acc):
    plan = blocks.plan

    def far(left, right, rows, partners):
        coef = [
            dot_t(fetched[partner], right[half * HALF : (half + 1) * HALF])
            for half, partner in enumerate(partners)
        ]
        coef = jnp.concatenate(coef, axis=1).astype(BF16).astype(F32)
        spread = [jnp.where(rows == cluster, coef, 0.0).astype(BF16) for cluster in range(CL)]
        acc[0:CL] += dot(jnp.concatenate(spread, axis=0), left).reshape(CL, RHS, B)

    def near(slot):
        acc[plan[0, slot]] += dot_t(fetched[plan[1, slot]], blocks.near[slot])

    blocks.far_loop(far)
    blocks.near_loop(near)


def make_plan(me, lists, few, draft):
    core = me % 2
    base = me - core - 6
    lane = lax.broadcasted_iota(jnp.int32, (1, SLOTS), 1)
    row16 = lax.broadcasted_iota(jnp.int32, (16, SLOTS), 0)
    kinds = []
    for kind in (0, 1):
        rows, cols = lists[2 * kind : 2 * kind + 1, :], lists[2 * kind + 1 : 2 * kind + 2, :]
        live = lane < few[0, kind]
        delta = ((cols >> 2) - base) & 15
        partner = jnp.full((1, SLOTS), DEAD, jnp.int32)
        for value in range(14):
            pair = [peer_number(value, a) for a in (0, 1)]
            partner = jnp.where(delta == value, jnp.where(core == 0, pair[0], pair[1]), partner)
        partner = jnp.where(live, partner, DEAD)
        kinds.append((jnp.where(live, rows & (CL - 1), CL), partner, cols & (CL - 1)))
    (near_row, near_rho, near_part), (far_row, far_rho, far_part) = kinds
    wide = lambda x: jnp.broadcast_to(x, (16, SLOTS))
    hot = row16 == wide(far_rho)
    wanted = jnp.maximum(
        jnp.where(row16 == wide(near_rho), wide(near_part).astype(F32), 0.0),
        jnp.where(hot, wide(far_part).astype(F32), 0.0),
    )
    wanted = jnp.max(wanted, axis=1, keepdims=True)
    hot = jnp.where(hot, 1.0, 0.0)
    square = (SLOTS, SLOTS)
    earlier = lax.broadcasted_iota(jnp.int32, square, 0) < lax.broadcasted_iota(jnp.int32, square, 1)
    rank = dot(hot.astype(BF16), jnp.where(earlier, 1.0, 0.0).astype(BF16)).astype(jnp.int32)
    number = wide(jnp.sum(hot, axis=1, keepdims=True)).astype(jnp.int32)
    padded = ((number + (QUAD - 1)) >> 2) << 2
    place = jnp.full((1, SLOTS), -1, jnp.int32)
    quad_rho = jnp.full((1, SLOTS), DEAD, jnp.int32)
    first = jnp.zeros((1, SLOTS), jnp.int32)
    for rho in range(PEERS):
        place = jnp.where(far_rho == rho, rank[rho : rho + 1] + first, place)
        last = first + padded[rho : rho + 1]
        quad_rho = jnp.where((lane * QUAD >= first) & (lane * QUAD < last), rho, quad_rho)
        first = last
    column = jnp.transpose(jnp.broadcast_to(place.astype(F32), square))
    spots = lax.broadcasted_iota(jnp.int32, square, 1).astype(F32)
    hits = jnp.concatenate([jnp.where(column == spots + shift, 1.0, 0.0).astype(BF16) for shift in (0.0, float(SLOTS))], axis=1)
    codes = jnp.where(row16 == 0, wide(lane), jnp.where(row16 == 1, wide(far_row), 1)).astype(F32).astype(BF16)
    found = dot(codes, hits)
    entry = jnp.where(found[2:3] > 0.5, found[0:1] + 256.0 * found[1:2], 256.0 * CL).astype(jnp.int32)
    draft[0:1, 0:SLOTS] = near_row
    draft[1:2, 0:SLOTS] = near_rho
    draft[2:3, :] = entry
    draft[3:4, 0:SLOTS] = quad_rho
    chunks = [(few[0, kind] + (CHUNK - 1)) // CHUNK for kind in (0, 1)]
    numbers = jnp.where(lane == 0, chunks[0], jnp.where(lane == 1, chunks[1], (first + 15) >> 4))
    draft[COUNTS : COUNTS + 1, 0:SLOTS] = numbers
    draft[WANTED : WANTED + 16, 0:SLOTS] = wide(wanted).astype(jnp.int32)


def place_out(rho):
    if rho == 11:
        return 3, 6
    if rho < 6:
        return 3, rho ^ 1
    k, same = divmod(rho - 6, 2)
    return k, 3 * same


def place_in(rho):
    if rho == 11:
        return 4, 6
    if rho < 6:
        return rho // 2, rho % 2
    return 3, rho - 6


MESSAGE = (4, 4, 3)


def back_first(
    me, near_rows, near_cols, far_rows, far_cols, counts, both, near, left, right,
    m1, m2, m3, give, plan, near_held, left_held, right_held,
    own, acc, lists, few, draft, near_sem, left_sem, right_sem, list_sem,
):
    copies = [pltpu.make_async_copy(counts, few, list_sem.at[4])]
    for index, source in enumerate((near_rows, near_cols, far_rows, far_cols)):
        copies.append(pltpu.make_async_copy(source, lists.at[pl.ds(index, 1)], list_sem.at[index]))
    for copy in copies:
        copy.start()
    for cluster in range(CL):
        own[cluster] = both[0, :, cluster * B : (cluster + 1) * B]
    own[CL] = jnp.zeros((RHS, B), BF16)
    draft[...] = jnp.zeros_like(draft)
    copies[0].wait()
    blocks = Blocks(plan, near_held, left_held, right_held, ((near, near_sem), (left, left_sem), (right, right_sem)))
    blocks.start((few[0, 0] + (CHUNK - 1)) // CHUNK, (few[0, 1] + (CHUNK - 1)) // CHUNK)
    for copy in copies[1:]:
        copy.wait()
    make_plan(me[0], lists, few, draft)
    copy = pltpu.make_async_copy(draft, plan, list_sem.at[5])
    copy.start()
    acc[...] = jnp.zeros_like(acc)
    copy.wait()
    back_products(blocks, own, acc)
    outs = (m1, m2, m3, give)
    for rho in range(PEERS):
        message, index = place_out(rho)
        outs[message][index, 0:RHS] = acc[rho]
        outs[message][index, RHS:] = jnp.full((EXTRA, B), plan[WANTED + rho, 0].astype(F32), F32)


def forward_first(
    plan, both, h1, h2, h3, post, diag, near, left, right,
    out,
    fetched, acc, fetch_sem,
):
    halo = (h1, h2, h3)
    copies = []
    for rho in range(PEERS):
        lanes = pl.ds(pl.multiple_of(plan[WANTED + rho, 0] * B, B), B)
        if rho == 11:
            source = both.at[1, :, lanes]
        elif rho < 6:
            source = halo[rho // 2].at[rho % 2, :, lanes]
        else:
            k, same = divmod(rho - 6, 2)
            source = post.at[2 * k + (1 - same if k < 2 else 0), :, lanes]
        copies.append(pltpu.make_async_copy(source, fetched.at[rho], fetch_sem.at[rho]))
    for copy in copies:
        copy.start()
    fetched[DEAD] = jnp.zeros((RHS, B), BF16)
    acc[CL] = jnp.zeros((RHS, B), F32)
    for cluster in range(CL):
        acc[cluster] = dot_t(both[0, :, cluster * B : (cluster + 1) * B], diag[cluster])
    for copy in copies:
        copy.wait()
    forward_products(Blocks(plan, near, left, right), fetched, acc)
    out[...] = acc[0:CL]


def back_second(
    plan, partial, r1, r2, r3, post, got, near, left, right,
    image, rounded, wanted, m1, m2, m3, give,
    own, acc,
):
    ins = (r1, r2, r3, post, got)
    own[CL] = jnp.zeros((RHS, B), BF16)
    acc[...] = jnp.zeros_like(acc)
    places = [place_in(rho) for rho in range(PEERS)]
    for rho, (message, index) in enumerate(places):
        wanted[rho] = ins[message][index, RHS:]
    for cluster in range(CL):
        total = partial[cluster]
        for message, index in places:
            mine = ins[message][index, RHS : RHS + 1] == float(cluster)
            total += jnp.where(jnp.broadcast_to(mine, (RHS, B)), ins[message][index, 0:RHS], 0.0)
        image[:, cluster * B : (cluster + 1) * B] = total
        own[cluster] = total.astype(BF16)
        rounded[cluster] = total.astype(BF16)
    back_products(Blocks(plan, near, left, right), own, acc)
    outs = (m1, m2, m3, give)
    for rho in range(PEERS):
        message, index = place_out(rho)
        outs[message][index, 0:RHS] = acc[rho].astype(BF16)
        pick = jnp.broadcast_to(wanted[rho, 0:1], (RHS, B))
        chosen = jnp.zeros((RHS, B), F32)
        for cluster in range(CL):
            chosen = jnp.where(pick == float(cluster), own[cluster].astype(F32), chosen)
        outs[message][index, RHS:] = chosen.astype(BF16)


def forward_second(
    plan, own, wanted, r1, r2, r3, post, got, diag, near, left, right,
    image,
    fetched, acc,
):
    ins = (r1, r2, r3, post, got)
    fetched[DEAD] = jnp.zeros((RHS, B), BF16)
    acc[CL] = jnp.zeros((RHS, B), F32)
    places = [place_in(rho) for rho in range(PEERS)]
    for rho, (message, index) in enumerate(places):
        fetched[rho] = ins[message][index, RHS:]
    for cluster in range(CL):
        total = dot_t(own[cluster], diag[cluster])
        for rho, (message, index) in enumerate(places):
            mine = wanted[rho, 0:1] == float(cluster)
            total += jnp.where(jnp.broadcast_to(mine, (RHS, B)), ins[message][index, 0:RHS].astype(F32), 0.0)
        acc[cluster] = total
    forward_products(Blocks(plan, near, left, right), fetched, acc)
    for cluster in range(CL):
        image[:, cluster * B : (cluster + 1) * B] = acc[cluster]


SMEM = pl.BlockSpec(memory_space=pltpu.SMEM)
VMEM = pl.BlockSpec(memory_space=pltpu.VMEM)
ANY = pl.BlockSpec(memory_space=pl.ANY)
HBM = pl.BlockSpec(memory_space=pltpu.HBM)


def call(kernel, name, outs, out_specs, in_specs, scratch):
    return pl.pallas_call(
        kernel,
        name=name,
        out_shape=outs,
        in_specs=in_specs,
        out_specs=out_specs,
        scratch_shapes=scratch,
        compiler_params=pltpu.CompilerParams(vmem_limit_bytes=VMEM_BYTES),
        cost_estimate=pl.CostEstimate(flops=2 * 10**9, bytes_accessed=22 * 10**6, transcendentals=0),
    )


def shaped(shape, dtype):
    return jax.ShapeDtypeStruct(shape, dtype)


def message_shapes(rows, dtype):
    return [shaped((n, rows, B), dtype) for n in MESSAGE + (7,)]


def k1(*args):
    held = [pltpu.VMEM(shape, BF16) for shape in ((SLOTS, B, B), (SLOTS, K, B), (SLOTS, K, B))]
    return call(
        back_first, "transposed_products",
        message_shapes(RHS + EXTRA, F32) + [shaped(PLAN, jnp.int32)] + held,
        [VMEM] * 4 + [SMEM] + [VMEM] * 3,
        [SMEM] + [HBM] * 5 + [VMEM] + [HBM] * 3,
        [
            pltpu.VMEM((CL + 1, RHS, B), BF16),
            pltpu.VMEM((PEERS + 1, RHS, B), F32),
            pltpu.VMEM((8, SLOTS), jnp.int32),
            pltpu.SMEM((1, 2), jnp.int32),
            pltpu.VMEM(PLAN, jnp.int32),
        ]
        + [pltpu.SemaphoreType.DMA((n,)) for n in (CHUNKS, CHUNKS, CHUNKS, 6)],
    )(*args)


def k2(*args):
    return call(
        forward_first, "forward_products",
        shaped((CL, RHS, B), F32), VMEM,
        [SMEM] + [VMEM] + [ANY] * 4 + [VMEM] * 4,
        [
            pltpu.VMEM((PEERS + 1, RHS, B), BF16),
            pltpu.VMEM((CL + 1, RHS, B), F32),
            pltpu.SemaphoreType.DMA((PEERS,)),
        ],
    )(*args)


def k3(*args):
    return call(
        back_second, "image_and_transposed_products",
        [
            shaped((RHS, CL * B), F32),
            shaped((CL, RHS, B), BF16),
            shaped((PEERS, EXTRA, B), F32),
        ]
        + message_shapes(2 * RHS, BF16),
        [VMEM] * 7,
        [SMEM] + [VMEM] * 9,
        [pltpu.VMEM((CL + 1, RHS, B), BF16), pltpu.VMEM((PEERS + 1, RHS, B), F32)],
    )(*args)


def k4(*args):
    return call(
        forward_second, "second_image",
        shaped((RHS, CL * B), F32), VMEM,
        [SMEM] + [VMEM] * 11,
        [pltpu.VMEM((PEERS + 1, RHS, B), BF16), pltpu.VMEM((CL + 1, RHS, B), F32)],
    )(*args)


def carriers(size, k):
    pairs = []
    for chip in range(size // 2):
        for core in range(2):
            step = k if core == 0 else -k
            pairs.append((2 * chip + core, (2 * (chip + step) + core) % size))
    return pairs


def per_device(
    vectors, diag_blocks, near_blocks, near_rows, near_cols, far_left, far_right, far_rows, far_cols, counts
):
    size = lax.axis_size("rows")
    me = lax.axis_index("rows").reshape(1)

    def swap(block):
        return lax.ppermute(block, "rows", [(i, i ^ 1) for i in range(size)])

    def carry(block, k):
        return lax.ppermute(block, "rows", carriers(size, k))

    def exchange(m1, m2, m3, give):
        got = swap(give)
        messages = []
        for k, message in enumerate((m1, m2, m3)):
            messages.append(lax.dynamic_update_slice(message, got[2 * k : 2 * k + 2], (1, 0, 0)))
        return [carry(message, k + 1) for k, message in enumerate(messages)] + [got, messages]

    def passed_on(r1, r2, r3):
        return swap(jnp.concatenate([r1[2:4], r2[2:4], r3[2:3]]))

    def in_hbm(x):
        return pltpu.with_memory_space_constraint(x, pltpu.HBM)

    lists = [in_hbm(x.reshape(1, SLOTS)) for x in (near_rows, near_cols, far_rows, far_cols)]
    sib = swap(vectors)
    both = jnp.stack([vectors, sib])
    halo = [carry(both, k) for k in (1, 2, 3)]
    m1, m2, m3, give, plan, *held = k1(
        me, *lists, in_hbm(counts), both, in_hbm(near_blocks), in_hbm(far_left), in_hbm(far_right)
    )
    r1, r2, r3, got, messages = exchange(m1, m2, m3, give)
    halo_post = swap(jnp.concatenate([halo[0], halo[1], halo[2][1:]]))
    halo_post, messages = lax.optimization_barrier((halo_post, messages))
    partial = k2(plan, both, *halo, halo_post, diag_blocks, *held)
    partial, r1, r2, r3 = lax.optimization_barrier((partial, r1, r2, r3))
    post = passed_on(r1, r2, r3)
    first_image, rounded, wanted, m1, m2, m3, give = k3(plan, partial, r1, r2, r3, post, got, *held)
    r1, r2, r3, got, messages = exchange(m1, m2, m3, give)
    post = passed_on(r1, r2, r3)
    second_image = k4(plan, rounded, wanted, r1, r2, r3, post, got, diag_blocks, *held)
    return first_image, second_image


def solution(mesh):
    return jax.shard_map(
        per_device,
        mesh=mesh,
        in_specs=(
            P(None, "rows"),
            P("rows", None, None),
            P("rows", None, None),
            P("rows"),
            P("rows"),
            P("rows", None, None),
            P("rows", None, None),
            P("rows"),
            P("rows"),
            P("rows", None),
        ),
        out_specs=(P(None, "rows"), P(None, "rows")),
        check_vma=False,
    )
```

```python
import functools

import jax
import jax.numpy as jnp
from jax import lax
from jax.experimental import pallas as pl
from jax.experimental.pallas import tpu as pltpu
from jax.sharding import PartitionSpec as P

RHS, B, K = 64, 256, 32
CL, SLOTS, CHUNK = 4, 128, 16
CHUNKS = SLOTS // CHUNK
GROUP = B // K
HALF = B // 2
PEERS = 12
DEAD = 12
EXTRA = 8
QUAD = 4
VMEM_BYTES = 16 * 2**20
F32, BF16 = jnp.float32, jnp.bfloat16


def dot(x, y):
    return lax.dot_general(x, y, (((1,), (0,)), ((), ())), preferred_element_type=F32)


def dot_t(x, y):
    return lax.dot_general(x, y, (((1,), (1,)), ((), ())), preferred_element_type=F32)


def peer_number(delta, core):
    kappa, other = delta // 2 - 3, delta % 2
    step = kappa * (1 - 2 * core)
    same = int(other != core)
    if step == 0:
        return 11 if same else DEAD
    if step < 0:
        return 2 * (-step - 1) + same
    return 6 + 2 * (step - 1) + same if step < 3 or not same else DEAD


PLAN = (4, 2 * SLOTS)
COUNTS, WANTED = 64, 80
STEP = 32
GROUPS = 4


class Blocks:
    def __init__(self, plan, near, left, right, sources=None):
        self.plan, self.near, self.left, self.right = plan, near, left, right
        self.sources = sources

    def copy(self, which, chunk):
        source, sem = self.sources[which]
        place = pl.ds(chunk * CHUNK, CHUNK)
        target = (self.near, self.left, self.right)[which]
        return pltpu.make_async_copy(source.at[place], target.at[place], sem.at[chunk])

    def start(self):
        for which in (1, 2, 0):
            self.copy(which, 0).start()

    def start_rest(self, near_chunks, far_chunks):
        def far_start(chunk, carry):
            self.copy(1, chunk).start()
            self.copy(2, chunk).start()
            return carry

        def near_start(chunk, carry):
            self.copy(0, chunk).start()
            return carry

        lax.fori_loop(1, far_chunks, far_start, 0)
        lax.fori_loop(1, near_chunks, near_start, 0)

    def far_loop(self, body):
        def arrived(chunk, carry):
            self.copy(1, chunk).wait()
            self.copy(2, chunk).wait()
            return carry

        if self.sources is not None:
            lax.fori_loop(0, self.plan[2, COUNTS + 1], arrived, 0)

        def step(index, carry):
            groups = []
            for part in range(GROUPS):
                first = index * GROUPS + part
                entries = [self.plan[1, first * GROUP + k] for k in range(GROUP)]
                slots = [entry & 255 for entry in entries]
                left = jnp.concatenate([self.left[slot] for slot in slots], axis=0)
                right = jnp.concatenate([self.right[slot] for slot in slots], axis=0)
                lane = lax.broadcasted_iota(jnp.int32, (1, B), 1) // K
                rows = jnp.zeros((1, B), jnp.int32)
                for k in range(GROUP):
                    rows = jnp.where(lane == k, entries[k] >> 8, rows)
                rows = jnp.broadcast_to(rows, (RHS, B))
                groups.append((left, right, rows, [self.plan[2, 2 * first + half] for half in (0, 1)]))
            body(groups)
            return carry

        lax.fori_loop(0, self.plan[2, COUNTS + 2], step, 0)

    def near_loop(self, body):
        size = STEP if self.sources is None else CHUNK

        def step(index, carry):
            if self.sources is not None:
                self.copy(0, index).wait()
            for part in range(size):
                slot = index * size + part
                code = self.plan[0, slot]
                body(part, code & 7, code >> 3, self.near[slot])
            return carry

        lax.fori_loop(0, self.plan[2, COUNTS] * (STEP // size), step, 0)


def halves(x, axis):
    return (x[:HALF], x[HALF:]) if axis == 0 else (x[:, :HALF], x[:, HALF:])


def back_products(blocks, own, acc):
    def far(groups):
        coefs = []
        for left, right, rows, partners in groups:
            every = dot_t(own[0:CL].reshape(CL * RHS, B), left)
            coef = jnp.zeros((RHS, B), F32)
            for cluster in range(CL):
                coef = jnp.where(rows == cluster, every[cluster * RHS : (cluster + 1) * RHS], coef)
            coefs.append(coef.astype(BF16))
        terms = []
        for coef, (left, right, rows, partners) in zip(coefs, groups):
            for part, block, partner in zip(halves(coef, 1), halves(right, 0), partners):
                terms.append((partner, dot(part, block)))
        for partner, term in terms:
            acc[partner] += term

    def near(part, row, partner, block):
        acc[partner] += dot(own[row], block)

    blocks.far_loop(far)
    blocks.near_loop(near)


def forward_products(blocks, fetched, turned, acc, acc_turned):
    turned[DEAD] = jnp.zeros((B, RHS), BF16)
    for partner in range(PEERS):
        turned[partner] = fetched[partner].T
    acc_turned[...] = jnp.zeros_like(acc_turned)

    def far(groups):
        spreads = []
        for left, right, rows, partners in groups:
            coef = [dot_t(fetched[partner], block) for partner, block in zip(partners, halves(right, 0))]
            coef = jnp.concatenate(coef, axis=1).astype(BF16).astype(F32)
            spread = [jnp.where(rows == cluster, coef, 0.0).astype(BF16) for cluster in range(CL)]
            spreads.append(jnp.concatenate(spread, axis=0))
        terms = [dot(spread, group[0]) for spread, group in zip(spreads, groups)]
        total = terms[0]
        for term in terms[1:]:
            total += term
        acc[0:CL] += total.reshape(CL, RHS, B)

    def near(part, row, partner, block):
        if part % 2 == 0:
            acc[row] += dot_t(fetched[partner], block)
        else:
            acc_turned[row] += dot(block, turned[partner])

    blocks.far_loop(far)
    blocks.near_loop(near)
    for cluster in range(CL):
        acc[cluster] += acc_turned[cluster].T


def make_plan(me, lists, few, draft):
    core = me % 2
    base = me - core - 6
    lane = lax.broadcasted_iota(jnp.int32, (1, SLOTS), 1)
    row16 = lax.broadcasted_iota(jnp.int32, (16, SLOTS), 0)
    kinds = []
    for kind in (0, 1):
        rows, cols = lists[2 * kind : 2 * kind + 1, :], lists[2 * kind + 1 : 2 * kind + 2, :]
        live = lane < few[0, kind]
        delta = ((cols >> 2) - base) & 15
        partner = jnp.full((1, SLOTS), DEAD, jnp.int32)
        for value in range(14):
            pair = [peer_number(value, a) for a in (0, 1)]
            partner = jnp.where(delta == value, jnp.where(core == 0, pair[0], pair[1]), partner)
        partner = jnp.where(live, partner, DEAD)
        kinds.append((jnp.where(live, rows & (CL - 1), CL), partner, cols & (CL - 1)))
    (near_row, near_rho, near_part), (far_row, far_rho, far_part) = kinds
    wide = lambda x: jnp.broadcast_to(x, (16, SLOTS))
    hot = row16 == wide(far_rho)
    wanted = jnp.maximum(
        jnp.where(row16 == wide(near_rho), wide(near_part).astype(F32), 0.0),
        jnp.where(hot, wide(far_part).astype(F32), 0.0),
    )
    wanted = jnp.max(wanted, axis=1, keepdims=True)
    hot = jnp.where(hot, 1.0, 0.0)
    square = (SLOTS, SLOTS)
    earlier = lax.broadcasted_iota(jnp.int32, square, 0) < lax.broadcasted_iota(jnp.int32, square, 1)
    rank = dot(hot.astype(BF16), jnp.where(earlier, 1.0, 0.0).astype(BF16)).astype(jnp.int32)
    number = wide(jnp.sum(hot, axis=1, keepdims=True)).astype(jnp.int32)
    padded = ((number + (QUAD - 1)) >> 2) << 2
    place = jnp.full((1, SLOTS), -1, jnp.int32)
    quad_rho = jnp.full((1, SLOTS), DEAD, jnp.int32)
    first = jnp.zeros((1, SLOTS), jnp.int32)
    for rho in range(PEERS):
        place = jnp.where(far_rho == rho, rank[rho : rho + 1] + first, place)
        last = first + padded[rho : rho + 1]
        quad_rho = jnp.where((lane * QUAD >= first) & (lane * QUAD < last), rho, quad_rho)
        first = last
    column = jnp.transpose(jnp.broadcast_to(place.astype(F32), square))
    spots = lax.broadcasted_iota(jnp.int32, square, 1).astype(F32)
    hits = jnp.concatenate([jnp.where(column == spots + shift, 1.0, 0.0).astype(BF16) for shift in (0.0, float(SLOTS))], axis=1)
    codes = jnp.where(row16 == 0, wide(lane), jnp.where(row16 == 1, wide(far_row), 1)).astype(F32).astype(BF16)
    found = dot(codes, hits)
    entry = jnp.where(found[2:3] > 0.5, found[0:1] + 256.0 * found[1:2], 256.0 * CL).astype(jnp.int32)
    wanted = jnp.sum(jnp.where(row16 + WANTED == wide(lane), wide(wanted), 0.0), axis=0, keepdims=True).astype(jnp.int32)
    draft[0:1, 0:SLOTS] = near_row + 8 * near_rho
    draft[1:2, :] = entry
    numbers = jnp.where(lane == COUNTS, (few[0, 0] + (STEP - 1)) // STEP, jnp.where(lane < COUNTS, quad_rho, wanted))
    numbers = jnp.where(lane == COUNTS + 1, (few[0, 1] + (CHUNK - 1)) // CHUNK, numbers)
    steps = (first + (2 * GROUPS * QUAD - 1)) >> (GROUPS.bit_length() + 2)
    draft[2:3, 0:SLOTS] = jnp.where(lane == COUNTS + 2, steps, numbers)


def place_out(rho):
    if rho == 11:
        return 3, 6
    if rho < 6:
        return 3, rho ^ 1
    k, same = divmod(rho - 6, 2)
    return k, 3 * same


def place_in(rho):
    if rho == 11:
        return 4, 6
    if rho < 6:
        return rho // 2, rho % 2
    return 3, rho - 6


MESSAGE = (4, 4, 3)


def back_first(
    me, near_rows, near_cols, far_rows, far_cols, counts, both, near, left, right,
    m1, m2, m3, give, plan, near_held, left_held, right_held,
    own, acc, lists, few, draft, near_sem, left_sem, right_sem, list_sem,
):
    blocks = Blocks(plan, near_held, left_held, right_held, ((near, near_sem), (left, left_sem), (right, right_sem)))
    copies = [pltpu.make_async_copy(counts, few, list_sem.at[4])]
    for index, source in enumerate((near_rows, near_cols, far_rows, far_cols)):
        copies.append(pltpu.make_async_copy(source, lists.at[pl.ds(index, 1)], list_sem.at[index]))
    for copy in copies:
        copy.start()
    blocks.start()
    for cluster in range(CL):
        own[cluster] = both[0, :, cluster * B : (cluster + 1) * B]
    own[CL] = jnp.zeros((RHS, B), BF16)
    draft[...] = jnp.zeros_like(draft)
    copies[0].wait()
    near_steps = (few[0, 0] + (STEP - 1)) // STEP
    blocks.start_rest(near_steps * (STEP // CHUNK), (few[0, 1] + (CHUNK - 1)) // CHUNK)
    for copy in copies[1:]:
        copy.wait()
    make_plan(me[0], lists, few, draft)
    copy = pltpu.make_async_copy(draft, plan, list_sem.at[5])
    copy.start()
    acc[...] = jnp.zeros_like(acc)
    copy.wait()
    back_products(blocks, own, acc)
    outs = (m1, m2, m3, give)
    for rho in range(PEERS):
        message, index = place_out(rho)
        outs[message][index, 0:RHS] = acc[rho]
        outs[message][index, RHS:] = jnp.full((EXTRA, B), plan[2, WANTED + rho].astype(F32), F32)


def forward_first(
    plan, both, h1, h2, h3, post, diag, near, left, right,
    out,
    fetched, turned, acc, acc_turned,
):
    halo = (h1, h2, h3)
    for rho in range(PEERS):
        lanes = pl.ds(pl.multiple_of(plan[2, WANTED + rho] * B, B), B)
        if rho == 11:
            fetched[rho] = both[1, :, lanes]
        elif rho < 6:
            fetched[rho] = halo[rho // 2][rho % 2, :, lanes]
        else:
            k, same = divmod(rho - 6, 2)
            fetched[rho] = post[2 * k + (1 - same if k < 2 else 0), :, lanes]
    fetched[DEAD] = jnp.zeros((RHS, B), BF16)
    acc[CL] = jnp.zeros((RHS, B), F32)
    for cluster in range(CL):
        acc[cluster] = dot_t(both[0, :, cluster * B : (cluster + 1) * B], diag[cluster])
    forward_products(Blocks(plan, near, left, right), fetched, turned, acc, acc_turned)
    out[...] = acc[0:CL]


STRIP = 16


def back_second(
    plan, partial, r1, r2, r3, post, got, near, left, right,
    image, rounded, wanted, m1, m2, m3, give,
    own, acc, draft, sem,
):
    ins = (r1, r2, r3, post, got)
    own[CL] = jnp.zeros((RHS, B), BF16)
    acc[...] = jnp.zeros_like(acc)
    places = [place_in(rho) for rho in range(PEERS)]
    marks = [ins[message][index, RHS : RHS + 1] for message, index in places]
    lane = lax.broadcasted_iota(jnp.int32, (1, SLOTS), 1)
    packed = jnp.zeros((1, SLOTS), F32)
    for rho, mark in enumerate(marks):
        packed = jnp.where(lane == rho, mark[:, 0:SLOTS], packed)
    draft[...] = packed.astype(jnp.int32)
    copy = pltpu.make_async_copy(draft, wanted, sem)
    copy.start()
    for first in range(0, RHS, STRIP):
        rows = slice(first, first + STRIP)
        totals = [partial[cluster, rows] for cluster in range(CL)]
        for (message, index), mark in zip(places, marks):
            block = ins[message][index, rows]
            mark = jnp.broadcast_to(mark, (STRIP, B))
            for cluster in range(CL):
                totals[cluster] += jnp.where(mark == float(cluster), block, 0.0)
        for cluster in range(CL):
            image[rows, cluster * B : (cluster + 1) * B] = totals[cluster]
            own[cluster, rows] = totals[cluster].astype(BF16)
            rounded[cluster, rows] = totals[cluster].astype(BF16)
    back_products(Blocks(plan, near, left, right), own, acc)
    outs = (m1, m2, m3, give)
    copy.wait()
    for rho in range(PEERS):
        message, index = place_out(rho)
        outs[message][index, 0:RHS] = acc[rho].astype(BF16)
        outs[message][index, RHS:] = own[wanted[0, rho]]


def forward_second(
    plan, wanted, own, r1, r2, r3, post, got, diag, near, left, right,
    image,
    fetched, turned, acc, acc_turned,
):
    ins = (r1, r2, r3, post, got)
    fetched[DEAD] = jnp.zeros((RHS, B), BF16)
    acc[CL] = jnp.zeros((RHS, B), F32)
    for cluster in range(CL):
        acc[cluster] = dot_t(own[cluster], diag[cluster])
    for rho in range(PEERS):
        message, index = place_in(rho)
        fetched[rho] = ins[message][index, RHS:]
        acc[wanted[0, rho]] += ins[message][index, 0:RHS].astype(F32)
    forward_products(Blocks(plan, near, left, right), fetched, turned, acc, acc_turned)
    for cluster in range(CL):
        image[:, cluster * B : (cluster + 1) * B] = acc[cluster]


SMEM = pl.BlockSpec(memory_space=pltpu.SMEM)
VMEM = pl.BlockSpec(memory_space=pltpu.VMEM)
ANY = pl.BlockSpec(memory_space=pl.ANY)
HBM = pl.BlockSpec(memory_space=pltpu.HBM)


def call(kernel, name, outs, out_specs, in_specs, scratch):
    return pl.pallas_call(
        kernel,
        name=name,
        out_shape=outs,
        in_specs=in_specs,
        out_specs=out_specs,
        scratch_shapes=scratch,
        compiler_params=pltpu.CompilerParams(vmem_limit_bytes=VMEM_BYTES),
        cost_estimate=pl.CostEstimate(flops=2 * 10**9, bytes_accessed=22 * 10**6, transcendentals=0),
    )


def shaped(shape, dtype):
    return jax.ShapeDtypeStruct(shape, dtype)


def message_shapes(rows, dtype):
    return [shaped((n, rows, B), dtype) for n in MESSAGE + (7,)]


def k1(*args):
    held = [pltpu.VMEM(shape, BF16) for shape in ((SLOTS, B, B), (SLOTS, K, B), (SLOTS, K, B))]
    return call(
        back_first, "transposed_products",
        message_shapes(RHS + EXTRA, F32) + [shaped(PLAN, jnp.int32)] + held,
        [VMEM] * 4 + [SMEM] + [VMEM] * 3,
        [SMEM] + [HBM] * 5 + [VMEM] + [HBM] * 3,
        [
            pltpu.VMEM((CL + 1, RHS, B), BF16),
            pltpu.VMEM((PEERS + 1, RHS, B), F32),
            pltpu.VMEM((8, SLOTS), jnp.int32),
            pltpu.SMEM((1, 2), jnp.int32),
            pltpu.VMEM(PLAN, jnp.int32),
        ]
        + [pltpu.SemaphoreType.DMA((n,)) for n in (CHUNKS, CHUNKS, CHUNKS, 6)],
    )(*args)


def forward_scratch():
    return [
        pltpu.VMEM((PEERS + 1, RHS, B), BF16),
        pltpu.VMEM((PEERS + 1, B, RHS), BF16),
        pltpu.VMEM((CL + 1, RHS, B), F32),
        pltpu.VMEM((CL + 1, B, RHS), F32),
    ]


def k2(*args):
    return call(
        forward_first, "forward_products",
        shaped((CL, RHS, B), F32), VMEM,
        [SMEM] + [VMEM] * 9,
        forward_scratch(),
    )(*args)


def k3(*args):
    return call(
        back_second, "image_and_transposed_products",
        [
            shaped((RHS, CL * B), F32),
            shaped((CL, RHS, B), BF16),
            shaped((1, SLOTS), jnp.int32),
        ]
        + message_shapes(2 * RHS, BF16),
        [VMEM] * 2 + [SMEM] + [VMEM] * 4,
        [SMEM] + [VMEM] * 9,
        [
            pltpu.VMEM((CL + 1, RHS, B), BF16),
            pltpu.VMEM((PEERS + 1, RHS, B), F32),
            pltpu.VMEM((1, SLOTS), jnp.int32),
            pltpu.SemaphoreType.DMA,
        ],
    )(*args)


def k4(*args):
    return call(
        forward_second, "second_image",
        shaped((RHS, CL * B), F32), VMEM,
        [SMEM] * 2 + [VMEM] * 10,
        forward_scratch(),
    )(*args)


def carriers(size, k):
    pairs = []
    for chip in range(size // 2):
        for core in range(2):
            step = k if core == 0 else -k
            pairs.append((2 * chip + core, (2 * (chip + step) + core) % size))
    return pairs


def per_device(
    vectors, diag_blocks, near_blocks, near_rows, near_cols, far_left, far_right, far_rows, far_cols, counts
):
    size = lax.axis_size("rows")
    me = lax.axis_index("rows").reshape(1)

    def swap(block):
        return lax.ppermute(block, "rows", [(i, i ^ 1) for i in range(size)])

    def carry(block, k):
        return lax.ppermute(block, "rows", carriers(size, k))

    def exchange(m1, m2, m3, give):
        got = swap(give)
        messages = []
        for k, message in enumerate((m1, m2, m3)):
            messages.append(lax.dynamic_update_slice(message, got[2 * k : 2 * k + 2], (1, 0, 0)))
        return [carry(message, k + 1) for k, message in enumerate(messages)] + [got, messages]

    def passed_on(r1, r2, r3):
        return swap(jnp.concatenate([r1[2:4], r2[2:4], r3[2:3]]))

    def in_hbm(x):
        return pltpu.with_memory_space_constraint(x, pltpu.HBM)

    lists = [in_hbm(x.reshape(1, SLOTS)) for x in (near_rows, near_cols, far_rows, far_cols)]
    sib = swap(vectors)
    both = jnp.stack([vectors, sib])
    halo = [carry(both, k) for k in (1, 2, 3)]
    m1, m2, m3, give, plan, *held = k1(
        me, *lists, in_hbm(counts), both, in_hbm(near_blocks), in_hbm(far_left), in_hbm(far_right)
    )
    r1, r2, r3, got, messages = exchange(m1, m2, m3, give)
    halo_post = swap(jnp.concatenate([halo[0], halo[1], halo[2][1:]]))
    halo_post, messages = lax.optimization_barrier((halo_post, messages))
    partial = k2(plan, both, *halo, halo_post, diag_blocks, *held)
    partial, r1, r2, r3 = lax.optimization_barrier((partial, r1, r2, r3))
    post = passed_on(r1, r2, r3)
    first_image, rounded, wanted, m1, m2, m3, give = k3(plan, partial, r1, r2, r3, post, got, *held)
    r1, r2, r3, got, messages = exchange(m1, m2, m3, give)
    post = passed_on(r1, r2, r3)
    second_image = k4(plan, wanted, rounded, r1, r2, r3, post, got, diag_blocks, *held)
    return first_image, second_image


def solution(mesh):
    return jax.shard_map(
        per_device,
        mesh=mesh,
        in_specs=(
            P(None, "rows"),
            P("rows", None, None),
            P("rows", None, None),
            P("rows"),
            P("rows"),
            P("rows", None, None),
            P("rows", None, None),
            P("rows"),
            P("rows"),
            P("rows", None),
        ),
        out_specs=(P(None, "rows"), P(None, "rows")),
        check_vma=False,
    )
```

```python
import functools

import jax
import jax.numpy as jnp
from jax import lax
from jax.experimental import pallas as pl
from jax.experimental.pallas import tpu as pltpu
from jax.sharding import PartitionSpec as P

RHS, B, K = 64, 256, 32
CL, SLOTS, CHUNK = 4, 128, 16
CHUNKS = SLOTS // CHUNK
GROUP = B // K
HALF = B // 2
PEERS = 12
DEAD = 12
EXTRA = 8
QUAD = 4
VMEM_BYTES = 16 * 2**20
F32, BF16 = jnp.float32, jnp.bfloat16


def dot(x, y):
    return lax.dot_general(x, y, (((1,), (0,)), ((), ())), preferred_element_type=F32)


def dot_t(x, y):
    return lax.dot_general(x, y, (((1,), (1,)), ((), ())), preferred_element_type=F32)


def peer_number(delta, core):
    kappa, other = delta // 2 - 3, delta % 2
    step = kappa * (1 - 2 * core)
    same = int(other != core)
    if step == 0:
        return 11 if same else DEAD
    if step < 0:
        return 2 * (-step - 1) + same
    return 6 + 2 * (step - 1) + same if step < 3 or not same else DEAD


PLAN = (4, 2 * SLOTS)
COUNTS, WANTED = 64, 80
STEP = 32
GROUPS = 4


class Blocks:
    def __init__(self, plan, near, left, right, sources=None):
        self.plan, self.near, self.left, self.right = plan, near, left, right
        self.sources = sources

    def copy(self, which, chunk):
        source, sem = self.sources[which]
        place = pl.ds(chunk * CHUNK, CHUNK)
        target = (self.near, self.left, self.right)[which]
        return pltpu.make_async_copy(source.at[place], target.at[place], sem.at[chunk])

    def start(self):
        for which in (1, 2, 0):
            self.copy(which, 0).start()

    def start_rest(self, near_chunks, far_chunks):
        def far_start(chunk, carry):
            self.copy(1, chunk).start()
            self.copy(2, chunk).start()
            return carry

        def near_start(chunk, carry):
            self.copy(0, chunk).start()
            return carry

        lax.fori_loop(1, far_chunks, far_start, 0)
        lax.fori_loop(1, near_chunks, near_start, 0)

    def far_loop(self, body):
        def arrived(chunk, carry):
            self.copy(1, chunk).wait()
            self.copy(2, chunk).wait()
            return carry

        if self.sources is not None:
            lax.fori_loop(0, self.plan[2, COUNTS + 1], arrived, 0)

        def step(index, carry):
            groups = []
            for part in range(GROUPS):
                first = index * GROUPS + part
                entries = [self.plan[1, first * GROUP + k] for k in range(GROUP)]
                slots = [entry & 255 for entry in entries]
                left = jnp.concatenate([self.left[slot] for slot in slots], axis=0)
                right = jnp.concatenate([self.right[slot] for slot in slots], axis=0)
                lane = lax.broadcasted_iota(jnp.int32, (1, B), 1) // K
                rows = jnp.zeros((1, B), jnp.int32)
                for k in range(GROUP):
                    rows = jnp.where(lane == k, entries[k] >> 8, rows)
                rows = jnp.broadcast_to(rows, (RHS, B))
                groups.append((left, right, rows, [self.plan[2, 2 * first + half] for half in (0, 1)]))
            body(groups)
            return carry

        lax.fori_loop(0, self.plan[2, COUNTS + 2], step, 0)

    def near_loop(self, body):
        size = STEP if self.sources is None else CHUNK

        def step(index, carry):
            if self.sources is not None:
                self.copy(0, index).wait()
            for part in range(size):
                slot = index * size + part
                code = self.plan[0, slot]
                body(part, code & 7, code >> 3, self.near[slot])
            return carry

        lax.fori_loop(0, self.plan[2, COUNTS] * (STEP // size), step, 0)


def halves(x, axis):
    return (x[:HALF], x[HALF:]) if axis == 0 else (x[:, :HALF], x[:, HALF:])


def back_products(blocks, own, acc):
    def far(groups):
        coefs = []
        for left, right, rows, partners in groups:
            every = dot_t(own[0:CL].reshape(CL * RHS, B), left)
            coef = jnp.zeros((RHS, B), F32)
            for cluster in range(CL):
                coef = jnp.where(rows == cluster, every[cluster * RHS : (cluster + 1) * RHS], coef)
            coefs.append(coef.astype(BF16))
        terms = []
        for coef, (left, right, rows, partners) in zip(coefs, groups):
            for part, block, partner in zip(halves(coef, 1), halves(right, 0), partners):
                terms.append((partner, dot(part, block)))
        for partner, term in terms:
            acc[partner] += term

    def near(part, row, partner, block):
        acc[partner] += dot(own[row], block)

    blocks.far_loop(far)
    blocks.near_loop(near)


def forward_products(blocks, fetched, turned, acc, acc_turned):
    turned[DEAD] = jnp.zeros((B, RHS), BF16)
    for partner in range(PEERS):
        turned[partner] = fetched[partner].T
    acc_turned[...] = jnp.zeros_like(acc_turned)

    def far(groups):
        spreads = []
        for left, right, rows, partners in groups:
            coef = [dot_t(fetched[partner], block) for partner, block in zip(partners, halves(right, 0))]
            coef = jnp.concatenate(coef, axis=1).astype(BF16).astype(F32)
            spread = [jnp.where(rows == cluster, coef, 0.0).astype(BF16) for cluster in range(CL)]
            spreads.append(jnp.concatenate(spread, axis=0))
        terms = [dot(spread, group[0]) for spread, group in zip(spreads, groups)]
        total = terms[0]
        for term in terms[1:]:
            total += term
        acc[0:CL] += total.reshape(CL, RHS, B)

    def near(part, row, partner, block):
        if part % 2 == 0:
            acc[row] += dot_t(fetched[partner], block)
        else:
            acc_turned[row] += dot(block, turned[partner])

    blocks.far_loop(far)
    blocks.near_loop(near)
    for cluster in range(CL):
        acc[cluster] += acc_turned[cluster].T


def make_plan(me, lists, few, draft):
    core = me % 2
    base = me - core - 6
    lane = lax.broadcasted_iota(jnp.int32, (1, SLOTS), 1)
    row16 = lax.broadcasted_iota(jnp.int32, (16, SLOTS), 0)
    kinds = []
    for kind in (0, 1):
        rows, cols = lists[2 * kind : 2 * kind + 1, :], lists[2 * kind + 1 : 2 * kind + 2, :]
        live = lane < few[0, kind]
        delta = ((cols >> 2) - base) & 15
        partner = jnp.full((1, SLOTS), DEAD, jnp.int32)
        for value in range(14):
            pair = [peer_number(value, a) for a in (0, 1)]
            partner = jnp.where(delta == value, jnp.where(core == 0, pair[0], pair[1]), partner)
        partner = jnp.where(live, partner, DEAD)
        kinds.append((jnp.where(live, rows & (CL - 1), CL), partner, cols & (CL - 1)))
    (near_row, near_rho, near_part), (far_row, far_rho, far_part) = kinds
    wide = lambda x: jnp.broadcast_to(x, (16, SLOTS))
    hot = row16 == wide(far_rho)
    wanted = jnp.maximum(
        jnp.where(row16 == wide(near_rho), wide(near_part).astype(F32), 0.0),
        jnp.where(hot, wide(far_part).astype(F32), 0.0),
    )
    wanted = jnp.max(wanted, axis=1, keepdims=True)
    hot = jnp.where(hot, 1.0, 0.0)
    square = (SLOTS, SLOTS)
    earlier = lax.broadcasted_iota(jnp.int32, square, 0) < lax.broadcasted_iota(jnp.int32, square, 1)
    rank = dot(hot.astype(BF16), jnp.where(earlier, 1.0, 0.0).astype(BF16)).astype(jnp.int32)
    number = wide(jnp.sum(hot, axis=1, keepdims=True)).astype(jnp.int32)
    padded = ((number + (QUAD - 1)) >> 2) << 2
    place = jnp.full((1, SLOTS), -1, jnp.int32)
    quad_rho = jnp.full((1, SLOTS), DEAD, jnp.int32)
    first = jnp.zeros((1, SLOTS), jnp.int32)
    for rho in range(PEERS):
        place = jnp.where(far_rho == rho, rank[rho : rho + 1] + first, place)
        last = first + padded[rho : rho + 1]
        quad_rho = jnp.where((lane * QUAD >= first) & (lane * QUAD < last), rho, quad_rho)
        first = last
    column = jnp.transpose(jnp.broadcast_to(place.astype(F32), square))
    spots = lax.broadcasted_iota(jnp.int32, square, 1).astype(F32)
    hits = jnp.concatenate([jnp.where(column == spots + shift, 1.0, 0.0).astype(BF16) for shift in (0.0, float(SLOTS))], axis=1)
    codes = jnp.where(row16 == 0, wide(lane), jnp.where(row16 == 1, wide(far_row), 1)).astype(F32).astype(BF16)
    found = dot(codes, hits)
    entry = jnp.where(found[2:3] > 0.5, found[0:1] + 256.0 * found[1:2], 256.0 * CL).astype(jnp.int32)
    wanted = jnp.sum(jnp.where(row16 + WANTED == wide(lane), wide(wanted), 0.0), axis=0, keepdims=True).astype(jnp.int32)
    draft[0:1, 0:SLOTS] = near_row + 8 * near_rho
    draft[1:2, :] = entry
    numbers = jnp.where(lane == COUNTS, (few[0, 0] + (STEP - 1)) // STEP, jnp.where(lane < COUNTS, quad_rho, wanted))
    numbers = jnp.where(lane == COUNTS + 1, (few[0, 1] + (CHUNK - 1)) // CHUNK, numbers)
    steps = (first + (2 * GROUPS * QUAD - 1)) >> (GROUPS.bit_length() + 2)
    draft[2:3, 0:SLOTS] = jnp.where(lane == COUNTS + 2, steps, numbers)


def place_out(rho):
    if rho == 11:
        return 3, 6
    if rho < 6:
        return 3, rho ^ 1
    k, same = divmod(rho - 6, 2)
    return k, 3 * same


def place_in(rho):
    if rho == 11:
        return 4, 6
    if rho < 6:
        return rho // 2, rho % 2
    return 3, rho - 6


MESSAGE = (4, 4, 3)


def back_first(
    me, near_rows, near_cols, far_rows, far_cols, counts, both, near, left, right,
    m1, m2, m3, give, plan, near_held, left_held, right_held,
    own, acc, lists, few, draft, near_sem, left_sem, right_sem, list_sem,
):
    blocks = Blocks(plan, near_held, left_held, right_held, ((near, near_sem), (left, left_sem), (right, right_sem)))
    copies = [pltpu.make_async_copy(counts, few, list_sem.at[4])]
    for index, source in enumerate((near_rows, near_cols, far_rows, far_cols)):
        copies.append(pltpu.make_async_copy(source, lists.at[pl.ds(index, 1)], list_sem.at[index]))
    for copy in copies:
        copy.start()
    blocks.start()
    for cluster in range(CL):
        own[cluster] = both[0, :, cluster * B : (cluster + 1) * B]
    own[CL] = jnp.zeros((RHS, B), BF16)
    draft[...] = jnp.zeros_like(draft)
    copies[0].wait()
    near_steps = (few[0, 0] + (STEP - 1)) // STEP
    blocks.start_rest(near_steps * (STEP // CHUNK), (few[0, 1] + (CHUNK - 1)) // CHUNK)
    for copy in copies[1:]:
        copy.wait()
    make_plan(me[0], lists, few, draft)
    copy = pltpu.make_async_copy(draft, plan, list_sem.at[5])
    copy.start()
    acc[...] = jnp.zeros_like(acc)
    copy.wait()
    back_products(blocks, own, acc)
    outs = (m1, m2, m3, give)
    for rho in range(PEERS):
        message, index = place_out(rho)
        outs[message][index, 0:RHS] = acc[rho]
        outs[message][index, RHS:] = jnp.full((EXTRA, B), plan[2, WANTED + rho].astype(F32), F32)


def forward_first(
    plan, both, h1, h2, h3, post, diag, near, left, right,
    out,
    fetched, turned, acc, acc_turned,
):
    halo = (h1, h2, h3)
    for rho in range(PEERS):
        lanes = pl.ds(pl.multiple_of(plan[2, WANTED + rho] * B, B), B)
        if rho == 11:
            fetched[rho] = both[1, :, lanes]
        elif rho < 6:
            fetched[rho] = halo[rho // 2][rho % 2, :, lanes]
        else:
            k, same = divmod(rho - 6, 2)
            fetched[rho] = post[2 * k + (1 - same if k < 2 else 0), :, lanes]
    fetched[DEAD] = jnp.zeros((RHS, B), BF16)
    acc[CL] = jnp.zeros((RHS, B), F32)
    for cluster in range(CL):
        acc[cluster] = dot_t(both[0, :, cluster * B : (cluster + 1) * B], diag[cluster])
    forward_products(Blocks(plan, near, left, right), fetched, turned, acc, acc_turned)
    out[...] = acc[0:CL]


STRIP = 16


def image_first(
    partial, r1, r2, r3, post, got,
    image, rounded, wanted, m1, m2, m3, give,
    draft, sem,
):
    ins = (r1, r2, r3, post, got)
    places = [place_in(rho) for rho in range(PEERS)]
    marks = [ins[message][index, RHS : RHS + 1] for message, index in places]
    lane = lax.broadcasted_iota(jnp.int32, (1, SLOTS), 1)
    packed = jnp.zeros((1, SLOTS), F32)
    for rho, mark in enumerate(marks):
        packed = jnp.where(lane == rho, mark[:, 0:SLOTS], packed)
    draft[...] = packed.astype(jnp.int32)
    copy = pltpu.make_async_copy(draft, wanted, sem)
    copy.start()
    for first in range(0, RHS, STRIP):
        rows = slice(first, first + STRIP)
        totals = [partial[cluster, rows] for cluster in range(CL)]
        for (message, index), mark in zip(places, marks):
            block = ins[message][index, rows]
            mark = jnp.broadcast_to(mark, (STRIP, B))
            for cluster in range(CL):
                totals[cluster] += jnp.where(mark == float(cluster), block, 0.0)
        for cluster in range(CL):
            image[rows, cluster * B : (cluster + 1) * B] = totals[cluster]
            rounded[cluster, rows] = totals[cluster].astype(BF16)
    copy.wait()
    outs = (m1, m2, m3, give)
    for rho in range(PEERS):
        message, index = place_out(rho)
        outs[message][index] = rounded[wanted[0, rho]]


def back_second(
    plan, rounded, near, left, right,
    m1, m2, m3, give,
    own, acc,
):
    own[0:CL] = rounded[...]
    own[CL] = jnp.zeros((RHS, B), BF16)
    acc[...] = jnp.zeros_like(acc)
    back_products(Blocks(plan, near, left, right), own, acc)
    outs = (m1, m2, m3, give)
    for rho in range(PEERS):
        message, index = place_out(rho)
        outs[message][index] = acc[rho].astype(BF16)


def forward_second(
    plan, own, r1, r2, r3, post, got, diag, near, left, right,
    out,
    fetched, turned, acc, acc_turned,
):
    ins = (r1, r2, r3, post, got)
    for rho in range(PEERS):
        message, index = place_in(rho)
        fetched[rho] = ins[message][index]
    fetched[DEAD] = jnp.zeros((RHS, B), BF16)
    acc[CL] = jnp.zeros((RHS, B), F32)
    for cluster in range(CL):
        acc[cluster] = dot_t(own[cluster], diag[cluster])
    forward_products(Blocks(plan, near, left, right), fetched, turned, acc, acc_turned)
    out[...] = acc[0:CL]


def image_second(partial, wanted, r1, r2, r3, post, got, image, acc):
    ins = (r1, r2, r3, post, got)
    acc[...] = partial[...]
    for rho in range(PEERS):
        message, index = place_in(rho)
        acc[wanted[0, rho]] += ins[message][index].astype(F32)
    for cluster in range(CL):
        image[:, cluster * B : (cluster + 1) * B] = acc[cluster]


SMEM = pl.BlockSpec(memory_space=pltpu.SMEM)
VMEM = pl.BlockSpec(memory_space=pltpu.VMEM)
ANY = pl.BlockSpec(memory_space=pl.ANY)
HBM = pl.BlockSpec(memory_space=pltpu.HBM)


def call(kernel, name, outs, out_specs, in_specs, scratch):
    return pl.pallas_call(
        kernel,
        name=name,
        out_shape=outs,
        in_specs=in_specs,
        out_specs=out_specs,
        scratch_shapes=scratch,
        compiler_params=pltpu.CompilerParams(vmem_limit_bytes=VMEM_BYTES),
        cost_estimate=pl.CostEstimate(flops=2 * 10**9, bytes_accessed=22 * 10**6, transcendentals=0),
    )


def shaped(shape, dtype):
    return jax.ShapeDtypeStruct(shape, dtype)


def message_shapes(rows, dtype):
    return [shaped((n, rows, B), dtype) for n in MESSAGE + (7,)]


def k1(*args):
    held = [pltpu.VMEM(shape, BF16) for shape in ((SLOTS, B, B), (SLOTS, K, B), (SLOTS, K, B))]
    return call(
        back_first, "transposed_products",
        message_shapes(RHS + EXTRA, F32) + [shaped(PLAN, jnp.int32)] + held,
        [VMEM] * 4 + [SMEM] + [VMEM] * 3,
        [SMEM] + [HBM] * 5 + [VMEM] + [HBM] * 3,
        [
            pltpu.VMEM((CL + 1, RHS, B), BF16),
            pltpu.VMEM((PEERS + 1, RHS, B), F32),
            pltpu.VMEM((8, SLOTS), jnp.int32),
            pltpu.SMEM((1, 2), jnp.int32),
            pltpu.VMEM(PLAN, jnp.int32),
        ]
        + [pltpu.SemaphoreType.DMA((n,)) for n in (CHUNKS, CHUNKS, CHUNKS, 6)],
    )(*args)


def forward_scratch():
    return [
        pltpu.VMEM((PEERS + 1, RHS, B), BF16),
        pltpu.VMEM((PEERS + 1, B, RHS), BF16),
        pltpu.VMEM((CL + 1, RHS, B), F32),
        pltpu.VMEM((CL + 1, B, RHS), F32),
    ]


def k2(*args):
    return call(
        forward_first, "forward_products",
        shaped((CL, RHS, B), F32), VMEM,
        [SMEM] + [VMEM] * 9,
        forward_scratch(),
    )(*args)


def k3(*args):
    return call(
        image_first, "first_image",
        [
            shaped((RHS, CL * B), F32),
            shaped((CL, RHS, B), BF16),
            shaped((1, SLOTS), jnp.int32),
        ]
        + message_shapes(RHS, BF16),
        [VMEM] * 2 + [SMEM] + [VMEM] * 4,
        [VMEM] * 6,
        [pltpu.VMEM((1, SLOTS), jnp.int32), pltpu.SemaphoreType.DMA],
    )(*args)


def k4(*args):
    return call(
        back_second, "second_transposed_products",
        message_shapes(RHS, BF16),
        [VMEM] * 4,
        [SMEM] + [VMEM] * 4,
        [pltpu.VMEM((CL + 1, RHS, B), BF16), pltpu.VMEM((PEERS + 1, RHS, B), F32)],
    )(*args)


def k5(*args):
    return call(
        forward_second, "second_forward_products",
        shaped((CL, RHS, B), F32), VMEM,
        [SMEM] + [VMEM] * 10,
        forward_scratch(),
    )(*args)


def k6(*args):
    return call(
        image_second, "second_image",
        shaped((RHS, CL * B), F32), VMEM,
        [VMEM, SMEM] + [VMEM] * 5,
        [pltpu.VMEM((CL, RHS, B), F32)],
    )(*args)


def carriers(size, k):
    pairs = []
    for chip in range(size // 2):
        for core in range(2):
            step = k if core == 0 else -k
            pairs.append((2 * chip + core, (2 * (chip + step) + core) % size))
    return pairs


def per_device(
    vectors, diag_blocks, near_blocks, near_rows, near_cols, far_left, far_right, far_rows, far_cols, counts
):
    size = lax.axis_size("rows")
    me = lax.axis_index("rows").reshape(1)

    def swap(block):
        return lax.ppermute(block, "rows", [(i, i ^ 1) for i in range(size)])

    def carry(block, k):
        return lax.ppermute(block, "rows", carriers(size, k))

    def exchange(m1, m2, m3, give):
        got = swap(give)
        messages = []
        for k, message in enumerate((m1, m2, m3)):
            messages.append(lax.dynamic_update_slice(message, got[2 * k : 2 * k + 2], (1, 0, 0)))
        return [carry(message, k + 1) for k, message in enumerate(messages)] + [got, messages]

    def passed_on(r1, r2, r3):
        return swap(jnp.concatenate([r1[2:4], r2[2:4], r3[2:3]]))

    def in_hbm(x):
        return pltpu.with_memory_space_constraint(x, pltpu.HBM)

    lists = [in_hbm(x.reshape(1, SLOTS)) for x in (near_rows, near_cols, far_rows, far_cols)]
    sib = swap(vectors)
    both = jnp.stack([vectors, sib])
    halo = [carry(both, k) for k in (1, 2, 3)]
    m1, m2, m3, give, plan, *held = k1(
        me, *lists, in_hbm(counts), both, in_hbm(near_blocks), in_hbm(far_left), in_hbm(far_right)
    )
    halo, m1 = lax.optimization_barrier((halo, m1))
    r1, r2, r3, got, messages = exchange(m1, m2, m3, give)
    halo_post = swap(jnp.concatenate([halo[0], halo[1], halo[2][1:]]))
    halo_post, messages = lax.optimization_barrier((halo_post, messages))
    partial = k2(plan, both, *halo, halo_post, diag_blocks, *held)
    partial, r1, r2, r3 = lax.optimization_barrier((partial, r1, r2, r3))
    post = passed_on(r1, r2, r3)
    first_image, rounded, wanted, m1, m2, m3, give = k3(partial, r1, r2, r3, post, got)
    f1, f2, f3, f_got, messages = exchange(m1, m2, m3, give)
    rounded, messages = lax.optimization_barrier((rounded, messages))
    m1, m2, m3, give = k4(plan, rounded, *held)
    f1, f2, f3, m1 = lax.optimization_barrier((f1, f2, f3, m1))
    r1, r2, r3, got, messages = exchange(m1, m2, m3, give)
    f_post = passed_on(f1, f2, f3)
    f_post, messages = lax.optimization_barrier((f_post, messages))
    partial = k5(plan, rounded, f1, f2, f3, f_post, f_got, diag_blocks, *held)
    partial, r1, r2, r3 = lax.optimization_barrier((partial, r1, r2, r3))
    post = passed_on(r1, r2, r3)
    return first_image, k6(partial, wanted, r1, r2, r3, post, got)


def solution(mesh):
    return jax.shard_map(
        per_device,
        mesh=mesh,
        in_specs=(
            P(None, "rows"),
            P("rows", None, None),
            P("rows", None, None),
            P("rows"),
            P("rows"),
            P("rows", None, None),
            P("rows", None, None),
            P("rows"),
            P("rows"),
            P("rows", None),
        ),
        out_specs=(P(None, "rows"), P(None, "rows")),
        check_vma=False,
    )
```

```python
import functools

import jax
import jax.numpy as jnp
from jax import lax
from jax.experimental import pallas as pl
from jax.experimental.pallas import tpu as pltpu
from jax.sharding import PartitionSpec as P

RHS, B, K = 64, 256, 32
CL, SLOTS, CHUNK = 4, 128, 16
CHUNKS = SLOTS // CHUNK
GROUP = B // K
HALF = B // 2
PEERS = 12
DEAD = 12
EXTRA = 16
LEVELS = 32766.0
TINY = 2.0**-100
LN2 = 0.6931471805599453
QUAD = 4
VMEM_BYTES = 16 * 2**20
F32, BF16 = jnp.float32, jnp.bfloat16


def dot(x, y):
    return lax.dot_general(x, y, (((1,), (0,)), ((), ())), preferred_element_type=F32)


def dot_t(x, y):
    return lax.dot_general(x, y, (((1,), (1,)), ((), ())), preferred_element_type=F32)


def peer_number(delta, core):
    kappa, other = delta // 2 - 3, delta % 2
    step = kappa * (1 - 2 * core)
    same = int(other != core)
    if step == 0:
        return 11 if same else DEAD
    if step < 0:
        return 2 * (-step - 1) + same
    return 6 + 2 * (step - 1) + same if step < 3 or not same else DEAD


PLAN = (4, 2 * SLOTS)
COUNTS, WANTED = 64, 80
STEP = 32
GROUPS = 4


class Blocks:
    def __init__(self, plan, near, left, right, sources=None):
        self.plan, self.near, self.left, self.right = plan, near, left, right
        self.sources = sources

    def copy(self, which, chunk):
        source, sem = self.sources[which]
        place = pl.ds(chunk * CHUNK, CHUNK)
        target = (self.near, self.left, self.right)[which]
        return pltpu.make_async_copy(source.at[place], target.at[place], sem.at[chunk])

    def start(self):
        for which in (1, 2, 0):
            self.copy(which, 0).start()

    def start_rest(self, near_chunks, far_chunks):
        def far_start(chunk, carry):
            self.copy(1, chunk).start()
            self.copy(2, chunk).start()
            return carry

        def near_start(chunk, carry):
            self.copy(0, chunk).start()
            return carry

        lax.fori_loop(1, far_chunks, far_start, 0)
        lax.fori_loop(1, near_chunks, near_start, 0)

    def far_loop(self, body):
        def arrived(chunk, carry):
            self.copy(1, chunk).wait()
            self.copy(2, chunk).wait()
            return carry

        if self.sources is not None:
            lax.fori_loop(0, self.plan[2, COUNTS + 1], arrived, 0)

        def step(index, carry):
            groups = []
            for part in range(GROUPS):
                first = index * GROUPS + part
                entries = [self.plan[1, first * GROUP + k] for k in range(GROUP)]
                slots = [entry & 255 for entry in entries]
                left = jnp.concatenate([self.left[slot] for slot in slots], axis=0)
                right = jnp.concatenate([self.right[slot] for slot in slots], axis=0)
                lane = lax.broadcasted_iota(jnp.int32, (1, B), 1) // K
                rows = jnp.zeros((1, B), jnp.int32)
                for k in range(GROUP):
                    rows = jnp.where(lane == k, entries[k] >> 8, rows)
                rows = jnp.broadcast_to(rows, (RHS, B))
                groups.append((left, right, rows, [self.plan[2, 2 * first + half] for half in (0, 1)]))
            body(groups)
            return carry

        lax.fori_loop(0, self.plan[2, COUNTS + 2], step, 0)

    def near_loop(self, body):
        size = STEP if self.sources is None else CHUNK

        def step(index, carry):
            if self.sources is not None:
                self.copy(0, index).wait()
            for part in range(size):
                slot = index * size + part
                code = self.plan[0, slot]
                body(part, code & 7, code >> 3, self.near[slot])
            return carry

        lax.fori_loop(0, self.plan[2, COUNTS] * (STEP // size), step, 0)


def halves(x, axis):
    return (x[:HALF], x[HALF:]) if axis == 0 else (x[:, :HALF], x[:, HALF:])


def back_products(blocks, own, acc):
    def far(groups):
        coefs = []
        for left, right, rows, partners in groups:
            every = dot_t(own[0:CL].reshape(CL * RHS, B), left)
            coef = jnp.zeros((RHS, B), F32)
            for cluster in range(CL):
                coef = jnp.where(rows == cluster, every[cluster * RHS : (cluster + 1) * RHS], coef)
            coefs.append(coef.astype(BF16))
        terms = []
        for coef, (left, right, rows, partners) in zip(coefs, groups):
            for part, block, partner in zip(halves(coef, 1), halves(right, 0), partners):
                terms.append((partner, dot(part, block)))
        for partner, term in terms:
            acc[partner] += term

    def near(part, row, partner, block):
        acc[partner] += dot(own[row], block)

    blocks.far_loop(far)
    blocks.near_loop(near)


def forward_products(blocks, fetched, turned, acc, acc_turned):
    turned[DEAD] = jnp.zeros((B, RHS), BF16)
    for partner in range(PEERS):
        turned[partner] = fetched[partner].T
    acc_turned[...] = jnp.zeros_like(acc_turned)

    def far(groups):
        spreads = []
        for left, right, rows, partners in groups:
            coef = [dot_t(fetched[partner], block) for partner, block in zip(partners, halves(right, 0))]
            coef = jnp.concatenate(coef, axis=1).astype(BF16).astype(F32)
            spread = [jnp.where(rows == cluster, coef, 0.0).astype(BF16) for cluster in range(CL)]
            spreads.append(jnp.concatenate(spread, axis=0))
        terms = [dot(spread, group[0]) for spread, group in zip(spreads, groups)]
        total = terms[0]
        for term in terms[1:]:
            total += term
        acc[0:CL] += total.reshape(CL, RHS, B)

    def near(part, row, partner, block):
        if part % 2 == 0:
            acc[row] += dot_t(fetched[partner], block)
        else:
            acc_turned[row] += dot(block, turned[partner])

    blocks.far_loop(far)
    blocks.near_loop(near)
    for cluster in range(CL):
        acc[cluster] += acc_turned[cluster].T


def make_plan(me, lists, few, draft):
    core = me % 2
    base = me - core - 6
    lane = lax.broadcasted_iota(jnp.int32, (1, SLOTS), 1)
    row16 = lax.broadcasted_iota(jnp.int32, (16, SLOTS), 0)
    kinds = []
    for kind in (0, 1):
        rows, cols = lists[2 * kind : 2 * kind + 1, :], lists[2 * kind + 1 : 2 * kind + 2, :]
        live = lane < few[0, kind]
        delta = ((cols >> 2) - base) & 15
        partner = jnp.full((1, SLOTS), DEAD, jnp.int32)
        for value in range(14):
            pair = [peer_number(value, a) for a in (0, 1)]
            partner = jnp.where(delta == value, jnp.where(core == 0, pair[0], pair[1]), partner)
        partner = jnp.where(live, partner, DEAD)
        kinds.append((jnp.where(live, rows & (CL - 1), CL), partner, cols & (CL - 1)))
    (near_row, near_rho, near_part), (far_row, far_rho, far_part) = kinds
    wide = lambda x: jnp.broadcast_to(x, (16, SLOTS))
    hot = row16 == wide(far_rho)
    wanted = jnp.maximum(
        jnp.where(row16 == wide(near_rho), wide(near_part).astype(F32), 0.0),
        jnp.where(hot, wide(far_part).astype(F32), 0.0),
    )
    wanted = jnp.max(wanted, axis=1, keepdims=True)
    hot = jnp.where(hot, 1.0, 0.0)
    square = (SLOTS, SLOTS)
    earlier = lax.broadcasted_iota(jnp.int32, square, 0) < lax.broadcasted_iota(jnp.int32, square, 1)
    rank = dot(hot.astype(BF16), jnp.where(earlier, 1.0, 0.0).astype(BF16)).astype(jnp.int32)
    number = wide(jnp.sum(hot, axis=1, keepdims=True)).astype(jnp.int32)
    padded = ((number + (QUAD - 1)) >> 2) << 2
    place = jnp.full((1, SLOTS), -1, jnp.int32)
    quad_rho = jnp.full((1, SLOTS), DEAD, jnp.int32)
    first = jnp.zeros((1, SLOTS), jnp.int32)
    for rho in range(PEERS):
        place = jnp.where(far_rho == rho, rank[rho : rho + 1] + first, place)
        last = first + padded[rho : rho + 1]
        quad_rho = jnp.where((lane * QUAD >= first) & (lane * QUAD < last), rho, quad_rho)
        first = last
    column = jnp.transpose(jnp.broadcast_to(place.astype(F32), square))
    spots = lax.broadcasted_iota(jnp.int32, square, 1).astype(F32)
    hits = jnp.concatenate([jnp.where(column == spots + shift, 1.0, 0.0).astype(BF16) for shift in (0.0, float(SLOTS))], axis=1)
    codes = jnp.where(row16 == 0, wide(lane), jnp.where(row16 == 1, wide(far_row), 1)).astype(F32).astype(BF16)
    found = dot(codes, hits)
    entry = jnp.where(found[2:3] > 0.5, found[0:1] + 256.0 * found[1:2], 256.0 * CL).astype(jnp.int32)
    wanted = jnp.sum(jnp.where(row16 + WANTED == wide(lane), wide(wanted), 0.0), axis=0, keepdims=True).astype(jnp.int32)
    draft[0:1, 0:SLOTS] = near_row + 8 * near_rho
    draft[1:2, :] = entry
    numbers = jnp.where(lane == COUNTS, (few[0, 0] + (STEP - 1)) // STEP, jnp.where(lane < COUNTS, quad_rho, wanted))
    numbers = jnp.where(lane == COUNTS + 1, (few[0, 1] + (CHUNK - 1)) // CHUNK, numbers)
    steps = (first + (2 * GROUPS * QUAD - 1)) >> (GROUPS.bit_length() + 2)
    draft[2:3, 0:SLOTS] = jnp.where(lane == COUNTS + 2, steps, numbers)


def place_out(rho):
    if rho == 11:
        return 3, 6
    if rho < 6:
        return 3, rho ^ 1
    k, same = divmod(rho - 6, 2)
    return k, 3 * same


def place_in(rho):
    if rho == 11:
        return 4, 6
    if rho < 6:
        return rho // 2, rho % 2
    return 3, rho - 6


MESSAGE = (4, 4, 3)


def back_first(
    me, near_rows, near_cols, far_rows, far_cols, counts, both, near, left, right,
    m1, m2, m3, give, plan, near_held, left_held, right_held,
    own, acc, lists, few, draft, near_sem, left_sem, right_sem, list_sem,
):
    blocks = Blocks(plan, near_held, left_held, right_held, ((near, near_sem), (left, left_sem), (right, right_sem)))
    copies = [pltpu.make_async_copy(counts, few, list_sem.at[4])]
    for index, source in enumerate((near_rows, near_cols, far_rows, far_cols)):
        copies.append(pltpu.make_async_copy(source, lists.at[pl.ds(index, 1)], list_sem.at[index]))
    for copy in copies:
        copy.start()
    blocks.start()
    for cluster in range(CL):
        own[cluster] = both[0, :, cluster * B : (cluster + 1) * B]
    own[CL] = jnp.zeros((RHS, B), BF16)
    draft[...] = jnp.zeros_like(draft)
    copies[0].wait()
    near_steps = (few[0, 0] + (STEP - 1)) // STEP
    blocks.start_rest(near_steps * (STEP // CHUNK), (few[0, 1] + (CHUNK - 1)) // CHUNK)
    for copy in copies[1:]:
        copy.wait()
    make_plan(me[0], lists, few, draft)
    copy = pltpu.make_async_copy(draft, plan, list_sem.at[5])
    copy.start()
    acc[...] = jnp.zeros_like(acc)
    copy.wait()
    back_products(blocks, own, acc)
    outs = (m1, m2, m3, give)
    for rho in range(PEERS):
        message, index = place_out(rho)
        outs[message][index, 0:RHS], power = coded(acc[rho])
        half = lax.broadcasted_iota(jnp.int32, (EXTRA, B), 0) < EXTRA // 2
        outs[message][index, RHS:] = jnp.where(half, power, plan[2, WANTED + rho]).astype(jnp.int16)


def forward_first(
    plan, both, h1, h2, h3, post, diag, near, left, right,
    out,
    fetched, turned, acc, acc_turned,
):
    halo = (h1, h2, h3)
    for rho in range(PEERS):
        lanes = pl.ds(pl.multiple_of(plan[2, WANTED + rho] * B, B), B)
        if rho == 11:
            fetched[rho] = both[1, :, lanes]
        elif rho < 6:
            fetched[rho] = halo[rho // 2][rho % 2, :, lanes]
        else:
            k, same = divmod(rho - 6, 2)
            fetched[rho] = post[2 * k + (1 - same if k < 2 else 0), :, lanes]
    fetched[DEAD] = jnp.zeros((RHS, B), BF16)
    acc[CL] = jnp.zeros((RHS, B), F32)
    for cluster in range(CL):
        acc[cluster] = dot_t(both[0, :, cluster * B : (cluster + 1) * B], diag[cluster])
    forward_products(Blocks(plan, near, left, right), fetched, turned, acc, acc_turned)
    out[...] = acc[0:CL]


STRIP = 16


def coded(block):
    top = jnp.maximum(jnp.max(jnp.abs(block), axis=0, keepdims=True), TINY)
    power = jnp.ceil(jnp.log(top * (1.0 / LEVELS)) * (1.0 / LN2) + 1e-3)
    scaled = block * jnp.exp(power * -LN2)
    return jnp.floor(scaled + 0.5).astype(jnp.int32).astype(jnp.int16), power.astype(jnp.int32)


def image_first(
    partial, r1, r2, r3, post, got,
    image, rounded, wanted, m1, m2, m3, give,
    draft, sem,
):
    ins = (r1, r2, r3, post, got)
    places = [place_in(rho) for rho in range(PEERS)]
    extras = [ins[message][index, RHS:].astype(jnp.int32) for message, index in places]
    units = [jnp.exp(extra[0:1].astype(F32) * LN2) for extra in extras]
    marks = [extra[EXTRA // 2 : EXTRA // 2 + 1] for extra in extras]
    lane = lax.broadcasted_iota(jnp.int32, (1, SLOTS), 1)
    packed = jnp.zeros((1, SLOTS), jnp.int32)
    for rho, mark in enumerate(marks):
        packed = jnp.where(lane == rho, mark[:, 0:SLOTS], packed)
    draft[...] = packed
    copy = pltpu.make_async_copy(draft, wanted, sem)
    copy.start()
    for first in range(0, RHS, STRIP):
        rows = slice(first, first + STRIP)
        totals = [partial[cluster, rows] for cluster in range(CL)]
        for (message, index), mark, unit in zip(places, marks, units):
            block = ins[message][index, rows].astype(jnp.int32).astype(F32) * unit
            mark = jnp.broadcast_to(mark, (STRIP, B))
            for cluster in range(CL):
                totals[cluster] += jnp.where(mark == cluster, block, 0.0)
        for cluster in range(CL):
            image[rows, cluster * B : (cluster + 1) * B] = totals[cluster]
            rounded[cluster, rows] = totals[cluster].astype(BF16)
    copy.wait()
    outs = (m1, m2, m3, give)
    for rho in range(PEERS):
        message, index = place_out(rho)
        outs[message][index] = rounded[wanted[0, rho]]


def back_second(
    plan, rounded, near, left, right,
    m1, m2, m3, give,
    own, acc,
):
    own[0:CL] = rounded[...]
    own[CL] = jnp.zeros((RHS, B), BF16)
    acc[...] = jnp.zeros_like(acc)
    back_products(Blocks(plan, near, left, right), own, acc)
    outs = (m1, m2, m3, give)
    for rho in range(PEERS):
        message, index = place_out(rho)
        outs[message][index] = acc[rho].astype(BF16)


def forward_second(
    plan, own, r1, r2, r3, post, got, diag, near, left, right,
    out,
    fetched, turned, acc, acc_turned,
):
    ins = (r1, r2, r3, post, got)
    for rho in range(PEERS):
        message, index = place_in(rho)
        fetched[rho] = ins[message][index]
    fetched[DEAD] = jnp.zeros((RHS, B), BF16)
    acc[CL] = jnp.zeros((RHS, B), F32)
    for cluster in range(CL):
        acc[cluster] = dot_t(own[cluster], diag[cluster])
    forward_products(Blocks(plan, near, left, right), fetched, turned, acc, acc_turned)
    out[...] = acc[0:CL]


def image_second(partial, wanted, r1, r2, r3, post, got, image, acc):
    ins = (r1, r2, r3, post, got)
    acc[...] = partial[...]
    for rho in range(PEERS):
        message, index = place_in(rho)
        acc[wanted[0, rho]] += ins[message][index].astype(F32)
    for cluster in range(CL):
        image[:, cluster * B : (cluster + 1) * B] = acc[cluster]


SMEM = pl.BlockSpec(memory_space=pltpu.SMEM)
VMEM = pl.BlockSpec(memory_space=pltpu.VMEM)
ANY = pl.BlockSpec(memory_space=pl.ANY)
HBM = pl.BlockSpec(memory_space=pltpu.HBM)


def call(kernel, name, outs, out_specs, in_specs, scratch):
    return pl.pallas_call(
        kernel,
        name=name,
        out_shape=outs,
        in_specs=in_specs,
        out_specs=out_specs,
        scratch_shapes=scratch,
        compiler_params=pltpu.CompilerParams(vmem_limit_bytes=VMEM_BYTES),
        cost_estimate=pl.CostEstimate(flops=2 * 10**9, bytes_accessed=22 * 10**6, transcendentals=0),
    )


def shaped(shape, dtype):
    return jax.ShapeDtypeStruct(shape, dtype)


def message_shapes(rows, dtype):
    return [shaped((n, rows, B), dtype) for n in MESSAGE + (7,)]


def k1(*args):
    held = [pltpu.VMEM(shape, BF16) for shape in ((SLOTS, B, B), (SLOTS, K, B), (SLOTS, K, B))]
    return call(
        back_first, "transposed_products",
        message_shapes(RHS + EXTRA, jnp.int16) + [shaped(PLAN, jnp.int32)] + held,
        [VMEM] * 4 + [SMEM] + [VMEM] * 3,
        [SMEM] + [HBM] * 5 + [VMEM] + [HBM] * 3,
        [
            pltpu.VMEM((CL + 1, RHS, B), BF16),
            pltpu.VMEM((PEERS + 1, RHS, B), F32),
            pltpu.VMEM((8, SLOTS), jnp.int32),
            pltpu.SMEM((1, 2), jnp.int32),
            pltpu.VMEM(PLAN, jnp.int32),
        ]
        + [pltpu.SemaphoreType.DMA((n,)) for n in (CHUNKS, CHUNKS, CHUNKS, 6)],
    )(*args)


def forward_scratch():
    return [
        pltpu.VMEM((PEERS + 1, RHS, B), BF16),
        pltpu.VMEM((PEERS + 1, B, RHS), BF16),
        pltpu.VMEM((CL + 1, RHS, B), F32),
        pltpu.VMEM((CL + 1, B, RHS), F32),
    ]


def k2(*args):
    return call(
        forward_first, "forward_products",
        shaped((CL, RHS, B), F32), VMEM,
        [SMEM] + [VMEM] * 9,
        forward_scratch(),
    )(*args)


def k3(*args):
    return call(
        image_first, "first_image",
        [
            shaped((RHS, CL * B), F32),
            shaped((CL, RHS, B), BF16),
            shaped((1, SLOTS), jnp.int32),
        ]
        + message_shapes(RHS, BF16),
        [VMEM] * 2 + [SMEM] + [VMEM] * 4,
        [VMEM] * 6,
        [pltpu.VMEM((1, SLOTS), jnp.int32), pltpu.SemaphoreType.DMA],
    )(*args)


def k4(*args):
    return call(
        back_second, "second_transposed_products",
        message_shapes(RHS, BF16),
        [VMEM] * 4,
        [SMEM] + [VMEM] * 4,
        [pltpu.VMEM((CL + 1, RHS, B), BF16), pltpu.VMEM((PEERS + 1, RHS, B), F32)],
    )(*args)


def k5(*args):
    return call(
        forward_second, "second_forward_products",
        shaped((CL, RHS, B), F32), VMEM,
        [SMEM] + [VMEM] * 10,
        forward_scratch(),
    )(*args)


def k6(*args):
    return call(
        image_second, "second_image",
        shaped((RHS, CL * B), F32), VMEM,
        [VMEM, SMEM] + [VMEM] * 5,
        [pltpu.VMEM((CL, RHS, B), F32)],
    )(*args)


def carriers(size, k):
    pairs = []
    for chip in range(size // 2):
        for core in range(2):
            step = k if core == 0 else -k
            pairs.append((2 * chip + core, (2 * (chip + step) + core) % size))
    return pairs


def per_device(
    vectors, diag_blocks, near_blocks, near_rows, near_cols, far_left, far_right, far_rows, far_cols, counts
):
    size = lax.axis_size("rows")
    me = lax.axis_index("rows").reshape(1)

    def swap(block):
        return lax.ppermute(block, "rows", [(i, i ^ 1) for i in range(size)])

    def carry(block, k):
        return lax.ppermute(block, "rows", carriers(size, k))

    def exchange(m1, m2, m3, give):
        got = swap(give)
        messages = []
        for k, message in enumerate((m1, m2, m3)):
            messages.append(lax.dynamic_update_slice(message, got[2 * k : 2 * k + 2], (1, 0, 0)))
        return [carry(message, k + 1) for k, message in enumerate(messages)] + [got, messages]

    def passed_on(r1, r2, r3):
        return swap(jnp.concatenate([r1[2:4], r2[2:4], r3[2:3]]))

    def in_hbm(x):
        return pltpu.with_memory_space_constraint(x, pltpu.HBM)

    lists = [in_hbm(x.reshape(1, SLOTS)) for x in (near_rows, near_cols, far_rows, far_cols)]
    sib = swap(vectors)
    both = jnp.stack([vectors, sib])
    halo = [carry(both, k) for k in (1, 2, 3)]
    m1, m2, m3, give, plan, *held = k1(
        me, *lists, in_hbm(counts), both, in_hbm(near_blocks), in_hbm(far_left), in_hbm(far_right)
    )
    halo, m1 = lax.optimization_barrier((halo, m1))
    r1, r2, r3, got, messages = exchange(m1, m2, m3, give)
    halo_post = swap(jnp.concatenate([halo[0], halo[1], halo[2][1:]]))
    halo_post, messages = lax.optimization_barrier((halo_post, messages))
    partial = k2(plan, both, *halo, halo_post, diag_blocks, *held)
    partial, r1, r2, r3 = lax.optimization_barrier((partial, r1, r2, r3))
    post = passed_on(r1, r2, r3)
    first_image, rounded, wanted, m1, m2, m3, give = k3(partial, r1, r2, r3, post, got)
    f1, f2, f3, f_got, messages = exchange(m1, m2, m3, give)
    rounded, messages = lax.optimization_barrier((rounded, messages))
    m1, m2, m3, give = k4(plan, rounded, *held)
    f1, f2, f3, give = lax.optimization_barrier((f1, f2, f3, give))
    r1, r2, r3, got, messages = exchange(m1, m2, m3, give)
    f_post = passed_on(f1, f2, f3)
    f_post, messages = lax.optimization_barrier((f_post, messages))
    partial = k5(plan, rounded, f1, f2, f3, f_post, f_got, diag_blocks, *held)
    partial, r1, r2, r3 = lax.optimization_barrier((partial, r1, r2, r3))
    post = passed_on(r1, r2, r3)
    return first_image, k6(partial, wanted, r1, r2, r3, post, got)


def solution(mesh):
    return jax.shard_map(
        per_device,
        mesh=mesh,
        in_specs=(
            P(None, "rows"),
            P("rows", None, None),
            P("rows", None, None),
            P("rows"),
            P("rows"),
            P("rows", None, None),
            P("rows", None, None),
            P("rows"),
            P("rows"),
            P("rows", None),
        ),
        out_specs=(P(None, "rows"), P(None, "rows")),
        check_vma=False,
    )
```

```python
import functools

import jax
import jax.numpy as jnp
from jax import lax
from jax.experimental import pallas as pl
from jax.experimental.pallas import tpu as pltpu
from jax.sharding import PartitionSpec as P

RHS, B, K = 64, 256, 32
CL, SLOTS, CHUNK = 4, 128, 16
CHUNKS = SLOTS // CHUNK
GROUP = B // K
HALF = B // 2
PEERS = 12
DEAD = 12
EXTRA = 16
LEVELS = 32766.0
TINY = 2.0**-100
LN2 = 0.6931471805599453
QUAD = 4
VMEM_BYTES = 16 * 2**20
F32, BF16 = jnp.float32, jnp.bfloat16


def dot(x, y):
    return lax.dot_general(x, y, (((1,), (0,)), ((), ())), preferred_element_type=F32)


def dot_t(x, y):
    return lax.dot_general(x, y, (((1,), (1,)), ((), ())), preferred_element_type=F32)


def peer_number(delta, core):
    kappa, other = delta // 2 - 3, delta % 2
    step = kappa * (1 - 2 * core)
    same = int(other != core)
    if step == 0:
        return 11 if same else DEAD
    if step < 0:
        return 2 * (-step - 1) + same
    return 6 + 2 * (step - 1) + same if step < 3 or not same else DEAD


PLAN = (4, 2 * SLOTS)
COUNTS, WANTED = 64, 80
STEP = 32
GROUPS = 4


class Blocks:
    def __init__(self, plan, near, left, right, sources=None):
        self.plan, self.near, self.left, self.right = plan, near, left, right
        self.sources = sources

    def copy(self, which, chunk):
        source, sem = self.sources[which]
        place = pl.ds(chunk * CHUNK, CHUNK)
        target = (self.near, self.left, self.right)[which]
        return pltpu.make_async_copy(source.at[place], target.at[place], sem.at[chunk])

    def start(self):
        for which in (1, 2, 0):
            self.copy(which, 0).start()

    def start_rest(self, near_chunks, far_chunks):
        def far_start(chunk, carry):
            self.copy(1, chunk).start()
            self.copy(2, chunk).start()
            return carry

        def near_start(chunk, carry):
            self.copy(0, chunk).start()
            return carry

        lax.fori_loop(1, far_chunks, far_start, 0)
        lax.fori_loop(1, near_chunks, near_start, 0)

    def far_loop(self, body):
        def arrived(chunk, carry):
            self.copy(1, chunk).wait()
            self.copy(2, chunk).wait()
            return carry

        if self.sources is not None:
            lax.fori_loop(0, self.plan[2, COUNTS + 1], arrived, 0)

        def step(index, carry):
            groups = []
            for part in range(GROUPS):
                first = index * GROUPS + part
                entries = [self.plan[1, first * GROUP + k] for k in range(GROUP)]
                slots = [entry & 255 for entry in entries]
                left = jnp.concatenate([self.left[slot] for slot in slots], axis=0)
                right = jnp.concatenate([self.right[slot] for slot in slots], axis=0)
                lane = lax.broadcasted_iota(jnp.int32, (1, B), 1) // K
                rows = jnp.zeros((1, B), jnp.int32)
                for k in range(GROUP):
                    rows = jnp.where(lane == k, entries[k] >> 8, rows)
                rows = jnp.broadcast_to(rows, (RHS, B))
                groups.append((left, right, rows, [self.plan[2, 2 * first + half] for half in (0, 1)]))
            body(groups)
            return carry

        lax.fori_loop(0, self.plan[2, COUNTS + 2], step, 0)

    def near_loop(self, body):
        size = STEP if self.sources is None else CHUNK

        def step(index, carry):
            if self.sources is not None:
                self.copy(0, index).wait()
            for part in range(size):
                slot = index * size + part
                code = self.plan[0, slot]
                body(part, code & 7, code >> 3, self.near[slot])
            return carry

        lax.fori_loop(0, self.plan[2, COUNTS] * (STEP // size), step, 0)


def halves(x, axis):
    return (x[:HALF], x[HALF:]) if axis == 0 else (x[:, :HALF], x[:, HALF:])


def back_products(blocks, own, acc):
    def far(groups):
        coefs = []
        for left, right, rows, partners in groups:
            every = dot_t(own[0:CL].reshape(CL * RHS, B), left)
            coef = jnp.zeros((RHS, B), F32)
            for cluster in range(CL):
                coef = jnp.where(rows == cluster, every[cluster * RHS : (cluster + 1) * RHS], coef)
            coefs.append(coef.astype(BF16))
        terms = []
        for coef, (left, right, rows, partners) in zip(coefs, groups):
            for part, block, partner in zip(halves(coef, 1), halves(right, 0), partners):
                terms.append((partner, dot(part, block)))
        for partner, term in terms:
            acc[partner] += term

    def near(part, row, partner, block):
        acc[partner] += dot(own[row], block)

    blocks.far_loop(far)
    blocks.near_loop(near)


def forward_products(blocks, fetched, turned, acc, acc_turned):
    turned[DEAD] = jnp.zeros((B, RHS), BF16)
    for partner in range(PEERS):
        turned[partner] = fetched[partner].T
    acc_turned[...] = jnp.zeros_like(acc_turned)

    def far(groups):
        spreads = []
        for left, right, rows, partners in groups:
            coef = [dot_t(fetched[partner], block) for partner, block in zip(partners, halves(right, 0))]
            coef = jnp.concatenate(coef, axis=1).astype(BF16).astype(F32)
            spread = [jnp.where(rows == cluster, coef, 0.0).astype(BF16) for cluster in range(CL)]
            spreads.append(jnp.concatenate(spread, axis=0))
        terms = [dot(spread, group[0]) for spread, group in zip(spreads, groups)]
        total = terms[0]
        for term in terms[1:]:
            total += term
        acc[0:CL] += total.reshape(CL, RHS, B)

    def near(part, row, partner, block):
        if part % 2 == 0:
            acc[row] += dot_t(fetched[partner], block)
        else:
            acc_turned[row] += dot(block, turned[partner])

    blocks.far_loop(far)
    blocks.near_loop(near)
    for cluster in range(CL):
        acc[cluster] += acc_turned[cluster].T


def make_plan(me, lists, few, draft):
    core = me % 2
    base = me - core - 6
    lane = lax.broadcasted_iota(jnp.int32, (1, SLOTS), 1)
    row16 = lax.broadcasted_iota(jnp.int32, (16, SLOTS), 0)
    kinds = []
    for kind in (0, 1):
        rows, cols = lists[2 * kind : 2 * kind + 1, :], lists[2 * kind + 1 : 2 * kind + 2, :]
        live = lane < few[0, kind]
        delta = ((cols >> 2) - base) & 15
        partner = jnp.full((1, SLOTS), DEAD, jnp.int32)
        for value in range(14):
            pair = [peer_number(value, a) for a in (0, 1)]
            partner = jnp.where(delta == value, jnp.where(core == 0, pair[0], pair[1]), partner)
        partner = jnp.where(live, partner, DEAD)
        kinds.append((jnp.where(live, rows & (CL - 1), CL), partner, cols & (CL - 1)))
    (near_row, near_rho, near_part), (far_row, far_rho, far_part) = kinds
    wide = lambda x: jnp.broadcast_to(x, (16, SLOTS))
    hot = row16 == wide(far_rho)
    wanted = jnp.maximum(
        jnp.where(row16 == wide(near_rho), wide(near_part).astype(F32), 0.0),
        jnp.where(hot, wide(far_part).astype(F32), 0.0),
    )
    wanted = jnp.max(wanted, axis=1, keepdims=True)
    hot = jnp.where(hot, 1.0, 0.0)
    square = (SLOTS, SLOTS)
    earlier = lax.broadcasted_iota(jnp.int32, square, 0) < lax.broadcasted_iota(jnp.int32, square, 1)
    rank = dot(hot.astype(BF16), jnp.where(earlier, 1.0, 0.0).astype(BF16)).astype(jnp.int32)
    number = wide(jnp.sum(hot, axis=1, keepdims=True)).astype(jnp.int32)
    padded = ((number + (QUAD - 1)) >> 2) << 2
    place = jnp.full((1, SLOTS), -1, jnp.int32)
    quad_rho = jnp.full((1, SLOTS), DEAD, jnp.int32)
    first = jnp.zeros((1, SLOTS), jnp.int32)
    for rho in range(PEERS):
        place = jnp.where(far_rho == rho, rank[rho : rho + 1] + first, place)
        last = first + padded[rho : rho + 1]
        quad_rho = jnp.where((lane * QUAD >= first) & (lane * QUAD < last), rho, quad_rho)
        first = last
    column = jnp.transpose(jnp.broadcast_to(place.astype(F32), square))
    spots = lax.broadcasted_iota(jnp.int32, square, 1).astype(F32)
    hits = jnp.concatenate([jnp.where(column == spots + shift, 1.0, 0.0).astype(BF16) for shift in (0.0, float(SLOTS))], axis=1)
    codes = jnp.where(row16 == 0, wide(lane), jnp.where(row16 == 1, wide(far_row), 1)).astype(F32).astype(BF16)
    found = dot(codes, hits)
    entry = jnp.where(found[2:3] > 0.5, found[0:1] + 256.0 * found[1:2], 256.0 * CL).astype(jnp.int32)
    wanted = jnp.sum(jnp.where(row16 + WANTED == wide(lane), wide(wanted), 0.0), axis=0, keepdims=True).astype(jnp.int32)
    draft[0:1, 0:SLOTS] = near_row + 8 * near_rho
    draft[1:2, :] = entry
    numbers = jnp.where(lane == COUNTS, (few[0, 0] + (STEP - 1)) // STEP, jnp.where(lane < COUNTS, quad_rho, wanted))
    numbers = jnp.where(lane == COUNTS + 1, (few[0, 1] + (CHUNK - 1)) // CHUNK, numbers)
    steps = (first + (2 * GROUPS * QUAD - 1)) >> (GROUPS.bit_length() + 2)
    draft[2:3, 0:SLOTS] = jnp.where(lane == COUNTS + 2, steps, numbers)


def place_out(rho):
    if rho == 11:
        return 3, 6
    if rho < 6:
        return 3, rho ^ 1
    k, same = divmod(rho - 6, 2)
    return k, 3 * same


def place_in(rho):
    if rho == 11:
        return 4, 6
    if rho < 6:
        return rho // 2, rho % 2
    return 3, rho - 6


MESSAGE = (4, 4, 3)


def back_first(
    me, near_rows, near_cols, far_rows, far_cols, counts, both, near, left, right,
    m1, m2, m3, give, plan, near_held, left_held, right_held,
    own, acc, lists, few, draft, near_sem, left_sem, right_sem, list_sem,
):
    blocks = Blocks(plan, near_held, left_held, right_held, ((near, near_sem), (left, left_sem), (right, right_sem)))
    copies = [pltpu.make_async_copy(counts, few, list_sem.at[4])]
    for index, source in enumerate((near_rows, near_cols, far_rows, far_cols)):
        copies.append(pltpu.make_async_copy(source, lists.at[pl.ds(index, 1)], list_sem.at[index]))
    for copy in copies:
        copy.start()
    blocks.start()
    for cluster in range(CL):
        own[cluster] = both[0, :, cluster * B : (cluster + 1) * B]
    own[CL] = jnp.zeros((RHS, B), BF16)
    draft[...] = jnp.zeros_like(draft)
    copies[0].wait()
    near_steps = (few[0, 0] + (STEP - 1)) // STEP
    blocks.start_rest(near_steps * (STEP // CHUNK), (few[0, 1] + (CHUNK - 1)) // CHUNK)
    for copy in copies[1:]:
        copy.wait()
    make_plan(me[0], lists, few, draft)
    copy = pltpu.make_async_copy(draft, plan, list_sem.at[5])
    copy.start()
    acc[...] = jnp.zeros_like(acc)
    copy.wait()
    back_products(blocks, own, acc)
    outs = (m1, m2, m3, give)
    for rho in range(PEERS):
        message, index = place_out(rho)
        outs[message][index, 0:RHS], power = coded(acc[rho])
        half = lax.broadcasted_iota(jnp.int32, (EXTRA, B), 0) < EXTRA // 2
        outs[message][index, RHS:] = jnp.where(half, power, plan[2, WANTED + rho]).astype(jnp.int16)


def forward_first(
    plan, both, h1, h2, h3, post, diag, near, left, right,
    out,
    fetched, turned, acc, acc_turned,
):
    halo = (h1, h2, h3)
    for rho in range(PEERS):
        lanes = pl.ds(pl.multiple_of(plan[2, WANTED + rho] * B, B), B)
        if rho == 11:
            fetched[rho] = both[1, :, lanes]
        elif rho < 6:
            fetched[rho] = halo[rho // 2][rho % 2, :, lanes]
        else:
            k, same = divmod(rho - 6, 2)
            fetched[rho] = post[2 * k + (1 - same if k < 2 else 0), :, lanes]
    fetched[DEAD] = jnp.zeros((RHS, B), BF16)
    acc[CL] = jnp.zeros((RHS, B), F32)
    for cluster in range(CL):
        acc[cluster] = dot_t(both[0, :, cluster * B : (cluster + 1) * B], diag[cluster])
    forward_products(Blocks(plan, near, left, right), fetched, turned, acc, acc_turned)
    out[...] = acc[0:CL]


STRIP = 16


def coded(block):
    top = jnp.maximum(jnp.max(jnp.abs(block), axis=0, keepdims=True), TINY)
    power = jnp.ceil(jnp.log(top * (1.0 / LEVELS)) * (1.0 / LN2) + 1e-3)
    scaled = block * jnp.exp(power * -LN2)
    return jnp.floor(scaled + 0.5).astype(jnp.int32).astype(jnp.int16), power.astype(jnp.int32)


def image_first(
    partial, r1, r2, r3, post, got,
    image, rounded, wanted, m1, m2, m3, give,
    draft, sem,
):
    ins = (r1, r2, r3, post, got)
    places = [place_in(rho) for rho in range(PEERS)]
    extras = [ins[message][index, RHS:].astype(jnp.int32) for message, index in places]
    units = [jnp.exp(extra[0:1].astype(F32) * LN2) for extra in extras]
    marks = [extra[EXTRA // 2 : EXTRA // 2 + 1] for extra in extras]
    lane = lax.broadcasted_iota(jnp.int32, (1, SLOTS), 1)
    packed = jnp.zeros((1, SLOTS), jnp.int32)
    for rho, mark in enumerate(marks):
        packed = jnp.where(lane == rho, mark[:, 0:SLOTS], packed)
    draft[...] = packed
    copy = pltpu.make_async_copy(draft, wanted, sem)
    copy.start()
    for first in range(0, RHS, STRIP):
        rows = slice(first, first + STRIP)
        totals = [partial[cluster, rows] for cluster in range(CL)]
        for (message, index), mark, unit in zip(places, marks, units):
            block = ins[message][index, rows].astype(jnp.int32).astype(F32) * unit
            mark = jnp.broadcast_to(mark, (STRIP, B))
            for cluster in range(CL):
                totals[cluster] += jnp.where(mark == cluster, block, 0.0)
        for cluster in range(CL):
            image[rows, cluster * B : (cluster + 1) * B] = totals[cluster]
            rounded[cluster, rows] = totals[cluster].astype(BF16)
    copy.wait()
    outs = (m1, m2, m3, give)
    for rho in range(PEERS):
        message, index = place_out(rho)
        outs[message][index] = rounded[wanted[0, rho]]


def back_second(
    plan, rounded, near, left, right,
    m1, m2, m3, give,
    own, acc,
):
    own[0:CL] = rounded[...]
    own[CL] = jnp.zeros((RHS, B), BF16)
    acc[...] = jnp.zeros_like(acc)
    back_products(Blocks(plan, near, left, right), own, acc)
    outs = (m1, m2, m3, give)
    for rho in range(PEERS):
        message, index = place_out(rho)
        outs[message][index] = acc[rho].astype(BF16)


def forward_second(
    plan, own, r1, r2, r3, post, got, diag, near, left, right,
    out,
    fetched, turned, acc, acc_turned,
):
    ins = (r1, r2, r3, post, got)
    for rho in range(PEERS):
        message, index = place_in(rho)
        fetched[rho] = ins[message][index]
    fetched[DEAD] = jnp.zeros((RHS, B), BF16)
    acc[CL] = jnp.zeros((RHS, B), F32)
    for cluster in range(CL):
        acc[cluster] = dot_t(own[cluster], diag[cluster])
    forward_products(Blocks(plan, near, left, right), fetched, turned, acc, acc_turned)
    out[...] = acc[0:CL]


def image_second(partial, wanted, r1, r2, r3, post, got, image, acc):
    ins = (r1, r2, r3, post, got)
    acc[...] = partial[...]
    for rho in range(PEERS):
        message, index = place_in(rho)
        acc[wanted[0, rho]] += ins[message][index].astype(F32)
    for cluster in range(CL):
        image[:, cluster * B : (cluster + 1) * B] = acc[cluster]


SMEM = pl.BlockSpec(memory_space=pltpu.SMEM)
VMEM = pl.BlockSpec(memory_space=pltpu.VMEM)
ANY = pl.BlockSpec(memory_space=pl.ANY)
HBM = pl.BlockSpec(memory_space=pltpu.HBM)


def call(kernel, name, outs, out_specs, in_specs, scratch):
    return pl.pallas_call(
        kernel,
        name=name,
        out_shape=outs,
        in_specs=in_specs,
        out_specs=out_specs,
        scratch_shapes=scratch,
        compiler_params=pltpu.CompilerParams(vmem_limit_bytes=VMEM_BYTES),
        cost_estimate=pl.CostEstimate(flops=2 * 10**9, bytes_accessed=22 * 10**6, transcendentals=0),
    )


def shaped(shape, dtype):
    return jax.ShapeDtypeStruct(shape, dtype)


def message_shapes(rows, dtype):
    return [shaped((n, rows, B), dtype) for n in MESSAGE + (7,)]


def stage(source, target, sem):
    copy = pltpu.make_async_copy(source, target.at[0], sem)
    copy.start()
    copy.wait()


def staged(vectors):
    return call(stage, "staged", shaped((2, *vectors.shape), BF16), VMEM, [HBM], [pltpu.SemaphoreType.DMA])(vectors)


def k1(*args):
    held = [pltpu.VMEM(shape, BF16) for shape in ((SLOTS, B, B), (SLOTS, K, B), (SLOTS, K, B))]
    return call(
        back_first, "transposed_products",
        message_shapes(RHS + EXTRA, jnp.int16) + [shaped(PLAN, jnp.int32)] + held,
        [VMEM] * 4 + [SMEM] + [VMEM] * 3,
        [SMEM] + [HBM] * 5 + [VMEM] + [HBM] * 3,
        [
            pltpu.VMEM((CL + 1, RHS, B), BF16),
            pltpu.VMEM((PEERS + 1, RHS, B), F32),
            pltpu.VMEM((8, SLOTS), jnp.int32),
            pltpu.SMEM((1, 2), jnp.int32),
            pltpu.VMEM(PLAN, jnp.int32),
        ]
        + [pltpu.SemaphoreType.DMA((n,)) for n in (CHUNKS, CHUNKS, CHUNKS, 6)],
    )(*args)


def forward_scratch():
    return [
        pltpu.VMEM((PEERS + 1, RHS, B), BF16),
        pltpu.VMEM((PEERS + 1, B, RHS), BF16),
        pltpu.VMEM((CL + 1, RHS, B), F32),
        pltpu.VMEM((CL + 1, B, RHS), F32),
    ]


def k2(*args):
    return call(
        forward_first, "forward_products",
        shaped((CL, RHS, B), F32), VMEM,
        [SMEM] + [VMEM] * 9,
        forward_scratch(),
    )(*args)


def k3(*args):
    return call(
        image_first, "first_image",
        [
            pltpu.VMEM((RHS, CL * B), F32),
            shaped((CL, RHS, B), BF16),
            shaped((1, SLOTS), jnp.int32),
        ]
        + message_shapes(RHS, BF16),
        [VMEM] * 2 + [SMEM] + [VMEM] * 4,
        [VMEM] * 6,
        [pltpu.VMEM((1, SLOTS), jnp.int32), pltpu.SemaphoreType.DMA],
    )(*args)


def k4(*args):
    return call(
        back_second, "second_transposed_products",
        message_shapes(RHS, BF16),
        [VMEM] * 4,
        [SMEM] + [VMEM] * 4,
        [pltpu.VMEM((CL + 1, RHS, B), BF16), pltpu.VMEM((PEERS + 1, RHS, B), F32)],
    )(*args)


def k5(*args):
    return call(
        forward_second, "second_forward_products",
        shaped((CL, RHS, B), F32), VMEM,
        [SMEM] + [VMEM] * 10,
        forward_scratch(),
    )(*args)


def k6(*args):
    return call(
        image_second, "second_image",
        shaped((RHS, CL * B), F32), VMEM,
        [VMEM, SMEM] + [VMEM] * 5,
        [pltpu.VMEM((CL, RHS, B), F32)],
    )(*args)


def carriers(size, k):
    pairs = []
    for chip in range(size // 2):
        for core in range(2):
            step = k if core == 0 else -k
            pairs.append((2 * chip + core, (2 * (chip + step) + core) % size))
    return pairs


def per_device(
    vectors, diag_blocks, near_blocks, near_rows, near_cols, far_left, far_right, far_rows, far_cols, counts
):
    size = lax.axis_size("rows")
    me = lax.axis_index("rows").reshape(1)

    def swap(block):
        return lax.ppermute(block, "rows", [(i, i ^ 1) for i in range(size)])

    def carry(block, k):
        return lax.ppermute(block, "rows", carriers(size, k))

    def carried(messages):
        second = carry(messages[1], 2)
        return [carry(messages[0], 1), second, carry(messages[2], 3)]

    def exchange(m1, m2, m3, give):
        got = swap(give)
        messages = []
        for k, message in enumerate((m1, m2, m3)):
            messages.append(lax.dynamic_update_slice(message, got[2 * k : 2 * k + 2], (1, 0, 0)))
        return carried(messages) + [got, messages]

    def passed_on(r1, r2, r3):
        return swap(jnp.concatenate([r1[2:4], r2[2:4], r3[2:3]]))

    def in_hbm(x):
        return pltpu.with_memory_space_constraint(x, pltpu.HBM)

    lists = [in_hbm(x.reshape(1, SLOTS)) for x in (near_rows, near_cols, far_rows, far_cols)]
    sib = swap(vectors)
    both = lax.dynamic_update_slice(staged(in_hbm(vectors)), sib[None], (1, 0, 0))
    halo = carried([both] * 3)
    m1, m2, m3, give, plan, *held = k1(
        me, *lists, in_hbm(counts), both, in_hbm(near_blocks), in_hbm(far_left), in_hbm(far_right)
    )
    halo, m1 = lax.optimization_barrier((halo, m1))
    r1, r2, r3, got, messages = exchange(m1, m2, m3, give)
    halo_post = swap(jnp.concatenate([halo[0], halo[1], halo[2][1:]]))
    halo_post, messages = lax.optimization_barrier((halo_post, messages))
    partial = k2(plan, both, *halo, halo_post, diag_blocks, *held)
    partial, r1, r2, r3 = lax.optimization_barrier((partial, r1, r2, r3))
    post = passed_on(r1, r2, r3)
    first_image, rounded, wanted, m1, m2, m3, give = k3(partial, r1, r2, r3, post, got)
    f1, f2, f3, f_got, messages = exchange(m1, m2, m3, give)
    rounded, messages = lax.optimization_barrier((rounded, messages))
    m1, m2, m3, give = k4(plan, rounded, *held)
    f1, f2, f3, give = lax.optimization_barrier((f1, f2, f3, give))
    r1, r2, r3, got, messages = exchange(m1, m2, m3, give)
    f_post = passed_on(f1, f2, f3)
    f_post, messages = lax.optimization_barrier((f_post, messages))
    partial = k5(plan, rounded, f1, f2, f3, f_post, f_got, diag_blocks, *held)
    partial, r1, r2, r3 = lax.optimization_barrier((partial, r1, r2, r3))
    post = passed_on(r1, r2, r3)
    return first_image, k6(partial, wanted, r1, r2, r3, post, got)


def solution(mesh):
    return jax.shard_map(
        per_device,
        mesh=mesh,
        in_specs=(
            P(None, "rows"),
            P("rows", None, None),
            P("rows", None, None),
            P("rows"),
            P("rows"),
            P("rows", None, None),
            P("rows", None, None),
            P("rows"),
            P("rows"),
            P("rows", None),
        ),
        out_specs=(P(None, "rows"), P(None, "rows")),
        check_vma=False,
    )
```

```python
import functools

import jax
import jax.numpy as jnp
from jax import lax
from jax.experimental import pallas as pl
from jax.experimental.pallas import tpu as pltpu
from jax.sharding import PartitionSpec as P

RHS, B, K = 64, 256, 32
CL, SLOTS, CHUNK = 4, 128, 16
CHUNKS = SLOTS // CHUNK
GROUP = B // K
HALF = B // 2
PEERS = 12
DEAD = 12
EXTRA = 16
LEVELS = 32766.0
TINY = 2.0**-100
LN2 = 0.6931471805599453
QUAD = 4
VMEM_BYTES = 16 * 2**20
F32, BF16 = jnp.float32, jnp.bfloat16


def dot(x, y):
    return lax.dot_general(x, y, (((1,), (0,)), ((), ())), preferred_element_type=F32)


def dot_t(x, y):
    return lax.dot_general(x, y, (((1,), (1,)), ((), ())), preferred_element_type=F32)


def peer_number(delta, core):
    kappa, other = delta // 2 - 3, delta % 2
    step = kappa * (1 - 2 * core)
    same = int(other != core)
    if step == 0:
        return 11 if same else DEAD
    if step < 0:
        return 2 * (-step - 1) + same
    return 6 + 2 * (step - 1) + same if step < 3 or not same else DEAD


PLAN = (4, 2 * SLOTS)
COUNTS, WANTED = 64, 80
STEP = 32
GROUPS = 4


class Blocks:
    def __init__(self, plan, near, left, right, sources=None):
        self.plan, self.near, self.left, self.right = plan, near, left, right
        self.sources = sources

    def copy(self, which, chunk):
        source, sem = self.sources[which]
        place = pl.ds(chunk * CHUNK, CHUNK)
        target = (self.near, self.left, self.right)[which]
        return pltpu.make_async_copy(source.at[place], target.at[place], sem.at[chunk])

    def start(self):
        for which in (1, 2, 0):
            self.copy(which, 0).start()

    def start_rest(self, near_chunks, far_chunks):
        def far_start(chunk, carry):
            self.copy(1, chunk).start()
            self.copy(2, chunk).start()
            return carry

        def near_start(chunk, carry):
            self.copy(0, chunk).start()
            return carry

        lax.fori_loop(1, far_chunks, far_start, 0)
        lax.fori_loop(1, near_chunks, near_start, 0)

    def far_loop(self, body):
        def arrived(chunk, carry):
            self.copy(1, chunk).wait()
            self.copy(2, chunk).wait()
            return carry

        if self.sources is not None:
            lax.fori_loop(0, self.plan[2, COUNTS + 1], arrived, 0)

        def step(index, carry):
            groups = []
            for part in range(GROUPS):
                first = index * GROUPS + part
                entries = [self.plan[1, first * GROUP + k] for k in range(GROUP)]
                slots = [entry & 255 for entry in entries]
                left = jnp.concatenate([self.left[slot] for slot in slots], axis=0)
                right = jnp.concatenate([self.right[slot] for slot in slots], axis=0)
                lane = lax.broadcasted_iota(jnp.int32, (1, B), 1) // K
                rows = jnp.zeros((1, B), jnp.int32)
                for k in range(GROUP):
                    rows = jnp.where(lane == k, entries[k] >> 8, rows)
                rows = jnp.broadcast_to(rows, (RHS, B))
                groups.append((left, right, rows, [self.plan[2, 2 * first + half] for half in (0, 1)]))
            body(groups)
            return carry

        lax.fori_loop(0, self.plan[2, COUNTS + 2], step, 0)

    def near_loop(self, body):
        size = STEP if self.sources is None else CHUNK

        def step(index, carry):
            if self.sources is not None:
                self.copy(0, index).wait()
            for part in range(size):
                slot = index * size + part
                code = self.plan[0, slot]
                body(part, code & 7, code >> 3, self.near[slot])
            return carry

        lax.fori_loop(0, self.plan[2, COUNTS] * (STEP // size), step, 0)


def halves(x, axis):
    return (x[:HALF], x[HALF:]) if axis == 0 else (x[:, :HALF], x[:, HALF:])


def back_products(blocks, own, acc):
    def far(groups):
        coefs = []
        for left, right, rows, partners in groups:
            every = dot_t(own[0:CL].reshape(CL * RHS, B), left)
            coef = jnp.zeros((RHS, B), F32)
            for cluster in range(CL):
                coef = jnp.where(rows == cluster, every[cluster * RHS : (cluster + 1) * RHS], coef)
            coefs.append(coef.astype(BF16))
        terms = []
        for coef, (left, right, rows, partners) in zip(coefs, groups):
            for part, block, partner in zip(halves(coef, 1), halves(right, 0), partners):
                terms.append((partner, dot(part, block)))
        for partner, term in terms:
            acc[partner] += term

    def near(part, row, partner, block):
        acc[partner] += dot(own[row], block)

    blocks.far_loop(far)
    blocks.near_loop(near)


def forward_products(blocks, fetched, turned, acc, acc_turned):
    turned[DEAD] = jnp.zeros((B, RHS), BF16)
    for partner in range(PEERS):
        turned[partner] = fetched[partner].T
    acc_turned[...] = jnp.zeros_like(acc_turned)

    def far(groups):
        spreads = []
        for left, right, rows, partners in groups:
            coef = [dot_t(fetched[partner], block) for partner, block in zip(partners, halves(right, 0))]
            coef = jnp.concatenate(coef, axis=1).astype(BF16).astype(F32)
            spread = [jnp.where(rows == cluster, coef, 0.0).astype(BF16) for cluster in range(CL)]
            spreads.append(jnp.concatenate(spread, axis=0))
        terms = [dot(spread, group[0]) for spread, group in zip(spreads, groups)]
        total = terms[0]
        for term in terms[1:]:
            total += term
        acc[0:CL] += total.reshape(CL, RHS, B)

    def near(part, row, partner, block):
        if part % 2 == 0:
            acc[row] += dot_t(fetched[partner], block)
        else:
            acc_turned[row] += dot(block, turned[partner])

    blocks.far_loop(far)
    blocks.near_loop(near)
    for cluster in range(CL):
        acc[cluster] += acc_turned[cluster].T


def make_plan(me, lists, few, draft):
    core = me % 2
    base = me - core - 6
    lane = lax.broadcasted_iota(jnp.int32, (1, SLOTS), 1)
    row16 = lax.broadcasted_iota(jnp.int32, (16, SLOTS), 0)
    kinds = []
    for kind in (0, 1):
        rows, cols = lists[2 * kind : 2 * kind + 1, :], lists[2 * kind + 1 : 2 * kind + 2, :]
        live = lane < few[0, kind]
        delta = ((cols >> 2) - base) & 15
        partner = jnp.full((1, SLOTS), DEAD, jnp.int32)
        for value in range(14):
            pair = [peer_number(value, a) for a in (0, 1)]
            partner = jnp.where(delta == value, jnp.where(core == 0, pair[0], pair[1]), partner)
        partner = jnp.where(live, partner, DEAD)
        kinds.append((jnp.where(live, rows & (CL - 1), CL), partner, cols & (CL - 1)))
    (near_row, near_rho, near_part), (far_row, far_rho, far_part) = kinds
    wide = lambda x: jnp.broadcast_to(x, (16, SLOTS))
    hot = row16 == wide(far_rho)
    wanted = jnp.maximum(
        jnp.where(row16 == wide(near_rho), wide(near_part).astype(F32), 0.0),
        jnp.where(hot, wide(far_part).astype(F32), 0.0),
    )
    wanted = jnp.max(wanted, axis=1, keepdims=True)
    hot = jnp.where(hot, 1.0, 0.0)
    square = (SLOTS, SLOTS)
    earlier = lax.broadcasted_iota(jnp.int32, square, 0) < lax.broadcasted_iota(jnp.int32, square, 1)
    rank = dot(hot.astype(BF16), jnp.where(earlier, 1.0, 0.0).astype(BF16)).astype(jnp.int32)
    number = wide(jnp.sum(hot, axis=1, keepdims=True)).astype(jnp.int32)
    padded = ((number + (QUAD - 1)) >> 2) << 2
    place = jnp.full((1, SLOTS), -1, jnp.int32)
    quad_rho = jnp.full((1, SLOTS), DEAD, jnp.int32)
    first = jnp.zeros((1, SLOTS), jnp.int32)
    for rho in range(PEERS):
        place = jnp.where(far_rho == rho, rank[rho : rho + 1] + first, place)
        last = first + padded[rho : rho + 1]
        quad_rho = jnp.where((lane * QUAD >= first) & (lane * QUAD < last), rho, quad_rho)
        first = last
    column = jnp.transpose(jnp.broadcast_to(place.astype(F32), square))
    spots = lax.broadcasted_iota(jnp.int32, square, 1).astype(F32)
    hits = jnp.concatenate([jnp.where(column == spots + shift, 1.0, 0.0).astype(BF16) for shift in (0.0, float(SLOTS))], axis=1)
    codes = jnp.where(row16 == 0, wide(lane), jnp.where(row16 == 1, wide(far_row), 1)).astype(F32).astype(BF16)
    found = dot(codes, hits)
    entry = jnp.where(found[2:3] > 0.5, found[0:1] + 256.0 * found[1:2], 256.0 * CL).astype(jnp.int32)
    wanted = jnp.sum(jnp.where(row16 + WANTED == wide(lane), wide(wanted), 0.0), axis=0, keepdims=True).astype(jnp.int32)
    draft[0:1, 0:SLOTS] = near_row + 8 * near_rho
    draft[1:2, :] = entry
    numbers = jnp.where(lane == COUNTS, (few[0, 0] + (STEP - 1)) // STEP, jnp.where(lane < COUNTS, quad_rho, wanted))
    numbers = jnp.where(lane == COUNTS + 1, (few[0, 1] + (CHUNK - 1)) // CHUNK, numbers)
    steps = (first + (2 * GROUPS * QUAD - 1)) >> (GROUPS.bit_length() + 2)
    draft[2:3, 0:SLOTS] = jnp.where(lane == COUNTS + 2, steps, numbers)


def place_out(rho):
    if rho == 11:
        return 3, 6
    if rho < 6:
        return 3, rho ^ 1
    k, same = divmod(rho - 6, 2)
    return k, 3 * same


def place_in(rho):
    if rho == 11:
        return 4, 6
    if rho < 6:
        return rho // 2, rho % 2
    return 3, rho - 6


MESSAGE = (4, 4, 3)


def back_first(
    me, near_rows, near_cols, far_rows, far_cols, counts, both, near, left, right,
    m1, m2, m3, give, plan, near_held, left_held, right_held,
    own, acc, lists, few, draft, near_sem, left_sem, right_sem, list_sem,
):
    blocks = Blocks(plan, near_held, left_held, right_held, ((near, near_sem), (left, left_sem), (right, right_sem)))
    copies = [pltpu.make_async_copy(counts, few, list_sem.at[4])]
    for index, source in enumerate((near_rows, near_cols, far_rows, far_cols)):
        copies.append(pltpu.make_async_copy(source, lists.at[pl.ds(index, 1)], list_sem.at[index]))
    for copy in copies:
        copy.start()
    blocks.start()
    for cluster in range(CL):
        own[cluster] = both[0, :, cluster * B : (cluster + 1) * B]
    own[CL] = jnp.zeros((RHS, B), BF16)
    draft[...] = jnp.zeros_like(draft)
    copies[0].wait()
    near_steps = (few[0, 0] + (STEP - 1)) // STEP
    blocks.start_rest(near_steps * (STEP // CHUNK), (few[0, 1] + (CHUNK - 1)) // CHUNK)
    for copy in copies[1:]:
        copy.wait()
    make_plan(me[0], lists, few, draft)
    copy = pltpu.make_async_copy(draft, plan, list_sem.at[5])
    copy.start()
    acc[...] = jnp.zeros_like(acc)
    copy.wait()
    back_products(blocks, own, acc)
    outs = (m1, m2, m3, give)
    for rho in range(PEERS):
        message, index = place_out(rho)
        outs[message][index, 0:RHS], power = coded(acc[rho])
        half = lax.broadcasted_iota(jnp.int32, (EXTRA, B), 0) < EXTRA // 2
        outs[message][index, RHS:] = jnp.where(half, power, plan[2, WANTED + rho]).astype(jnp.int16)


def forward_first(
    plan, both, h1, h2, h3, post, diag, near, left, right,
    out,
    fetched, turned, acc, acc_turned,
):
    halo = (h1, h2, h3)
    for rho in range(PEERS):
        lanes = pl.ds(pl.multiple_of(plan[2, WANTED + rho] * B, B), B)
        if rho == 11:
            fetched[rho] = both[1, :, lanes]
        elif rho < 6:
            fetched[rho] = halo[rho // 2][rho % 2, :, lanes]
        else:
            k, same = divmod(rho - 6, 2)
            fetched[rho] = post[2 * k + (1 - same if k < 2 else 0), :, lanes]
    fetched[DEAD] = jnp.zeros((RHS, B), BF16)
    acc[CL] = jnp.zeros((RHS, B), F32)
    for cluster in range(CL):
        acc[cluster] = dot_t(both[0, :, cluster * B : (cluster + 1) * B], diag[cluster])
    forward_products(Blocks(plan, near, left, right), fetched, turned, acc, acc_turned)
    out[...] = acc[0:CL]


STRIP = 16


def coded(block):
    top = jnp.maximum(jnp.max(jnp.abs(block), axis=0, keepdims=True), TINY)
    power = jnp.ceil(jnp.log(top * (1.0 / LEVELS)) * (1.0 / LN2) + 1e-3)
    scaled = block * jnp.exp(power * -LN2)
    return jnp.floor(scaled + 0.5).astype(jnp.int32).astype(jnp.int16), power.astype(jnp.int32)


def image_first(
    partial, r1, r2, r3, post, got,
    image, rounded, marked, m1, m2, m3, give,
    draft, wanted, sem,
):
    ins = (r1, r2, r3, post, got)
    places = [place_in(rho) for rho in range(PEERS)]
    extras = [ins[message][index, RHS:].astype(jnp.int32) for message, index in places]
    units = [jnp.exp(extra[0:1].astype(F32) * LN2) for extra in extras]
    marks = [extra[EXTRA // 2 : EXTRA // 2 + 1] for extra in extras]
    lane = lax.broadcasted_iota(jnp.int32, (1, SLOTS), 1)
    packed = jnp.zeros((1, SLOTS), jnp.int32)
    for rho, mark in enumerate(marks):
        packed = jnp.where(lane == rho, mark[:, 0:SLOTS], packed)
        marked[rho : rho + 1] = mark
    draft[...] = packed
    copy = pltpu.make_async_copy(draft, wanted, sem)
    copy.start()
    for first in range(0, RHS, STRIP):
        rows = slice(first, first + STRIP)
        totals = [partial[cluster, rows] for cluster in range(CL)]
        for (message, index), mark, unit in zip(places, marks, units):
            block = ins[message][index, rows].astype(jnp.int32).astype(F32) * unit
            mark = jnp.broadcast_to(mark, (STRIP, B))
            for cluster in range(CL):
                totals[cluster] += jnp.where(mark == cluster, block, 0.0)
        for cluster in range(CL):
            image[rows, cluster * B : (cluster + 1) * B] = totals[cluster]
            rounded[cluster, rows] = totals[cluster].astype(BF16)
    copy.wait()
    outs = (m1, m2, m3, give)
    for rho in range(PEERS):
        message, index = place_out(rho)
        outs[message][index] = rounded[wanted[0, rho]]


def back_second(
    plan, rounded, near, left, right,
    m1, m2, m3, give,
    own, acc,
):
    own[0:CL] = rounded[...]
    own[CL] = jnp.zeros((RHS, B), BF16)
    acc[...] = jnp.zeros_like(acc)
    back_products(Blocks(plan, near, left, right), own, acc)
    outs = (m1, m2, m3, give)
    for rho in range(PEERS):
        message, index = place_out(rho)
        outs[message][index] = acc[rho].astype(BF16)


def forward_second(
    plan, own, r1, r2, r3, post, got, diag, near, left, right,
    out,
    fetched, turned, acc, acc_turned,
):
    ins = (r1, r2, r3, post, got)
    for rho in range(PEERS):
        message, index = place_in(rho)
        fetched[rho] = ins[message][index]
    fetched[DEAD] = jnp.zeros((RHS, B), BF16)
    acc[CL] = jnp.zeros((RHS, B), F32)
    for cluster in range(CL):
        acc[cluster] = dot_t(own[cluster], diag[cluster])
    forward_products(Blocks(plan, near, left, right), fetched, turned, acc, acc_turned)
    out[...] = acc[0:CL]


def image_second(partial, marked, r1, r2, r3, post, got, image, acc, sem):
    ins = (r1, r2, r3, post, got)
    places = [place_in(rho) for rho in range(PEERS)]
    marks = [marked[rho : rho + 1] for rho in range(PEERS)]
    copies = []
    for first in range(0, RHS, STRIP):
        rows = slice(first, first + STRIP)
        totals = [partial[cluster, rows] for cluster in range(CL)]
        for (message, index), mark in zip(places, marks):
            block = ins[message][index, rows].astype(F32)
            mark = jnp.broadcast_to(mark, (STRIP, B))
            for cluster in range(CL):
                totals[cluster] += jnp.where(mark == cluster, block, 0.0)
        for cluster in range(CL):
            acc[rows, cluster * B : (cluster + 1) * B] = totals[cluster]
        copies.append(pltpu.make_async_copy(acc.at[rows], image.at[rows], sem.at[first // STRIP]))
        copies[-1].start()
    for copy in copies:
        copy.wait()


SMEM = pl.BlockSpec(memory_space=pltpu.SMEM)
VMEM = pl.BlockSpec(memory_space=pltpu.VMEM)
ANY = pl.BlockSpec(memory_space=pl.ANY)
HBM = pl.BlockSpec(memory_space=pltpu.HBM)


def call(kernel, name, outs, out_specs, in_specs, scratch):
    return pl.pallas_call(
        kernel,
        name=name,
        out_shape=outs,
        in_specs=in_specs,
        out_specs=out_specs,
        scratch_shapes=scratch,
        compiler_params=pltpu.CompilerParams(vmem_limit_bytes=VMEM_BYTES),
        cost_estimate=pl.CostEstimate(flops=2 * 10**9, bytes_accessed=22 * 10**6, transcendentals=0),
    )


def shaped(shape, dtype):
    return jax.ShapeDtypeStruct(shape, dtype)


def message_shapes(rows, dtype):
    return [shaped((n, rows, B), dtype) for n in MESSAGE + (7,)]


def stage(source, target, sem):
    copy = pltpu.make_async_copy(source, target.at[0], sem)
    copy.start()
    copy.wait()


def staged(vectors):
    return call(stage, "staged", shaped((2, *vectors.shape), BF16), VMEM, [HBM], [pltpu.SemaphoreType.DMA])(vectors)


def k1(*args):
    held = [pltpu.VMEM(shape, BF16) for shape in ((SLOTS, B, B), (SLOTS, K, B), (SLOTS, K, B))]
    return call(
        back_first, "transposed_products",
        message_shapes(RHS + EXTRA, jnp.int16) + [shaped(PLAN, jnp.int32)] + held,
        [VMEM] * 4 + [SMEM] + [VMEM] * 3,
        [SMEM] + [HBM] * 5 + [VMEM] + [HBM] * 3,
        [
            pltpu.VMEM((CL + 1, RHS, B), BF16),
            pltpu.VMEM((PEERS + 1, RHS, B), F32),
            pltpu.VMEM((8, SLOTS), jnp.int32),
            pltpu.SMEM((1, 2), jnp.int32),
            pltpu.VMEM(PLAN, jnp.int32),
        ]
        + [pltpu.SemaphoreType.DMA((n,)) for n in (CHUNKS, CHUNKS, CHUNKS, 6)],
    )(*args)


def forward_scratch():
    return [
        pltpu.VMEM((PEERS + 1, RHS, B), BF16),
        pltpu.VMEM((PEERS + 1, B, RHS), BF16),
        pltpu.VMEM((CL + 1, RHS, B), F32),
        pltpu.VMEM((CL + 1, B, RHS), F32),
    ]


def k2(*args):
    return call(
        forward_first, "forward_products",
        shaped((CL, RHS, B), F32), VMEM,
        [SMEM] + [VMEM] * 9,
        forward_scratch(),
    )(*args)


def k3(*args):
    return call(
        image_first, "first_image",
        [
            pltpu.VMEM((RHS, CL * B), F32),
            shaped((CL, RHS, B), BF16),
            shaped((16, B), jnp.int32),
        ]
        + message_shapes(RHS, BF16),
        [VMEM] * 7,
        [VMEM] * 6,
        [pltpu.VMEM((1, SLOTS), jnp.int32), pltpu.SMEM((1, SLOTS), jnp.int32), pltpu.SemaphoreType.DMA],
    )(*args)


def k4(*args):
    return call(
        back_second, "second_transposed_products",
        message_shapes(RHS, BF16),
        [VMEM] * 4,
        [SMEM] + [VMEM] * 4,
        [pltpu.VMEM((CL + 1, RHS, B), BF16), pltpu.VMEM((PEERS + 1, RHS, B), F32)],
    )(*args)


def k5(*args):
    return call(
        forward_second, "second_forward_products",
        shaped((CL, RHS, B), F32), VMEM,
        [SMEM] + [VMEM] * 10,
        forward_scratch(),
    )(*args)


def k6(*args):
    return call(
        image_second, "second_image",
        shaped((RHS, CL * B), F32), HBM,
        [VMEM] * 7,
        [pltpu.VMEM((RHS, CL * B), F32), pltpu.SemaphoreType.DMA((RHS // STRIP,))],
    )(*args)


def carriers(size, k):
    pairs = []
    for chip in range(size // 2):
        for core in range(2):
            step = k if core == 0 else -k
            pairs.append((2 * chip + core, (2 * (chip + step) + core) % size))
    return pairs


def per_device(
    vectors, diag_blocks, near_blocks, near_rows, near_cols, far_left, far_right, far_rows, far_cols, counts
):
    size = lax.axis_size("rows")
    me = lax.axis_index("rows").reshape(1)

    def swap(block):
        return lax.ppermute(block, "rows", [(i, i ^ 1) for i in range(size)])

    def carry(block, k):
        return lax.ppermute(block, "rows", carriers(size, k))

    def carried(messages):
        second = carry(messages[1], 2)
        return [carry(messages[0], 1), second, carry(messages[2], 3)]

    def exchange(m1, m2, m3, give):
        got = swap(give)
        messages = []
        for k, message in enumerate((m1, m2, m3)):
            messages.append(lax.dynamic_update_slice(message, got[2 * k : 2 * k + 2], (1, 0, 0)))
        return carried(messages) + [got, messages]

    def passed_on(r1, r2, r3):
        return swap(jnp.concatenate([r1[2:4], r2[2:4], r3[2:3]]))

    def in_hbm(x):
        return pltpu.with_memory_space_constraint(x, pltpu.HBM)

    lists = [in_hbm(x.reshape(1, SLOTS)) for x in (near_rows, near_cols, far_rows, far_cols)]
    sib = swap(vectors)
    both = lax.dynamic_update_slice(staged(in_hbm(vectors)), sib[None], (1, 0, 0))
    halo = carried([both] * 3)
    m1, m2, m3, give, plan, *held = k1(
        me, *lists, in_hbm(counts), both, in_hbm(near_blocks), in_hbm(far_left), in_hbm(far_right)
    )
    halo, give = lax.optimization_barrier((halo, give))
    r1, r2, r3, got, messages = exchange(m1, m2, m3, give)
    halo, got = lax.optimization_barrier((halo, got))
    halo_post = swap(jnp.concatenate([halo[0], halo[1], halo[2][1:]]))
    halo_post, messages = lax.optimization_barrier((halo_post, messages))
    partial = k2(plan, both, *halo, halo_post, diag_blocks, *held)
    partial, r1, r2, r3 = lax.optimization_barrier((partial, r1, r2, r3))
    post = passed_on(r1, r2, r3)
    first_image, rounded, marked, m1, m2, m3, give = k3(partial, r1, r2, r3, post, got)
    f1, f2, f3, f_got, messages = exchange(m1, m2, m3, give)
    rounded, messages = lax.optimization_barrier((rounded, messages))
    m1, m2, m3, give = k4(plan, rounded, *held)
    f1, f2, f3, give = lax.optimization_barrier((f1, f2, f3, give))
    r1, r2, r3, got, messages = exchange(m1, m2, m3, give)
    f_post = passed_on(f1, f2, f3)
    f_post, messages = lax.optimization_barrier((f_post, messages))
    partial = k5(plan, rounded, f1, f2, f3, f_post, f_got, diag_blocks, *held)
    partial, r1, r2, r3 = lax.optimization_barrier((partial, r1, r2, r3))
    post = passed_on(r1, r2, r3)
    return first_image, k6(partial, marked, r1, r2, r3, post, got)


def solution(mesh):
    return jax.shard_map(
        per_device,
        mesh=mesh,
        in_specs=(
            P(None, "rows"),
            P("rows", None, None),
            P("rows", None, None),
            P("rows"),
            P("rows"),
            P("rows", None, None),
            P("rows", None, None),
            P("rows"),
            P("rows"),
            P("rows", None),
        ),
        out_specs=(P(None, "rows"), P(None, "rows")),
        check_vma=False,
    )
```

```python
import functools

import jax
import jax.numpy as jnp
from jax import lax
from jax.experimental import pallas as pl
from jax.experimental.pallas import tpu as pltpu
from jax.sharding import PartitionSpec as P

RHS, B, K = 64, 256, 32
CL, SLOTS, CHUNK = 4, 128, 16
CHUNKS = SLOTS // CHUNK
GROUP = B // K
HALF = B // 2
PEERS = 12
DEAD = 12
EXTRA = 16
LEVELS = 32766.0
TINY = 2.0**-100
LN2 = 0.6931471805599453
QUAD = 4
VMEM_BYTES = 16 * 2**20
F32, BF16 = jnp.float32, jnp.bfloat16


def dot(x, y):
    return lax.dot_general(x, y, (((1,), (0,)), ((), ())), preferred_element_type=F32)


def dot_t(x, y):
    return lax.dot_general(x, y, (((1,), (1,)), ((), ())), preferred_element_type=F32)


def peer_number(delta, core):
    kappa, other = delta // 2 - 3, delta % 2
    step = kappa * (1 - 2 * core)
    same = int(other != core)
    if step == 0:
        return 11 if same else DEAD
    if step < 0:
        return 2 * (-step - 1) + same
    return 6 + 2 * (step - 1) + same if step < 3 or not same else DEAD


PLAN = (4, 2 * SLOTS)
COUNTS, WANTED = 64, 80
STEP = 32
GROUPS = 4


class Blocks:
    def __init__(self, plan, near, left, right, sources=None):
        self.plan, self.near, self.left, self.right = plan, near, left, right
        self.sources = sources

    def copy(self, which, chunk):
        source, sem = self.sources[which]
        place = pl.ds(chunk * CHUNK, CHUNK)
        target = (self.near, self.left, self.right)[which]
        return pltpu.make_async_copy(source.at[place], target.at[place], sem.at[chunk])

    def start(self):
        for which in (1, 2, 0):
            self.copy(which, 0).start()

    def start_rest(self, near_chunks, far_chunks):
        def far_start(chunk, carry):
            self.copy(1, chunk).start()
            self.copy(2, chunk).start()
            return carry

        def near_start(chunk, carry):
            self.copy(0, chunk).start()
            return carry

        lax.fori_loop(1, far_chunks, far_start, 0)
        lax.fori_loop(1, near_chunks, near_start, 0)

    def far_loop(self, body):
        def arrived(chunk, carry):
            self.copy(1, chunk).wait()
            self.copy(2, chunk).wait()
            return carry

        if self.sources is not None:
            lax.fori_loop(0, self.plan[2, COUNTS + 1], arrived, 0)

        def step(index, carry):
            groups = []
            for part in range(GROUPS):
                first = index * GROUPS + part
                entries = [self.plan[1, first * GROUP + k] for k in range(GROUP)]
                slots = [entry & 255 for entry in entries]
                left = jnp.concatenate([self.left[slot] for slot in slots], axis=0)
                right = jnp.concatenate([self.right[slot] for slot in slots], axis=0)
                lane = lax.broadcasted_iota(jnp.int32, (1, B), 1) // K
                rows = jnp.zeros((1, B), jnp.int32)
                for k in range(GROUP):
                    rows = jnp.where(lane == k, entries[k] >> 8, rows)
                rows = jnp.broadcast_to(rows, (RHS, B))
                groups.append((left, right, rows, [self.plan[2, 2 * first + half] for half in (0, 1)]))
            body(groups)
            return carry

        lax.fori_loop(0, self.plan[2, COUNTS + 2], step, 0)

    def near_loop(self, body):
        size = STEP if self.sources is None else CHUNK

        def step(index, carry):
            if self.sources is not None:
                self.copy(0, index).wait()
            for part in range(size):
                slot = index * size + part
                code = self.plan[0, slot]
                body(part, code & 7, code >> 3, self.near[slot])
            return carry

        lax.fori_loop(0, self.plan[2, COUNTS] * (STEP // size), step, 0)


def halves(x, axis):
    return (x[:HALF], x[HALF:]) if axis == 0 else (x[:, :HALF], x[:, HALF:])


def back_products(blocks, own, acc):
    def far(groups):
        coefs = []
        for left, right, rows, partners in groups:
            every = dot_t(own[0:CL].reshape(CL * RHS, B), left)
            coef = jnp.zeros((RHS, B), F32)
            for cluster in range(CL):
                coef = jnp.where(rows == cluster, every[cluster * RHS : (cluster + 1) * RHS], coef)
            coefs.append(coef.astype(BF16))
        terms = []
        for coef, (left, right, rows, partners) in zip(coefs, groups):
            for part, block, partner in zip(halves(coef, 1), halves(right, 0), partners):
                terms.append((partner, dot(part, block)))
        for partner, term in terms:
            acc[partner] += term

    def near(part, row, partner, block):
        acc[partner] += dot(own[row], block)

    blocks.far_loop(far)
    blocks.near_loop(near)


def forward_products(blocks, fetched, turned, acc, acc_turned):
    turned[DEAD] = jnp.zeros((B, RHS), BF16)
    for partner in range(PEERS):
        turned[partner] = fetched[partner].T
    acc_turned[...] = jnp.zeros_like(acc_turned)

    def far(groups):
        spreads = []
        for left, right, rows, partners in groups:
            coef = [dot_t(fetched[partner], block) for partner, block in zip(partners, halves(right, 0))]
            coef = jnp.concatenate(coef, axis=1).astype(BF16).astype(F32)
            spread = [jnp.where(rows == cluster, coef, 0.0).astype(BF16) for cluster in range(CL)]
            spreads.append(jnp.concatenate(spread, axis=0))
        terms = [dot(spread, group[0]) for spread, group in zip(spreads, groups)]
        total = terms[0]
        for term in terms[1:]:
            total += term
        acc[0:CL] += total.reshape(CL, RHS, B)

    def near(part, row, partner, block):
        if part % 2 == 0:
            acc[row] += dot_t(fetched[partner], block)
        else:
            acc_turned[row] += dot(block, turned[partner])

    blocks.far_loop(far)
    blocks.near_loop(near)
    for cluster in range(CL):
        acc[cluster] += acc_turned[cluster].T


def make_plan(me, lists, few, draft):
    core = me % 2
    base = me - core - 6
    lane = lax.broadcasted_iota(jnp.int32, (1, SLOTS), 1)
    row16 = lax.broadcasted_iota(jnp.int32, (16, SLOTS), 0)
    kinds = []
    for kind in (0, 1):
        rows, cols = lists[2 * kind : 2 * kind + 1, :], lists[2 * kind + 1 : 2 * kind + 2, :]
        live = lane < few[0, kind]
        delta = ((cols >> 2) - base) & 15
        partner = jnp.full((1, SLOTS), DEAD, jnp.int32)
        for value in range(14):
            pair = [peer_number(value, a) for a in (0, 1)]
            partner = jnp.where(delta == value, jnp.where(core == 0, pair[0], pair[1]), partner)
        partner = jnp.where(live, partner, DEAD)
        kinds.append((jnp.where(live, rows & (CL - 1), CL), partner, cols & (CL - 1)))
    (near_row, near_rho, near_part), (far_row, far_rho, far_part) = kinds
    wide = lambda x: jnp.broadcast_to(x, (16, SLOTS))
    hot = row16 == wide(far_rho)
    wanted = jnp.maximum(
        jnp.where(row16 == wide(near_rho), wide(near_part).astype(F32), 0.0),
        jnp.where(hot, wide(far_part).astype(F32), 0.0),
    )
    wanted = jnp.max(wanted, axis=1, keepdims=True)
    hot = jnp.where(hot, 1.0, 0.0)
    square = (SLOTS, SLOTS)
    earlier = lax.broadcasted_iota(jnp.int32, square, 0) < lax.broadcasted_iota(jnp.int32, square, 1)
    rank = dot(hot.astype(BF16), jnp.where(earlier, 1.0, 0.0).astype(BF16)).astype(jnp.int32)
    number = wide(jnp.sum(hot, axis=1, keepdims=True)).astype(jnp.int32)
    padded = ((number + (QUAD - 1)) >> 2) << 2
    place = jnp.full((1, SLOTS), -1, jnp.int32)
    quad_rho = jnp.full((1, SLOTS), DEAD, jnp.int32)
    first = jnp.zeros((1, SLOTS), jnp.int32)
    for rho in range(PEERS):
        place = jnp.where(far_rho == rho, rank[rho : rho + 1] + first, place)
        last = first + padded[rho : rho + 1]
        quad_rho = jnp.where((lane * QUAD >= first) & (lane * QUAD < last), rho, quad_rho)
        first = last
    column = jnp.transpose(jnp.broadcast_to(place.astype(F32), square))
    spots = lax.broadcasted_iota(jnp.int32, square, 1).astype(F32)
    hits = jnp.concatenate([jnp.where(column == spots + shift, 1.0, 0.0).astype(BF16) for shift in (0.0, float(SLOTS))], axis=1)
    codes = jnp.where(row16 == 0, wide(lane), jnp.where(row16 == 1, wide(far_row), 1)).astype(F32).astype(BF16)
    found = dot(codes, hits)
    entry = jnp.where(found[2:3] > 0.5, found[0:1] + 256.0 * found[1:2], 256.0 * CL).astype(jnp.int32)
    wanted = jnp.sum(jnp.where(row16 + WANTED == wide(lane), wide(wanted), 0.0), axis=0, keepdims=True).astype(jnp.int32)
    draft[0:1, 0:SLOTS] = near_row + 8 * near_rho
    draft[1:2, :] = entry
    numbers = jnp.where(lane == COUNTS, (few[0, 0] + (STEP - 1)) // STEP, jnp.where(lane < COUNTS, quad_rho, wanted))
    numbers = jnp.where(lane == COUNTS + 1, (few[0, 1] + (CHUNK - 1)) // CHUNK, numbers)
    steps = (first + (2 * GROUPS * QUAD - 1)) >> (GROUPS.bit_length() + 2)
    draft[2:3, 0:SLOTS] = jnp.where(lane == COUNTS + 2, steps, numbers)


def place_out(rho):
    if rho == 11:
        return 3, 6
    if rho < 6:
        return 3, rho ^ 1
    k, same = divmod(rho - 6, 2)
    return k, 3 * same


def place_in(rho):
    if rho == 11:
        return 4, 6
    if rho < 6:
        return rho // 2, rho % 2
    return 3, rho - 6


MESSAGE = (4, 4, 3)


def back_first(
    me, near_rows, near_cols, far_rows, far_cols, counts, both, near, left, right,
    m1, m2, m3, give, draft, near_held, left_held, right_held,
    own, acc, lists, few, plan, near_sem, left_sem, right_sem, list_sem,
):
    blocks = Blocks(plan, near_held, left_held, right_held, ((near, near_sem), (left, left_sem), (right, right_sem)))
    copies = [pltpu.make_async_copy(counts, few, list_sem.at[4])]
    for index, source in enumerate((near_rows, near_cols, far_rows, far_cols)):
        copies.append(pltpu.make_async_copy(source, lists.at[pl.ds(index, 1)], list_sem.at[index]))
    for copy in copies:
        copy.start()
    blocks.start()
    for cluster in range(CL):
        own[cluster] = both[0, :, cluster * B : (cluster + 1) * B]
    own[CL] = jnp.zeros((RHS, B), BF16)
    draft[...] = jnp.zeros_like(draft)
    copies[0].wait()
    near_steps = (few[0, 0] + (STEP - 1)) // STEP
    blocks.start_rest(near_steps * (STEP // CHUNK), (few[0, 1] + (CHUNK - 1)) // CHUNK)
    for copy in copies[1:]:
        copy.wait()
    make_plan(me[0], lists, few, draft)
    copy = pltpu.make_async_copy(draft, plan, list_sem.at[5])
    copy.start()
    acc[...] = jnp.zeros_like(acc)
    copy.wait()
    back_products(blocks, own, acc)
    outs = (m1, m2, m3, give)
    for rho in range(PEERS):
        message, index = place_out(rho)
        outs[message][index, 0:RHS], power = coded(acc[rho])
        half = lax.broadcasted_iota(jnp.int32, (EXTRA, B), 0) < EXTRA // 2
        outs[message][index, RHS:] = jnp.where(half, power, plan[2, WANTED + rho]).astype(jnp.int16)


def forward_first(
    draft, both, h1, h2, h3, post, diag, near, left, right,
    out,
    fetched, turned, acc, acc_turned, plan, sem,
):
    copy = pltpu.make_async_copy(draft, plan, sem)
    copy.start()
    fetched[DEAD] = jnp.zeros((RHS, B), BF16)
    acc[CL] = jnp.zeros((RHS, B), F32)
    for cluster in range(CL):
        acc[cluster] = dot_t(both[0, :, cluster * B : (cluster + 1) * B], diag[cluster])
    copy.wait()
    halo = (h1, h2, h3)
    for rho in range(PEERS):
        lanes = pl.ds(pl.multiple_of(plan[2, WANTED + rho] * B, B), B)
        if rho == 11:
            fetched[rho] = both[1, :, lanes]
        elif rho < 6:
            fetched[rho] = halo[rho // 2][rho % 2, :, lanes]
        else:
            k, same = divmod(rho - 6, 2)
            fetched[rho] = post[2 * k + (1 - same if k < 2 else 0), :, lanes]
    forward_products(Blocks(plan, near, left, right), fetched, turned, acc, acc_turned)
    out[...] = acc[0:CL]


STRIP = 16


def coded(block):
    top = jnp.maximum(jnp.max(jnp.abs(block), axis=0, keepdims=True), TINY)
    power = jnp.ceil(jnp.log(top * (1.0 / LEVELS)) * (1.0 / LN2) + 1e-3)
    scaled = block * jnp.exp(power * -LN2)
    return jnp.floor(scaled + 0.5).astype(jnp.int32).astype(jnp.int16), power.astype(jnp.int32)


def image_first(
    partial, r1, r2, r3, post, got,
    image, rounded, marked, m1, m2, m3, give,
    draft, wanted, sem,
):
    ins = (r1, r2, r3, post, got)
    places = [place_in(rho) for rho in range(PEERS)]
    extras = [ins[message][index, RHS:].astype(jnp.int32) for message, index in places]
    units = [jnp.exp(extra[0:1].astype(F32) * LN2) for extra in extras]
    marks = [extra[EXTRA // 2 : EXTRA // 2 + 1] for extra in extras]
    lane = lax.broadcasted_iota(jnp.int32, (1, SLOTS), 1)
    packed = jnp.zeros((1, SLOTS), jnp.int32)
    for rho, mark in enumerate(marks):
        packed = jnp.where(lane == rho, mark[:, 0:SLOTS], packed)
        marked[rho : rho + 1] = mark
    draft[...] = packed
    copy = pltpu.make_async_copy(draft, wanted, sem)
    copy.start()
    for first in range(0, RHS, STRIP):
        rows = slice(first, first + STRIP)
        totals = [partial[cluster, rows] for cluster in range(CL)]
        for (message, index), mark, unit in zip(places, marks, units):
            block = ins[message][index, rows].astype(jnp.int32).astype(F32) * unit
            mark = jnp.broadcast_to(mark, (STRIP, B))
            for cluster in range(CL):
                totals[cluster] += jnp.where(mark == cluster, block, 0.0)
        for cluster in range(CL):
            image[rows, cluster * B : (cluster + 1) * B] = totals[cluster]
            rounded[cluster, rows] = totals[cluster].astype(BF16)
    copy.wait()
    outs = (m1, m2, m3, give)
    for rho in range(PEERS):
        message, index = place_out(rho)
        outs[message][index] = rounded[wanted[0, rho]]


def back_second(
    draft, rounded, near, left, right,
    m1, m2, m3, give,
    own, acc, plan, sem,
):
    copy = pltpu.make_async_copy(draft, plan, sem)
    copy.start()
    own[0:CL] = rounded[...]
    own[CL] = jnp.zeros((RHS, B), BF16)
    acc[...] = jnp.zeros_like(acc)
    copy.wait()
    back_products(Blocks(plan, near, left, right), own, acc)
    outs = (m1, m2, m3, give)
    for rho in range(PEERS):
        message, index = place_out(rho)
        outs[message][index] = acc[rho].astype(BF16)


def forward_second(
    draft, own, r1, r2, r3, post, got, diag, near, left, right,
    out,
    fetched, turned, acc, acc_turned, plan, sem,
):
    copy = pltpu.make_async_copy(draft, plan, sem)
    copy.start()
    ins = (r1, r2, r3, post, got)
    for rho in range(PEERS):
        message, index = place_in(rho)
        fetched[rho] = ins[message][index]
    fetched[DEAD] = jnp.zeros((RHS, B), BF16)
    acc[CL] = jnp.zeros((RHS, B), F32)
    for cluster in range(CL):
        acc[cluster] = dot_t(own[cluster], diag[cluster])
    copy.wait()
    forward_products(Blocks(plan, near, left, right), fetched, turned, acc, acc_turned)
    out[...] = acc[0:CL]


def image_second(partial, marked, r1, r2, r3, post, got, image, acc, sem):
    ins = (r1, r2, r3, post, got)
    places = [place_in(rho) for rho in range(PEERS)]
    marks = [marked[rho : rho + 1] for rho in range(PEERS)]
    copies = []
    for first in range(0, RHS, STRIP):
        rows = slice(first, first + STRIP)
        totals = [partial[cluster, rows] for cluster in range(CL)]
        for (message, index), mark in zip(places, marks):
            block = ins[message][index, rows].astype(F32)
            mark = jnp.broadcast_to(mark, (STRIP, B))
            for cluster in range(CL):
                totals[cluster] += jnp.where(mark == cluster, block, 0.0)
        for cluster in range(CL):
            acc[rows, cluster * B : (cluster + 1) * B] = totals[cluster]
        copies.append(pltpu.make_async_copy(acc.at[rows], image.at[rows], sem.at[first // STRIP]))
        copies[-1].start()
    for copy in copies:
        copy.wait()


SMEM = pl.BlockSpec(memory_space=pltpu.SMEM)
VMEM = pl.BlockSpec(memory_space=pltpu.VMEM)
ANY = pl.BlockSpec(memory_space=pl.ANY)
HBM = pl.BlockSpec(memory_space=pltpu.HBM)


def call(kernel, name, outs, out_specs, in_specs, scratch):
    return pl.pallas_call(
        kernel,
        name=name,
        out_shape=outs,
        in_specs=in_specs,
        out_specs=out_specs,
        scratch_shapes=scratch,
        compiler_params=pltpu.CompilerParams(vmem_limit_bytes=VMEM_BYTES),
        cost_estimate=pl.CostEstimate(flops=2 * 10**9, bytes_accessed=22 * 10**6, transcendentals=0),
    )


def shaped(shape, dtype):
    return jax.ShapeDtypeStruct(shape, dtype)


def message_shapes(rows, dtype):
    return [shaped((n, rows, B), dtype) for n in MESSAGE + (7,)]


def stage(source, target, sem):
    copy = pltpu.make_async_copy(source, target.at[0], sem)
    copy.start()
    copy.wait()


def staged(vectors):
    return call(stage, "staged", shaped((2, *vectors.shape), BF16), VMEM, [HBM], [pltpu.SemaphoreType.DMA])(vectors)


def k1(*args):
    held = [pltpu.VMEM(shape, BF16) for shape in ((SLOTS, B, B), (SLOTS, K, B), (SLOTS, K, B))]
    return call(
        back_first, "transposed_products",
        message_shapes(RHS + EXTRA, jnp.int16) + [shaped(PLAN, jnp.int32)] + held,
        [VMEM] * 8,
        [SMEM] + [HBM] * 5 + [VMEM] + [HBM] * 3,
        [
            pltpu.VMEM((CL + 1, RHS, B), BF16),
            pltpu.VMEM((PEERS + 1, RHS, B), F32),
            pltpu.VMEM((8, SLOTS), jnp.int32),
            pltpu.SMEM((1, 2), jnp.int32),
            pltpu.SMEM(PLAN, jnp.int32),
        ]
        + [pltpu.SemaphoreType.DMA((n,)) for n in (CHUNKS, CHUNKS, CHUNKS, 6)],
    )(*args)


def plan_scratch():
    return [pltpu.SMEM(PLAN, jnp.int32), pltpu.SemaphoreType.DMA]


def forward_scratch():
    return [
        pltpu.VMEM((PEERS + 1, RHS, B), BF16),
        pltpu.VMEM((PEERS + 1, B, RHS), BF16),
        pltpu.VMEM((CL + 1, RHS, B), F32),
        pltpu.VMEM((CL + 1, B, RHS), F32),
    ] + plan_scratch()


def k2(*args):
    return call(
        forward_first, "forward_products",
        shaped((CL, RHS, B), F32), VMEM,
        [VMEM] * 10,
        forward_scratch(),
    )(*args)


def k3(*args):
    return call(
        image_first, "first_image",
        [
            pltpu.VMEM((RHS, CL * B), F32),
            shaped((CL, RHS, B), BF16),
            shaped((16, B), jnp.int32),
        ]
        + message_shapes(RHS, BF16),
        [VMEM] * 7,
        [VMEM] * 6,
        [pltpu.VMEM((1, SLOTS), jnp.int32), pltpu.SMEM((1, SLOTS), jnp.int32), pltpu.SemaphoreType.DMA],
    )(*args)


def k4(*args):
    return call(
        back_second, "second_transposed_products",
        message_shapes(RHS, BF16),
        [VMEM] * 4,
        [VMEM] * 5,
        [pltpu.VMEM((CL + 1, RHS, B), BF16), pltpu.VMEM((PEERS + 1, RHS, B), F32)] + plan_scratch(),
    )(*args)


def k5(*args):
    return call(
        forward_second, "second_forward_products",
        shaped((CL, RHS, B), F32), VMEM,
        [VMEM] * 11,
        forward_scratch(),
    )(*args)


def k6(*args):
    return call(
        image_second, "second_image",
        shaped((RHS, CL * B), F32), HBM,
        [VMEM] * 7,
        [pltpu.VMEM((RHS, CL * B), F32), pltpu.SemaphoreType.DMA((RHS // STRIP,))],
    )(*args)


def carriers(size, k):
    pairs = []
    for chip in range(size // 2):
        for core in range(2):
            step = k if core == 0 else -k
            pairs.append((2 * chip + core, (2 * (chip + step) + core) % size))
    return pairs


def per_device(
    vectors, diag_blocks, near_blocks, near_rows, near_cols, far_left, far_right, far_rows, far_cols, counts
):
    size = lax.axis_size("rows")
    me = lax.axis_index("rows").reshape(1)

    def swap(block):
        return lax.ppermute(block, "rows", [(i, i ^ 1) for i in range(size)])

    def carry(block, k):
        return lax.ppermute(block, "rows", carriers(size, k))

    def carried(messages):
        second = carry(messages[1], 2)
        return [carry(messages[0], 1), second, carry(messages[2], 3)]

    def exchange(m1, m2, m3, give):
        got = swap(give)
        messages = []
        for k, message in enumerate((m1, m2, m3)):
            messages.append(lax.dynamic_update_slice(message, got[2 * k : 2 * k + 2], (1, 0, 0)))
        return carried(messages) + [got, messages]

    def passed_on(r1, r2, r3):
        return swap(jnp.concatenate([r1[2:4], r2[2:4], r3[2:3]]))

    def in_hbm(x):
        return pltpu.with_memory_space_constraint(x, pltpu.HBM)

    lists = [in_hbm(x.reshape(1, SLOTS)) for x in (near_rows, near_cols, far_rows, far_cols)]
    sib = swap(vectors)
    both = lax.dynamic_update_slice(staged(in_hbm(vectors)), sib[None], (1, 0, 0))
    halo = carried([both] * 3)
    m1, m2, m3, give, plan, *held = k1(
        me, *lists, in_hbm(counts), both, in_hbm(near_blocks), in_hbm(far_left), in_hbm(far_right)
    )
    halo, give = lax.optimization_barrier((halo, give))
    r1, r2, r3, got, messages = exchange(m1, m2, m3, give)
    halo, got = lax.optimization_barrier((halo, got))
    halo_post = swap(jnp.concatenate([halo[0], halo[1], halo[2][1:]]))
    halo_post, messages = lax.optimization_barrier((halo_post, messages))
    partial = k2(plan, both, *halo, halo_post, diag_blocks, *held)
    partial, r1, r2, r3 = lax.optimization_barrier((partial, r1, r2, r3))
    post = passed_on(r1, r2, r3)
    first_image, rounded, marked, m1, m2, m3, give = k3(partial, r1, r2, r3, post, got)
    f1, f2, f3, f_got, messages = exchange(m1, m2, m3, give)
    rounded, messages = lax.optimization_barrier((rounded, messages))
    m1, m2, m3, give = k4(plan, rounded, *held)
    f1, f2, f3, give = lax.optimization_barrier((f1, f2, f3, give))
    r1, r2, r3, got, messages = exchange(m1, m2, m3, give)
    f_post = passed_on(f1, f2, f3)
    f_post, messages = lax.optimization_barrier((f_post, messages))
    partial = k5(plan, rounded, f1, f2, f3, f_post, f_got, diag_blocks, *held)
    partial, r1, r2, r3 = lax.optimization_barrier((partial, r1, r2, r3))
    post = passed_on(r1, r2, r3)
    return first_image, k6(partial, marked, r1, r2, r3, post, got)


def solution(mesh):
    return jax.shard_map(
        per_device,
        mesh=mesh,
        in_specs=(
            P(None, "rows"),
            P("rows", None, None),
            P("rows", None, None),
            P("rows"),
            P("rows"),
            P("rows", None, None),
            P("rows", None, None),
            P("rows"),
            P("rows"),
            P("rows", None),
        ),
        out_specs=(P(None, "rows"), P(None, "rows")),
        check_vma=False,
    )
```

```python
import functools

import jax
import jax.numpy as jnp
from jax import lax
from jax.experimental import pallas as pl
from jax.experimental.pallas import tpu as pltpu
from jax.sharding import PartitionSpec as P

RHS, B, K = 64, 256, 32
CL, SLOTS, CHUNK = 4, 128, 16
CHUNKS = SLOTS // CHUNK
GROUP = B // K
HALF = B // 2
PEERS = 12
DEAD = 12
EXTRA = 16
LEVELS = 32766.0
TINY = 2.0**-100
LN2 = 0.6931471805599453
QUAD = 4
VMEM_BYTES = 16 * 2**20
F32, BF16 = jnp.float32, jnp.bfloat16


def dot(x, y):
    return lax.dot_general(x, y, (((1,), (0,)), ((), ())), preferred_element_type=F32)


def dot_t(x, y):
    return lax.dot_general(x, y, (((1,), (1,)), ((), ())), preferred_element_type=F32)


def peer_number(delta, core):
    kappa, other = delta // 2 - 3, delta % 2
    step = kappa * (1 - 2 * core)
    same = int(other != core)
    if step == 0:
        return 11 if same else DEAD
    if step < 0:
        return 2 * (-step - 1) + same
    return 6 + 2 * (step - 1) + same if step < 3 or not same else DEAD


PLAN = (4, 2 * SLOTS)
COUNTS, WANTED = 64, 80
STEP = 32
GROUPS = 4


class Blocks:
    def __init__(self, plan, near, left, right, sources=None):
        self.plan, self.near, self.left, self.right = plan, near, left, right
        self.sources = sources

    def copy(self, which, chunk):
        source, sem = self.sources[which]
        place = pl.ds(chunk * CHUNK, CHUNK)
        target = (self.near, self.left, self.right)[which]
        return pltpu.make_async_copy(source.at[place], target.at[place], sem.at[chunk])

    def start(self):
        for which in (1, 2, 0):
            self.copy(which, 0).start()

    def start_rest(self, near_chunks, far_chunks):
        def far_start(chunk, carry):
            self.copy(1, chunk).start()
            self.copy(2, chunk).start()
            return carry

        def near_start(chunk, carry):
            self.copy(0, chunk).start()
            return carry

        lax.fori_loop(1, far_chunks, far_start, 0)
        lax.fori_loop(1, near_chunks, near_start, 0)

    def far_loop(self, body):
        def arrived(chunk, carry):
            self.copy(1, chunk).wait()
            self.copy(2, chunk).wait()
            return carry

        if self.sources is not None:
            lax.fori_loop(0, self.plan[2, COUNTS + 1], arrived, 0)

        def step(index, carry):
            groups = []
            for part in range(GROUPS):
                first = index * GROUPS + part
                entries = [self.plan[1, first * GROUP + k] for k in range(GROUP)]
                slots = [entry & 255 for entry in entries]
                left = jnp.concatenate([self.left[slot] for slot in slots], axis=0)
                right = jnp.concatenate([self.right[slot] for slot in slots], axis=0)
                lane = lax.broadcasted_iota(jnp.int32, (1, B), 1) // K
                rows = jnp.zeros((1, B), jnp.int32)
                for k in range(GROUP):
                    rows = jnp.where(lane == k, entries[k] >> 8, rows)
                rows = jnp.broadcast_to(rows, (RHS, B))
                groups.append((left, right, rows, [self.plan[2, 2 * first + half] for half in (0, 1)]))
            body(groups)
            return carry

        lax.fori_loop(0, self.plan[2, COUNTS + 2], step, 0)

    def near_loop(self, body):
        size = STEP if self.sources is None else CHUNK

        def step(index, carry):
            if self.sources is not None:
                self.copy(0, index).wait()
            for part in range(size):
                slot = index * size + part
                code = self.plan[0, slot]
                body(part, code & 7, code >> 3, self.near[slot])
            return carry

        lax.fori_loop(0, self.plan[2, COUNTS] * (STEP // size), step, 0)


def halves(x, axis):
    return (x[:HALF], x[HALF:]) if axis == 0 else (x[:, :HALF], x[:, HALF:])


def back_products(blocks, own, acc):
    def far(groups):
        coefs = []
        for left, right, rows, partners in groups:
            every = dot_t(own[0:CL].reshape(CL * RHS, B), left)
            coef = jnp.zeros((RHS, B), F32)
            for cluster in range(CL):
                coef = jnp.where(rows == cluster, every[cluster * RHS : (cluster + 1) * RHS], coef)
            coefs.append(coef.astype(BF16))
        terms = []
        for coef, (left, right, rows, partners) in zip(coefs, groups):
            for part, block, partner in zip(halves(coef, 1), halves(right, 0), partners):
                terms.append((partner, dot(part, block)))
        for partner, term in terms:
            acc[partner] += term

    def near(part, row, partner, block):
        acc[partner] += dot(own[row], block)

    blocks.far_loop(far)
    blocks.near_loop(near)


def forward_products(blocks, fetched, turned, acc, acc_turned):
    turned[DEAD] = jnp.zeros((B, RHS), BF16)
    for partner in range(PEERS):
        turned[partner] = fetched[partner].T
    acc_turned[...] = jnp.zeros_like(acc_turned)

    def far(groups):
        spreads = []
        for left, right, rows, partners in groups:
            coef = [dot_t(fetched[partner], block) for partner, block in zip(partners, halves(right, 0))]
            coef = jnp.concatenate(coef, axis=1).astype(BF16).astype(F32)
            spread = [jnp.where(rows == cluster, coef, 0.0).astype(BF16) for cluster in range(CL)]
            spreads.append(jnp.concatenate(spread, axis=0))
        terms = [dot(spread, group[0]) for spread, group in zip(spreads, groups)]
        total = terms[0]
        for term in terms[1:]:
            total += term
        acc[0:CL] += total.reshape(CL, RHS, B)

    def near(part, row, partner, block):
        if part % 2 == 0:
            acc[row] += dot_t(fetched[partner], block)
        else:
            acc_turned[row] += dot(block, turned[partner])

    blocks.far_loop(far)
    blocks.near_loop(near)
    for cluster in range(CL):
        acc[cluster] += acc_turned[cluster].T


def make_plan(me, lists, few, draft):
    core = me % 2
    base = me - core - 6
    lane = lax.broadcasted_iota(jnp.int32, (1, SLOTS), 1)
    row16 = lax.broadcasted_iota(jnp.int32, (16, SLOTS), 0)
    kinds = []
    for kind in (0, 1):
        rows, cols = lists[2 * kind : 2 * kind + 1, :], lists[2 * kind + 1 : 2 * kind + 2, :]
        live = lane < few[0, kind]
        delta = ((cols >> 2) - base) & 15
        partner = jnp.full((1, SLOTS), DEAD, jnp.int32)
        for value in range(14):
            pair = [peer_number(value, a) for a in (0, 1)]
            partner = jnp.where(delta == value, jnp.where(core == 0, pair[0], pair[1]), partner)
        partner = jnp.where(live, partner, DEAD)
        kinds.append((jnp.where(live, rows & (CL - 1), CL), partner, cols & (CL - 1)))
    (near_row, near_rho, near_part), (far_row, far_rho, far_part) = kinds
    wide = lambda x: jnp.broadcast_to(x, (16, SLOTS))
    hot = row16 == wide(far_rho)
    wanted = jnp.maximum(
        jnp.where(row16 == wide(near_rho), wide(near_part).astype(F32), 0.0),
        jnp.where(hot, wide(far_part).astype(F32), 0.0),
    )
    wanted = jnp.max(wanted, axis=1, keepdims=True)
    hot = jnp.where(hot, 1.0, 0.0)
    square = (SLOTS, SLOTS)
    earlier = lax.broadcasted_iota(jnp.int32, square, 0) < lax.broadcasted_iota(jnp.int32, square, 1)
    rank = dot(hot.astype(BF16), jnp.where(earlier, 1.0, 0.0).astype(BF16)).astype(jnp.int32)
    number = wide(jnp.sum(hot, axis=1, keepdims=True)).astype(jnp.int32)
    padded = ((number + (QUAD - 1)) >> 2) << 2
    place = jnp.full((1, SLOTS), -1, jnp.int32)
    quad_rho = jnp.full((1, SLOTS), DEAD, jnp.int32)
    first = jnp.zeros((1, SLOTS), jnp.int32)
    for rho in range(PEERS):
        place = jnp.where(far_rho == rho, rank[rho : rho + 1] + first, place)
        last = first + padded[rho : rho + 1]
        quad_rho = jnp.where((lane * QUAD >= first) & (lane * QUAD < last), rho, quad_rho)
        first = last
    column = jnp.transpose(jnp.broadcast_to(place.astype(F32), square))
    spots = lax.broadcasted_iota(jnp.int32, square, 1).astype(F32)
    hits = jnp.concatenate([jnp.where(column == spots + shift, 1.0, 0.0).astype(BF16) for shift in (0.0, float(SLOTS))], axis=1)
    codes = jnp.where(row16 == 0, wide(lane), jnp.where(row16 == 1, wide(far_row), 1)).astype(F32).astype(BF16)
    found = dot(codes, hits)
    entry = jnp.where(found[2:3] > 0.5, found[0:1] + 256.0 * found[1:2], 256.0 * CL).astype(jnp.int32)
    wanted = jnp.sum(jnp.where(row16 + WANTED == wide(lane), wide(wanted), 0.0), axis=0, keepdims=True).astype(jnp.int32)
    draft[0:1, 0:SLOTS] = near_row + 8 * near_rho
    draft[1:2, :] = entry
    numbers = jnp.where(lane == COUNTS, (few[0, 0] + (STEP - 1)) // STEP, jnp.where(lane < COUNTS, quad_rho, wanted))
    numbers = jnp.where(lane == COUNTS + 1, (few[0, 1] + (CHUNK - 1)) // CHUNK, numbers)
    steps = (first + (2 * GROUPS * QUAD - 1)) >> (GROUPS.bit_length() + 2)
    draft[2:3, 0:SLOTS] = jnp.where(lane == COUNTS + 2, steps, numbers)


def place_out(rho):
    if rho == 11:
        return 3, 6
    if rho < 6:
        return 3, rho ^ 1
    k, same = divmod(rho - 6, 2)
    return k, 3 * same


def place_in(rho):
    if rho == 11:
        return 4, 6
    if rho < 6:
        return rho // 2, rho % 2
    return 3, rho - 6


MESSAGE = (4, 4, 3)


def back_first(
    me, near_rows, near_cols, far_rows, far_cols, counts, both, near, left, right,
    m1, m2, m3, give, draft, near_held, left_held, right_held,
    own, acc, lists, few, plan, near_sem, left_sem, right_sem, list_sem,
):
    blocks = Blocks(plan, near_held, left_held, right_held, ((near, near_sem), (left, left_sem), (right, right_sem)))
    copies = [pltpu.make_async_copy(counts, few, list_sem.at[4])]
    for index, source in enumerate((near_rows, near_cols, far_rows, far_cols)):
        copies.append(pltpu.make_async_copy(source, lists.at[pl.ds(index, 1)], list_sem.at[index]))
    for copy in copies:
        copy.start()
    blocks.start()
    for cluster in range(CL):
        own[cluster] = both[0, :, cluster * B : (cluster + 1) * B]
    own[CL] = jnp.zeros((RHS, B), BF16)
    draft[...] = jnp.zeros_like(draft)
    copies[0].wait()
    near_steps = (few[0, 0] + (STEP - 1)) // STEP
    blocks.start_rest(near_steps * (STEP // CHUNK), (few[0, 1] + (CHUNK - 1)) // CHUNK)
    for copy in copies[1:]:
        copy.wait()
    make_plan(me[0], lists, few, draft)
    copy = pltpu.make_async_copy(draft, plan, list_sem.at[5])
    copy.start()
    acc[...] = jnp.zeros_like(acc)
    copy.wait()
    back_products(blocks, own, acc)
    outs = (m1, m2, m3, give)
    for rho in range(PEERS):
        message, index = place_out(rho)
        outs[message][index, 0:RHS], power = coded(acc[rho])
        half = lax.broadcasted_iota(jnp.int32, (EXTRA, B), 0) < EXTRA // 2
        outs[message][index, RHS:] = jnp.where(half, power, plan[2, WANTED + rho]).astype(jnp.int16)


def forward_first(
    draft, both, h1, h2, h3, post, diag, near, left, right,
    out,
    fetched, turned, acc, acc_turned, plan, sem,
):
    copy = pltpu.make_async_copy(draft, plan, sem)
    copy.start()
    fetched[DEAD] = jnp.zeros((RHS, B), BF16)
    acc[CL] = jnp.zeros((RHS, B), F32)
    for cluster in range(CL):
        acc[cluster] = dot_t(both[0, :, cluster * B : (cluster + 1) * B], diag[cluster])
    copy.wait()
    halo = (h1, h2, h3)
    for rho in range(PEERS):
        lanes = pl.ds(pl.multiple_of(plan[2, WANTED + rho] * B, B), B)
        if rho == 11:
            fetched[rho] = both[1, :, lanes]
        elif rho < 6:
            fetched[rho] = halo[rho // 2][rho % 2, :, lanes]
        else:
            k, same = divmod(rho - 6, 2)
            fetched[rho] = post[2 * k + (1 - same if k < 2 else 0), :, lanes]
    forward_products(Blocks(plan, near, left, right), fetched, turned, acc, acc_turned)
    out[...] = acc[0:CL]


STRIP = 16


def coded(block):
    top = jnp.maximum(jnp.max(jnp.abs(block), axis=0, keepdims=True), TINY)
    power = jnp.ceil(jnp.log(top * (1.0 / LEVELS)) * (1.0 / LN2) + 1e-3)
    scaled = block * jnp.exp(power * -LN2)
    return jnp.floor(scaled + 0.5).astype(jnp.int32).astype(jnp.int16), power.astype(jnp.int32)


def image_first(
    partial, r1, r2, r3, post, got,
    image, rounded, marked, m1, m2, m3, give,
    draft, wanted, sem,
):
    ins = (r1, r2, r3, post, got)
    places = [place_in(rho) for rho in range(PEERS)]
    extras = [ins[message][index, RHS:].astype(jnp.int32) for message, index in places]
    units = [jnp.exp(extra[0:1].astype(F32) * LN2) for extra in extras]
    marks = [extra[EXTRA // 2 : EXTRA // 2 + 1] for extra in extras]
    lane = lax.broadcasted_iota(jnp.int32, (1, SLOTS), 1)
    packed = jnp.zeros((1, SLOTS), jnp.int32)
    for rho, mark in enumerate(marks):
        packed = jnp.where(lane == rho, mark[:, 0:SLOTS], packed)
        marked[rho : rho + 1] = mark
    draft[...] = packed
    copy = pltpu.make_async_copy(draft, wanted, sem)
    copy.start()
    for first in range(0, RHS, STRIP):
        rows = slice(first, first + STRIP)
        totals = [partial[cluster, rows] for cluster in range(CL)]
        for (message, index), mark, unit in zip(places, marks, units):
            block = ins[message][index, rows].astype(jnp.int32).astype(F32) * unit
            mark = jnp.broadcast_to(mark, (STRIP, B))
            for cluster in range(CL):
                totals[cluster] += jnp.where(mark == cluster, block, 0.0)
        for cluster in range(CL):
            image[rows, cluster * B : (cluster + 1) * B] = totals[cluster]
            rounded[cluster, rows] = totals[cluster].astype(BF16)
    copy.wait()
    outs = (m1, m2, m3, give)
    for rho in range(PEERS):
        message, index = place_out(rho)
        outs[message][index] = rounded[wanted[0, rho]]


def back_second(
    draft, rounded, near, left, right,
    m1, m2, m3, give,
    own, acc, plan, sem,
):
    copy = pltpu.make_async_copy(draft, plan, sem)
    copy.start()
    own[0:CL] = rounded[...]
    own[CL] = jnp.zeros((RHS, B), BF16)
    acc[...] = jnp.zeros_like(acc)
    copy.wait()
    back_products(Blocks(plan, near, left, right), own, acc)
    outs = (m1, m2, m3, give)
    for rho in range(PEERS):
        message, index = place_out(rho)
        outs[message][index] = acc[rho].astype(BF16)


def forward_second(
    draft, own, r1, r2, r3, post, got, diag, near, left, right,
    out,
    fetched, turned, acc, acc_turned, plan, sem,
):
    copy = pltpu.make_async_copy(draft, plan, sem)
    copy.start()
    ins = (r1, r2, r3, post, got)
    for rho in range(PEERS):
        message, index = place_in(rho)
        fetched[rho] = ins[message][index]
    fetched[DEAD] = jnp.zeros((RHS, B), BF16)
    acc[CL] = jnp.zeros((RHS, B), F32)
    for cluster in range(CL):
        acc[cluster] = dot_t(own[cluster], diag[cluster])
    copy.wait()
    forward_products(Blocks(plan, near, left, right), fetched, turned, acc, acc_turned)
    out[...] = acc[0:CL]


def image_second(partial, marked, r1, r2, r3, post, got, image, acc, sem):
    ins = (r1, r2, r3, post, got)
    places = [place_in(rho) for rho in range(PEERS)]
    marks = [marked[rho : rho + 1] for rho in range(PEERS)]
    copies = []
    for first in range(0, RHS, STRIP):
        rows = slice(first, first + STRIP)
        totals = [partial[cluster, rows] for cluster in range(CL)]
        for (message, index), mark in zip(places, marks):
            block = ins[message][index, rows].astype(F32)
            mark = jnp.broadcast_to(mark, (STRIP, B))
            for cluster in range(CL):
                totals[cluster] += jnp.where(mark == cluster, block, 0.0)
        for cluster in range(CL):
            acc[rows, cluster * B : (cluster + 1) * B] = totals[cluster]
        copies.append(pltpu.make_async_copy(acc.at[rows], image.at[rows], sem.at[first // STRIP]))
        copies[-1].start()
    for copy in copies:
        copy.wait()


SMEM = pl.BlockSpec(memory_space=pltpu.SMEM)
VMEM = pl.BlockSpec(memory_space=pltpu.VMEM)
ANY = pl.BlockSpec(memory_space=pl.ANY)
HBM = pl.BlockSpec(memory_space=pltpu.HBM)


def call(kernel, name, outs, out_specs, in_specs, scratch):
    return pl.pallas_call(
        kernel,
        name=name,
        out_shape=outs,
        in_specs=in_specs,
        out_specs=out_specs,
        scratch_shapes=scratch,
        compiler_params=pltpu.CompilerParams(vmem_limit_bytes=VMEM_BYTES),
        cost_estimate=pl.CostEstimate(flops=2 * 10**9, bytes_accessed=22 * 10**6, transcendentals=0),
    )


def shaped(shape, dtype):
    return jax.ShapeDtypeStruct(shape, dtype)


def message_shapes(rows, dtype, given=7):
    return [shaped((n, rows, B), dtype) for n in MESSAGE + (given,)]


def stage(source, target, sem):
    copy = pltpu.make_async_copy(source, target.at[0], sem)
    copy.start()
    copy.wait()


def staged(vectors):
    return call(stage, "staged", shaped((2, *vectors.shape), BF16), VMEM, [HBM], [pltpu.SemaphoreType.DMA])(vectors)


def k1(*args):
    held = [pltpu.VMEM(shape, BF16) for shape in ((SLOTS, B, B), (SLOTS, K, B), (SLOTS, K, B))]
    return call(
        back_first, "transposed_products",
        message_shapes(RHS + EXTRA, jnp.int16, 11) + [shaped(PLAN, jnp.int32)] + held,
        [VMEM] * 8,
        [SMEM] + [HBM] * 5 + [VMEM] + [HBM] * 3,
        [
            pltpu.VMEM((CL + 1, RHS, B), BF16),
            pltpu.VMEM((PEERS + 1, RHS, B), F32),
            pltpu.VMEM((8, SLOTS), jnp.int32),
            pltpu.SMEM((1, 2), jnp.int32),
            pltpu.SMEM(PLAN, jnp.int32),
        ]
        + [pltpu.SemaphoreType.DMA((n,)) for n in (CHUNKS, CHUNKS, CHUNKS, 6)],
    )(*args)


def plan_scratch():
    return [pltpu.SMEM(PLAN, jnp.int32), pltpu.SemaphoreType.DMA]


def forward_scratch():
    return [
        pltpu.VMEM((PEERS + 1, RHS, B), BF16),
        pltpu.VMEM((PEERS + 1, B, RHS), BF16),
        pltpu.VMEM((CL + 1, RHS, B), F32),
        pltpu.VMEM((CL + 1, B, RHS), F32),
    ] + plan_scratch()


def k2(*args):
    return call(
        forward_first, "forward_products",
        shaped((CL, RHS, B), F32), VMEM,
        [VMEM] * 10,
        forward_scratch(),
    )(*args)


def k3(*args):
    return call(
        image_first, "first_image",
        [
            pltpu.VMEM((RHS, CL * B), F32),
            shaped((CL, RHS, B), BF16),
            shaped((16, B), jnp.int32),
        ]
        + message_shapes(RHS, BF16),
        [VMEM] * 7,
        [VMEM] * 6,
        [pltpu.VMEM((1, SLOTS), jnp.int32), pltpu.SMEM((1, SLOTS), jnp.int32), pltpu.SemaphoreType.DMA],
    )(*args)


def k4(*args):
    return call(
        back_second, "second_transposed_products",
        message_shapes(RHS, BF16),
        [VMEM] * 4,
        [VMEM] * 5,
        [pltpu.VMEM((CL + 1, RHS, B), BF16), pltpu.VMEM((PEERS + 1, RHS, B), F32)] + plan_scratch(),
    )(*args)


def k5(*args):
    return call(
        forward_second, "second_forward_products",
        shaped((CL, RHS, B), F32), VMEM,
        [VMEM] * 11,
        forward_scratch(),
    )(*args)


def k6(*args):
    return call(
        image_second, "second_image",
        shaped((RHS, CL * B), F32), HBM,
        [VMEM] * 7,
        [pltpu.VMEM((RHS, CL * B), F32), pltpu.SemaphoreType.DMA((RHS // STRIP,))],
    )(*args)


def carriers(size, k):
    pairs = []
    for chip in range(size // 2):
        for core in range(2):
            step = k if core == 0 else -k
            pairs.append((2 * chip + core, (2 * (chip + step) + core) % size))
    return pairs


def per_device(
    vectors, diag_blocks, near_blocks, near_rows, near_cols, far_left, far_right, far_rows, far_cols, counts
):
    size = lax.axis_size("rows")
    me = lax.axis_index("rows").reshape(1)

    def swap(block):
        return lax.ppermute(block, "rows", [(i, i ^ 1) for i in range(size)])

    def carry(block, k):
        return lax.ppermute(block, "rows", carriers(size, k))

    def carried(messages):
        second = carry(messages[1], 2)
        return [carry(messages[0], 1), second, carry(messages[2], 3)]

    def exchange(m1, m2, m3, give):
        got = swap(give)
        messages = []
        for k, message in enumerate((m1, m2, m3)):
            messages.append(lax.dynamic_update_slice(message, got[2 * k : 2 * k + 2], (1, 0, 0)))
        return carried(messages) + [got, messages]

    def passed_on(r1, r2, r3):
        return swap(jnp.concatenate([r1[2:4], r2[2:4], r3[2:3]]))

    def in_hbm(x):
        return pltpu.with_memory_space_constraint(x, pltpu.HBM)

    lists = [in_hbm(x.reshape(1, SLOTS)) for x in (near_rows, near_cols, far_rows, far_cols)]
    sib = swap(vectors)
    both = lax.dynamic_update_slice(staged(in_hbm(vectors)), sib[None], (1, 0, 0))
    halo = carried([both] * 3)
    m1, m2, m3, give, plan, *held = k1(
        me, *lists, in_hbm(counts), both, in_hbm(near_blocks), in_hbm(far_left), in_hbm(far_right)
    )
    halo, m1 = lax.optimization_barrier((halo, m1))
    r1, r2, r3, got, messages = exchange(m1, m2, m3, give)
    halo_post = swap(jnp.concatenate([halo[0], halo[1], halo[2][1:]]))
    halo_post, messages = lax.optimization_barrier((halo_post, messages))
    partial = k2(plan, both, *halo, halo_post, diag_blocks, *held)
    partial, r1, r2, r3 = lax.optimization_barrier((partial, r1, r2, r3))
    post = passed_on(r1, r2, r3)
    first_image, rounded, marked, m1, m2, m3, give = k3(partial, r1, r2, r3, post, got)
    f1, f2, f3, f_got, messages = exchange(m1, m2, m3, give)
    rounded, messages = lax.optimization_barrier((rounded, messages))
    m1, m2, m3, give = k4(plan, rounded, *held)
    f1, f2, f3, give = lax.optimization_barrier((f1, f2, f3, give))
    r1, r2, r3, got, messages = exchange(m1, m2, m3, give)
    f_post = passed_on(f1, f2, f3)
    f_post, messages = lax.optimization_barrier((f_post, messages))
    partial = k5(plan, rounded, f1, f2, f3, f_post, f_got, diag_blocks, *held)
    partial, r1, r2, r3 = lax.optimization_barrier((partial, r1, r2, r3))
    post = passed_on(r1, r2, r3)
    return first_image, k6(partial, marked, r1, r2, r3, post, got)


def solution(mesh):
    return jax.shard_map(
        per_device,
        mesh=mesh,
        in_specs=(
            P(None, "rows"),
            P("rows", None, None),
            P("rows", None, None),
            P("rows"),
            P("rows"),
            P("rows", None, None),
            P("rows", None, None),
            P("rows"),
            P("rows"),
            P("rows", None),
        ),
        out_specs=(P(None, "rows"), P(None, "rows")),
        check_vma=False,
    )
```

```python
import functools

import jax
import jax.numpy as jnp
from jax import lax
from jax.experimental import pallas as pl
from jax.experimental.pallas import tpu as pltpu
from jax.sharding import PartitionSpec as P

RHS, B, K = 64, 256, 32
CL, SLOTS, CHUNK = 4, 128, 16
CHUNKS = SLOTS // CHUNK
GROUP = B // K
HALF = B // 2
PEERS = 12
DEAD = 12
EXTRA = 16
LEVELS = 32766.0
TINY = 2.0**-100
LN2 = 0.6931471805599453
QUAD = 4
VMEM_BYTES = 16 * 2**20
F32, BF16 = jnp.float32, jnp.bfloat16


def dot(x, y):
    return lax.dot_general(x, y, (((1,), (0,)), ((), ())), preferred_element_type=F32)


def dot_t(x, y):
    return lax.dot_general(x, y, (((1,), (1,)), ((), ())), preferred_element_type=F32)


def peer_number(delta, core):
    kappa, other = delta // 2 - 3, delta % 2
    step = kappa * (1 - 2 * core)
    same = int(other != core)
    if step == 0:
        return 11 if same else DEAD
    if step < 0:
        return 2 * (-step - 1) + same
    return 6 + 2 * (step - 1) + same if step < 3 or not same else DEAD


PLAN = (4, 2 * SLOTS)
COUNTS, WANTED = 64, 80
STEP = 32
GROUPS = 4


class Blocks:
    def __init__(self, plan, near, left, right, sources=None):
        self.plan, self.near, self.left, self.right = plan, near, left, right
        self.sources = sources

    def copy(self, which, chunk):
        source, sem = self.sources[which]
        place = pl.ds(chunk * CHUNK, CHUNK)
        target = (self.near, self.left, self.right)[which]
        return pltpu.make_async_copy(source.at[place], target.at[place], sem.at[chunk])

    def start(self):
        for which in (1, 2, 0):
            self.copy(which, 0).start()

    def start_rest(self, near_chunks, far_chunks):
        def far_start(chunk, carry):
            self.copy(1, chunk).start()
            self.copy(2, chunk).start()
            return carry

        def near_start(chunk, carry):
            self.copy(0, chunk).start()
            return carry

        lax.fori_loop(1, far_chunks, far_start, 0)
        lax.fori_loop(1, near_chunks, near_start, 0)

    def far_loop(self, body):
        def arrived(chunk, carry):
            self.copy(1, chunk).wait()
            self.copy(2, chunk).wait()
            return carry

        if self.sources is not None:
            lax.fori_loop(0, self.plan[2, COUNTS + 1], arrived, 0)

        def step(index, carry):
            groups = []
            for part in range(GROUPS):
                first = index * GROUPS + part
                entries = [self.plan[1, first * GROUP + k] for k in range(GROUP)]
                slots = [entry & 255 for entry in entries]
                left = jnp.concatenate([self.left[slot] for slot in slots], axis=0)
                right = jnp.concatenate([self.right[slot] for slot in slots], axis=0)
                lane = lax.broadcasted_iota(jnp.int32, (1, B), 1) // K
                rows = jnp.zeros((1, B), jnp.int32)
                for k in range(GROUP):
                    rows = jnp.where(lane == k, entries[k] >> 8, rows)
                rows = jnp.broadcast_to(rows, (RHS, B))
                groups.append((left, right, rows, [self.plan[2, 2 * first + half] for half in (0, 1)]))
            body(groups)
            return carry

        lax.fori_loop(0, self.plan[2, COUNTS + 2], step, 0)

    def near_loop(self, body):
        size = STEP if self.sources is None else CHUNK

        def step(index, carry):
            if self.sources is not None:
                self.copy(0, index).wait()
            for part in range(size):
                slot = index * size + part
                code = self.plan[0, slot]
                body(part, code & 7, code >> 3, self.near[slot])
            return carry

        lax.fori_loop(0, self.plan[2, COUNTS] * (STEP // size), step, 0)


def halves(x, axis):
    return (x[:HALF], x[HALF:]) if axis == 0 else (x[:, :HALF], x[:, HALF:])


def back_products(blocks, own, acc):
    def far(groups):
        coefs = []
        for left, right, rows, partners in groups:
            every = dot_t(own[0:CL].reshape(CL * RHS, B), left)
            coef = jnp.zeros((RHS, B), F32)
            for cluster in range(CL):
                coef = jnp.where(rows == cluster, every[cluster * RHS : (cluster + 1) * RHS], coef)
            coefs.append(coef.astype(BF16))
        terms = []
        for coef, (left, right, rows, partners) in zip(coefs, groups):
            for part, block, partner in zip(halves(coef, 1), halves(right, 0), partners):
                terms.append((partner, dot(part, block)))
        for partner, term in terms:
            acc[partner] += term

    def near(part, row, partner, block):
        acc[partner] += dot(own[row], block)

    blocks.far_loop(far)
    blocks.near_loop(near)


def forward_products(blocks, fetched, turned, acc, acc_turned):
    turned[DEAD] = jnp.zeros((B, RHS), BF16)
    for partner in range(PEERS):
        turned[partner] = fetched[partner].T
    acc_turned[...] = jnp.zeros_like(acc_turned)

    def far(groups):
        spreads = []
        for left, right, rows, partners in groups:
            coef = [dot_t(fetched[partner], block) for partner, block in zip(partners, halves(right, 0))]
            coef = jnp.concatenate(coef, axis=1).astype(BF16).astype(F32)
            spread = [jnp.where(rows == cluster, coef, 0.0).astype(BF16) for cluster in range(CL)]
            spreads.append(jnp.concatenate(spread, axis=0))
        terms = [dot(spread, group[0]) for spread, group in zip(spreads, groups)]
        total = terms[0]
        for term in terms[1:]:
            total += term
        acc[0:CL] += total.reshape(CL, RHS, B)

    def near(part, row, partner, block):
        if part % 2 == 0:
            acc[row] += dot_t(fetched[partner], block)
        else:
            acc_turned[row] += dot(block, turned[partner])

    blocks.far_loop(far)
    blocks.near_loop(near)
    for cluster in range(CL):
        acc[cluster] += acc_turned[cluster].T


def make_plan(me, lists, few, draft):
    core = me % 2
    base = me - core - 6
    lane = lax.broadcasted_iota(jnp.int32, (1, SLOTS), 1)
    row16 = lax.broadcasted_iota(jnp.int32, (16, SLOTS), 0)
    kinds = []
    for kind in (0, 1):
        rows, cols = lists[2 * kind : 2 * kind + 1, :], lists[2 * kind + 1 : 2 * kind + 2, :]
        live = lane < few[0, kind]
        delta = ((cols >> 2) - base) & 15
        partner = jnp.full((1, SLOTS), DEAD, jnp.int32)
        for value in range(14):
            pair = [peer_number(value, a) for a in (0, 1)]
            partner = jnp.where(delta == value, jnp.where(core == 0, pair[0], pair[1]), partner)
        partner = jnp.where(live, partner, DEAD)
        kinds.append((jnp.where(live, rows & (CL - 1), CL), partner, cols & (CL - 1)))
    (near_row, near_rho, near_part), (far_row, far_rho, far_part) = kinds
    wide = lambda x: jnp.broadcast_to(x, (16, SLOTS))
    hot = row16 == wide(far_rho)
    wanted = jnp.maximum(
        jnp.where(row16 == wide(near_rho), wide(near_part).astype(F32), 0.0),
        jnp.where(hot, wide(far_part).astype(F32), 0.0),
    )
    wanted = jnp.max(wanted, axis=1, keepdims=True)
    hot = jnp.where(hot, 1.0, 0.0)
    square = (SLOTS, SLOTS)
    earlier = lax.broadcasted_iota(jnp.int32, square, 0) < lax.broadcasted_iota(jnp.int32, square, 1)
    rank = dot(hot.astype(BF16), jnp.where(earlier, 1.0, 0.0).astype(BF16)).astype(jnp.int32)
    number = wide(jnp.sum(hot, axis=1, keepdims=True)).astype(jnp.int32)
    padded = ((number + (QUAD - 1)) >> 2) << 2
    place = jnp.full((1, SLOTS), -1, jnp.int32)
    quad_rho = jnp.full((1, SLOTS), DEAD, jnp.int32)
    first = jnp.zeros((1, SLOTS), jnp.int32)
    for rho in range(PEERS):
        place = jnp.where(far_rho == rho, rank[rho : rho + 1] + first, place)
        last = first + padded[rho : rho + 1]
        quad_rho = jnp.where((lane * QUAD >= first) & (lane * QUAD < last), rho, quad_rho)
        first = last
    column = jnp.transpose(jnp.broadcast_to(place.astype(F32), square))
    spots = lax.broadcasted_iota(jnp.int32, square, 1).astype(F32)
    hits = jnp.concatenate([jnp.where(column == spots + shift, 1.0, 0.0).astype(BF16) for shift in (0.0, float(SLOTS))], axis=1)
    codes = jnp.where(row16 == 0, wide(lane), jnp.where(row16 == 1, wide(far_row), 1)).astype(F32).astype(BF16)
    found = dot(codes, hits)
    entry = jnp.where(found[2:3] > 0.5, found[0:1] + 256.0 * found[1:2], 256.0 * CL).astype(jnp.int32)
    wanted = jnp.sum(jnp.where(row16 + WANTED == wide(lane), wide(wanted), 0.0), axis=0, keepdims=True).astype(jnp.int32)
    draft[0:1, 0:SLOTS] = near_row + 8 * near_rho
    draft[1:2, :] = entry
    numbers = jnp.where(lane == COUNTS, (few[0, 0] + (STEP - 1)) // STEP, jnp.where(lane < COUNTS, quad_rho, wanted))
    numbers = jnp.where(lane == COUNTS + 1, (few[0, 1] + (CHUNK - 1)) // CHUNK, numbers)
    steps = (first + (2 * GROUPS * QUAD - 1)) >> (GROUPS.bit_length() + 2)
    draft[2:3, 0:SLOTS] = jnp.where(lane == COUNTS + 2, steps, numbers)


def place_out(rho):
    if rho == 11:
        return 3, 6
    if rho < 6:
        return 3, rho ^ 1
    k, same = divmod(rho - 6, 2)
    return k, 3 * same


def place_in(rho):
    if rho == 11:
        return 4, 6
    if rho < 6:
        return rho // 2, rho % 2
    return 3, rho - 6


def back_first(
    me, near_rows, near_cols, far_rows, far_cols, counts, both, near, left, right,
    m1, m2, m3, give, draft, near_held, left_held, right_held,
    own, acc, lists, few, plan, near_sem, left_sem, right_sem, list_sem,
):
    blocks = Blocks(plan, near_held, left_held, right_held, ((near, near_sem), (left, left_sem), (right, right_sem)))
    copies = [pltpu.make_async_copy(counts, few, list_sem.at[4])]
    for index, source in enumerate((near_rows, near_cols, far_rows, far_cols)):
        copies.append(pltpu.make_async_copy(source, lists.at[pl.ds(index, 1)], list_sem.at[index]))
    for copy in copies:
        copy.start()
    blocks.start()
    for cluster in range(CL):
        own[cluster] = both[0, :, cluster * B : (cluster + 1) * B]
    own[CL] = jnp.zeros((RHS, B), BF16)
    draft[...] = jnp.zeros_like(draft)
    copies[0].wait()
    near_steps = (few[0, 0] + (STEP - 1)) // STEP
    blocks.start_rest(near_steps * (STEP // CHUNK), (few[0, 1] + (CHUNK - 1)) // CHUNK)
    for copy in copies[1:]:
        copy.wait()
    make_plan(me[0], lists, few, draft)
    copy = pltpu.make_async_copy(draft, plan, list_sem.at[5])
    copy.start()
    acc[...] = jnp.zeros_like(acc)
    copy.wait()
    back_products(blocks, own, acc)
    outs = (m1, m2, m3, give)
    for rho in range(PEERS):
        message, index = place_out(rho)
        outs[message][index, 0:RHS], power = coded(acc[rho])
        half = lax.broadcasted_iota(jnp.int32, (EXTRA, B), 0) < EXTRA // 2
        outs[message][index, RHS:] = jnp.where(half, power, plan[2, WANTED + rho]).astype(jnp.int16)


def forward_first(
    draft, both, h1, h2, h3, post, diag, near, left, right,
    out,
    fetched, turned, acc, acc_turned, plan, sem,
):
    copy = pltpu.make_async_copy(draft, plan, sem)
    copy.start()
    fetched[DEAD] = jnp.zeros((RHS, B), BF16)
    acc[CL] = jnp.zeros((RHS, B), F32)
    for cluster in range(CL):
        acc[cluster] = dot_t(both[0, :, cluster * B : (cluster + 1) * B], diag[cluster])
    copy.wait()
    halo = (h1, h2, h3)
    for rho in range(PEERS):
        lanes = pl.ds(pl.multiple_of(plan[2, WANTED + rho] * B, B), B)
        if rho == 11:
            fetched[rho] = both[1, :, lanes]
        elif rho < 6:
            fetched[rho] = halo[rho // 2][rho % 2, :, lanes]
        else:
            k, same = divmod(rho - 6, 2)
            fetched[rho] = post[2 * k + (1 - same if k < 2 else 0), :, lanes]
    forward_products(Blocks(plan, near, left, right), fetched, turned, acc, acc_turned)
    out[...] = acc[0:CL]


STRIP = 16


def coded(block):
    top = jnp.maximum(jnp.max(jnp.abs(block), axis=0, keepdims=True), TINY)
    power = jnp.ceil(jnp.log(top * (1.0 / LEVELS)) * (1.0 / LN2) + 1e-3)
    scaled = block * jnp.exp(power * -LN2)
    return jnp.floor(scaled + 0.5).astype(jnp.int32).astype(jnp.int16), power.astype(jnp.int32)


def image_first(
    partial, r1, r2, r3, post, got,
    image, rounded, marked, m1, m2, m3, give,
    draft, wanted, sem,
):
    ins = (r1, r2, r3, post, got)
    places = [place_in(rho) for rho in range(PEERS)]
    extras = [ins[message][index, RHS:].astype(jnp.int32) for message, index in places]
    units = [jnp.exp(extra[0:1].astype(F32) * LN2) for extra in extras]
    marks = [extra[EXTRA // 2 : EXTRA // 2 + 1] for extra in extras]
    lane = lax.broadcasted_iota(jnp.int32, (1, SLOTS), 1)
    packed = jnp.zeros((1, SLOTS), jnp.int32)
    for rho, mark in enumerate(marks):
        packed = jnp.where(lane == rho, mark[:, 0:SLOTS], packed)
        marked[rho : rho + 1] = mark
    draft[...] = packed
    copy = pltpu.make_async_copy(draft, wanted, sem)
    copy.start()
    for first in range(0, RHS, STRIP):
        rows = slice(first, first + STRIP)
        totals = [partial[cluster, rows] for cluster in range(CL)]
        for (message, index), mark, unit in zip(places, marks, units):
            block = ins[message][index, rows].astype(jnp.int32).astype(F32) * unit
            mark = jnp.broadcast_to(mark, (STRIP, B))
            for cluster in range(CL):
                totals[cluster] += jnp.where(mark == cluster, block, 0.0)
        for cluster in range(CL):
            image[rows, cluster * B : (cluster + 1) * B] = totals[cluster]
            rounded[cluster, rows] = totals[cluster].astype(BF16)
    copy.wait()
    outs = (m1, m2, m3, give)
    for rho in range(PEERS):
        message, index = place_out(rho)
        outs[message][index] = rounded[wanted[0, rho]]


def back_second(
    draft, rounded, near, left, right,
    m1, m2, m3, give,
    own, acc, plan, sem,
):
    copy = pltpu.make_async_copy(draft, plan, sem)
    copy.start()
    own[0:CL] = rounded[...]
    own[CL] = jnp.zeros((RHS, B), BF16)
    acc[...] = jnp.zeros_like(acc)
    copy.wait()
    back_products(Blocks(plan, near, left, right), own, acc)
    outs = (m1, m2, m3, give)
    for rho in range(PEERS):
        message, index = place_out(rho)
        outs[message][index] = acc[rho].astype(BF16)


def forward_second(
    draft, own, r1, r2, r3, post, got, diag, near, left, right,
    out,
    fetched, turned, acc, acc_turned, plan, sem,
):
    copy = pltpu.make_async_copy(draft, plan, sem)
    copy.start()
    ins = (r1, r2, r3, post, got)
    for rho in range(PEERS):
        message, index = place_in(rho)
        fetched[rho] = ins[message][index]
    fetched[DEAD] = jnp.zeros((RHS, B), BF16)
    acc[CL] = jnp.zeros((RHS, B), F32)
    for cluster in range(CL):
        acc[cluster] = dot_t(own[cluster], diag[cluster])
    copy.wait()
    forward_products(Blocks(plan, near, left, right), fetched, turned, acc, acc_turned)
    out[...] = acc[0:CL]


def image_second(partial, marked, r1, r2, r3, post, got, image, acc, sem):
    ins = (r1, r2, r3, post, got)
    places = [place_in(rho) for rho in range(PEERS)]
    marks = [marked[rho : rho + 1] for rho in range(PEERS)]
    copies = []
    for first in range(0, RHS, STRIP):
        rows = slice(first, first + STRIP)
        totals = [partial[cluster, rows] for cluster in range(CL)]
        for (message, index), mark in zip(places, marks):
            block = ins[message][index, rows].astype(F32)
            mark = jnp.broadcast_to(mark, (STRIP, B))
            for cluster in range(CL):
                totals[cluster] += jnp.where(mark == cluster, block, 0.0)
        for cluster in range(CL):
            acc[rows, cluster * B : (cluster + 1) * B] = totals[cluster]
        copies.append(pltpu.make_async_copy(acc.at[rows], image.at[rows], sem.at[first // STRIP]))
        copies[-1].start()
    for copy in copies:
        copy.wait()


SMEM = pl.BlockSpec(memory_space=pltpu.SMEM)
VMEM = pl.BlockSpec(memory_space=pltpu.VMEM)
ANY = pl.BlockSpec(memory_space=pl.ANY)
HBM = pl.BlockSpec(memory_space=pltpu.HBM)


def call(kernel, name, outs, out_specs, in_specs, scratch):
    return pl.pallas_call(
        kernel,
        name=name,
        out_shape=outs,
        in_specs=in_specs,
        out_specs=out_specs,
        scratch_shapes=scratch,
        compiler_params=pltpu.CompilerParams(vmem_limit_bytes=VMEM_BYTES),
        cost_estimate=pl.CostEstimate(flops=2 * 10**9, bytes_accessed=22 * 10**6, transcendentals=0),
    )


def shaped(shape, dtype):
    return jax.ShapeDtypeStruct(shape, dtype)


def message_shapes(rows, dtype, given=7, third=3):
    return [shaped((n, rows, B), dtype) for n in (4, 4, third, given)]


def stage(source, target, sem):
    copy = pltpu.make_async_copy(source, target.at[0], sem)
    copy.start()
    copy.wait()


def staged(vectors):
    return call(stage, "staged", shaped((2, *vectors.shape), BF16), VMEM, [HBM], [pltpu.SemaphoreType.DMA])(vectors)


def k1(*args):
    held = [pltpu.VMEM(shape, BF16) for shape in ((SLOTS, B, B), (SLOTS, K, B), (SLOTS, K, B))]
    return call(
        back_first, "transposed_products",
        message_shapes(RHS + EXTRA, jnp.int16, 11) + [shaped(PLAN, jnp.int32)] + held,
        [VMEM] * 8,
        [SMEM] + [HBM] * 5 + [VMEM] + [HBM] * 3,
        [
            pltpu.VMEM((CL + 1, RHS, B), BF16),
            pltpu.VMEM((PEERS + 1, RHS, B), F32),
            pltpu.VMEM((8, SLOTS), jnp.int32),
            pltpu.SMEM((1, 2), jnp.int32),
            pltpu.SMEM(PLAN, jnp.int32),
        ]
        + [pltpu.SemaphoreType.DMA((n,)) for n in (CHUNKS, CHUNKS, CHUNKS, 6)],
    )(*args)


def plan_scratch():
    return [pltpu.SMEM(PLAN, jnp.int32), pltpu.SemaphoreType.DMA]


def forward_scratch():
    return [
        pltpu.VMEM((PEERS + 1, RHS, B), BF16),
        pltpu.VMEM((PEERS + 1, B, RHS), BF16),
        pltpu.VMEM((CL + 1, RHS, B), F32),
        pltpu.VMEM((CL + 1, B, RHS), F32),
    ] + plan_scratch()


def k2(*args):
    return call(
        forward_first, "forward_products",
        shaped((CL, RHS, B), F32), VMEM,
        [VMEM] * 10,
        forward_scratch(),
    )(*args)


def k3(*args):
    return call(
        image_first, "first_image",
        [
            pltpu.VMEM((RHS, CL * B), F32),
            shaped((CL, RHS, B), BF16),
            shaped((16, B), jnp.int32),
        ]
        + message_shapes(RHS, BF16, third=4),
        [VMEM] * 7,
        [VMEM] * 6,
        [pltpu.VMEM((1, SLOTS), jnp.int32), pltpu.SMEM((1, SLOTS), jnp.int32), pltpu.SemaphoreType.DMA],
    )(*args)


def k4(*args):
    return call(
        back_second, "second_transposed_products",
        message_shapes(RHS, BF16),
        [VMEM] * 4,
        [VMEM] * 5,
        [pltpu.VMEM((CL + 1, RHS, B), BF16), pltpu.VMEM((PEERS + 1, RHS, B), F32)] + plan_scratch(),
    )(*args)


def k5(*args):
    return call(
        forward_second, "second_forward_products",
        shaped((CL, RHS, B), F32), VMEM,
        [VMEM] * 11,
        forward_scratch(),
    )(*args)


def k6(*args):
    return call(
        image_second, "second_image",
        shaped((RHS, CL * B), F32), HBM,
        [VMEM] * 7,
        [pltpu.VMEM((RHS, CL * B), F32), pltpu.SemaphoreType.DMA((RHS // STRIP,))],
    )(*args)


def carriers(size, k):
    pairs = []
    for chip in range(size // 2):
        for core in range(2):
            step = k if core == 0 else -k
            pairs.append((2 * chip + core, (2 * (chip + step) + core) % size))
    return pairs


def per_device(
    vectors, diag_blocks, near_blocks, near_rows, near_cols, far_left, far_right, far_rows, far_cols, counts
):
    size = lax.axis_size("rows")
    me = lax.axis_index("rows").reshape(1)

    def swap(block):
        return lax.ppermute(block, "rows", [(i, i ^ 1) for i in range(size)])

    def carry(block, k):
        return lax.ppermute(block, "rows", carriers(size, k))

    def carried(messages):
        second, first, third = [carry(messages[k - 1], k) for k in (2, 1, 3)]
        return [first, second, third]

    def exchange(m1, m2, m3, give):
        got = swap(give)
        messages = []
        for k, message in enumerate((m1, m2, m3)):
            messages.append(lax.dynamic_update_slice(message, got[2 * k : 2 * k + 2], (1, 0, 0)))
        return carried(messages) + [got, messages]

    def passed_on(r1, r2, r3):
        return swap(jnp.concatenate([r1[2:4], r2[2:4], r3[2:3]]))

    def in_hbm(x):
        return pltpu.with_memory_space_constraint(x, pltpu.HBM)

    lists = [in_hbm(x.reshape(1, SLOTS)) for x in (near_rows, near_cols, far_rows, far_cols)]
    sib = swap(vectors)
    both = lax.dynamic_update_slice(staged(in_hbm(vectors)), sib[None], (1, 0, 0))
    halo = carried([both] * 3)
    m1, m2, m3, give, plan, *held = k1(
        me, *lists, in_hbm(counts), both, in_hbm(near_blocks), in_hbm(far_left), in_hbm(far_right)
    )
    far_halo, halo_1, halo_3, m1 = lax.optimization_barrier((halo[1], halo[0], halo[2], m1))
    halo = (halo_1, far_halo, halo_3)
    r1, r2, r3, got, messages = exchange(m1, m2, m3, give)
    halo_post = swap(jnp.concatenate([halo[0], halo[1], halo[2][1:]]))
    halo_post, messages = lax.optimization_barrier((halo_post, messages))
    partial = k2(plan, both, *halo, halo_post, diag_blocks, *held)
    partial, r2, r1, r3 = lax.optimization_barrier((partial, r2, r1, r3))
    post = passed_on(r1, r2, r3)
    first_image, rounded, marked, m1, m2, m3, give = k3(partial, r1, r2, r3, post, got)
    f1, f2, f3, f_got, messages = exchange(m1, m2, m3, give)
    rounded, messages = lax.optimization_barrier((rounded, messages))
    m1, m2, m3, give = k4(plan, rounded, *held)
    f1, f2, f3, m1 = lax.optimization_barrier((f1, f2, f3, m1))
    r1, r2, r3, got, messages = exchange(m1, m2, m3, give)
    f_post = passed_on(f1, f2, f3)
    f_post, messages = lax.optimization_barrier((f_post, messages))
    partial = k5(plan, rounded, f1, f2, f3, f_post, f_got, diag_blocks, *held)
    partial, r2, r1, r3 = lax.optimization_barrier((partial, r2, r1, r3))
    post = passed_on(r1, r2, r3)
    return first_image, k6(partial, marked, r1, r2, r3, post, got)


def solution(mesh):
    return jax.shard_map(
        per_device,
        mesh=mesh,
        in_specs=(
            P(None, "rows"),
            P("rows", None, None),
            P("rows", None, None),
            P("rows"),
            P("rows"),
            P("rows", None, None),
            P("rows", None, None),
            P("rows"),
            P("rows"),
            P("rows", None),
        ),
        out_specs=(P(None, "rows"), P(None, "rows")),
        check_vma=False,
    )
```

```python
import functools

import jax
import jax.numpy as jnp
from jax import lax
from jax.experimental import pallas as pl
from jax.experimental.pallas import tpu as pltpu
from jax.sharding import PartitionSpec as P

RHS, B, K = 64, 256, 32
CL, SLOTS, CHUNK = 4, 128, 16
CHUNKS = SLOTS // CHUNK
GROUP = B // K
HALF = B // 2
PEERS = 12
DEAD = 12
EXTRA = 16
LEVELS = 32766.0
TINY = 2.0**-100
LN2 = 0.6931471805599453
QUAD = 4
VMEM_BYTES = 16 * 2**20
F32, BF16 = jnp.float32, jnp.bfloat16


def dot(x, y):
    return lax.dot_general(x, y, (((1,), (0,)), ((), ())), preferred_element_type=F32)


def dot_t(x, y):
    return lax.dot_general(x, y, (((1,), (1,)), ((), ())), preferred_element_type=F32)


def peer_number(delta, core):
    kappa, other = delta // 2 - 3, delta % 2
    step = kappa * (1 - 2 * core)
    same = int(other != core)
    if step == 0:
        return 11 if same else DEAD
    if step < 0:
        return 2 * (-step - 1) + same
    return 6 + 2 * (step - 1) + same if step < 3 or not same else DEAD


PLAN = (4, 2 * SLOTS)
COUNTS, WANTED = 64, 80
STEP = 32
GROUPS = 4


class Blocks:
    def __init__(self, plan, near, left, right, sources=None):
        self.plan, self.near, self.left, self.right = plan, near, left, right
        self.sources = sources

    def copy(self, which, chunk):
        source, sem = self.sources[which]
        place = pl.ds(chunk * CHUNK, CHUNK)
        target = (self.near, self.left, self.right)[which]
        return pltpu.make_async_copy(source.at[place], target.at[place], sem.at[chunk])

    def start(self):
        for which in (1, 2, 0):
            self.copy(which, 0).start()

    def start_rest(self, near_chunks, far_chunks):
        def far_start(chunk, carry):
            self.copy(1, chunk).start()
            self.copy(2, chunk).start()
            return carry

        def near_start(chunk, carry):
            self.copy(0, chunk).start()
            return carry

        lax.fori_loop(1, far_chunks, far_start, 0)
        lax.fori_loop(1, near_chunks, near_start, 0)

    def far_loop(self, body):
        def arrived(chunk, carry):
            self.copy(1, chunk).wait()
            self.copy(2, chunk).wait()
            return carry

        if self.sources is not None:
            lax.fori_loop(0, self.plan[2, COUNTS + 1], arrived, 0)

        def step(index, carry):
            groups = []
            for part in range(GROUPS):
                first = index * GROUPS + part
                entries = [self.plan[1, first * GROUP + k] for k in range(GROUP)]
                slots = [entry & 255 for entry in entries]
                left = jnp.concatenate([self.left[slot] for slot in slots], axis=0)
                right = jnp.concatenate([self.right[slot] for slot in slots], axis=0)
                lane = lax.broadcasted_iota(jnp.int32, (1, B), 1) // K
                rows = jnp.zeros((1, B), jnp.int32)
                for k in range(GROUP):
                    rows = jnp.where(lane == k, entries[k] >> 8, rows)
                rows = jnp.broadcast_to(rows, (RHS, B))
                groups.append((left, right, rows, [self.plan[2, 2 * first + half] for half in (0, 1)]))
            body(groups)
            return carry

        lax.fori_loop(0, self.plan[2, COUNTS + 2], step, 0)

    def near_loop(self, body):
        size = STEP if self.sources is None else CHUNK

        def step(index, carry):
            if self.sources is not None:
                self.copy(0, index).wait()
            for part in range(size):
                slot = index * size + part
                code = self.plan[0, slot]
                body(part, code & 7, code >> 3, self.near[slot])
            return carry

        lax.fori_loop(0, self.plan[2, COUNTS] * (STEP // size), step, 0)


def halves(x, axis):
    return (x[:HALF], x[HALF:]) if axis == 0 else (x[:, :HALF], x[:, HALF:])


def back_products(blocks, own, acc):
    def far(groups):
        coefs = []
        for left, right, rows, partners in groups:
            every = dot_t(own[0:CL].reshape(CL * RHS, B), left)
            coef = jnp.zeros((RHS, B), F32)
            for cluster in range(CL):
                coef = jnp.where(rows == cluster, every[cluster * RHS : (cluster + 1) * RHS], coef)
            coefs.append(coef.astype(BF16))
        terms = []
        for coef, (left, right, rows, partners) in zip(coefs, groups):
            for part, block, partner in zip(halves(coef, 1), halves(right, 0), partners):
                terms.append((partner, dot(part, block)))
        for partner, term in terms:
            acc[partner] += term

    def near(part, row, partner, block):
        acc[partner] += dot(own[row], block)

    blocks.far_loop(far)
    blocks.near_loop(near)


def forward_products(blocks, fetched, turned, acc, acc_turned):
    turned[DEAD] = jnp.zeros((B, RHS), BF16)
    for partner in range(PEERS):
        turned[partner] = fetched[partner].T
    acc_turned[...] = jnp.zeros_like(acc_turned)

    def far(groups):
        spreads = []
        for left, right, rows, partners in groups:
            coef = [dot_t(fetched[partner], block) for partner, block in zip(partners, halves(right, 0))]
            coef = jnp.concatenate(coef, axis=1).astype(BF16).astype(F32)
            spread = [jnp.where(rows == cluster, coef, 0.0).astype(BF16) for cluster in range(CL)]
            spreads.append(jnp.concatenate(spread, axis=0))
        terms = [dot(spread, group[0]) for spread, group in zip(spreads, groups)]
        total = terms[0]
        for term in terms[1:]:
            total += term
        acc[0:CL] += total.reshape(CL, RHS, B)

    def near(part, row, partner, block):
        if part % 2 == 0:
            acc[row] += dot_t(fetched[partner], block)
        else:
            acc_turned[row] += dot(block, turned[partner])

    blocks.far_loop(far)
    blocks.near_loop(near)
    for cluster in range(CL):
        acc[cluster] += acc_turned[cluster].T


def make_plan(me, lists, few, draft):
    core = me % 2
    base = me - core - 6
    lane = lax.broadcasted_iota(jnp.int32, (1, SLOTS), 1)
    row16 = lax.broadcasted_iota(jnp.int32, (16, SLOTS), 0)
    kinds = []
    for kind in (0, 1):
        rows, cols = lists[2 * kind : 2 * kind + 1, :], lists[2 * kind + 1 : 2 * kind + 2, :]
        live = lane < few[0, kind]
        delta = ((cols >> 2) - base) & 15
        partner = jnp.full((1, SLOTS), DEAD, jnp.int32)
        for value in range(14):
            pair = [peer_number(value, a) for a in (0, 1)]
            partner = jnp.where(delta == value, jnp.where(core == 0, pair[0], pair[1]), partner)
        partner = jnp.where(live, partner, DEAD)
        kinds.append((jnp.where(live, rows & (CL - 1), CL), partner, cols & (CL - 1)))
    (near_row, near_rho, near_part), (far_row, far_rho, far_part) = kinds
    wide = lambda x: jnp.broadcast_to(x, (16, SLOTS))
    hot = row16 == wide(far_rho)
    wanted = jnp.maximum(
        jnp.where(row16 == wide(near_rho), wide(near_part).astype(F32), 0.0),
        jnp.where(hot, wide(far_part).astype(F32), 0.0),
    )
    wanted = jnp.max(wanted, axis=1, keepdims=True)
    hot = jnp.where(hot, 1.0, 0.0)
    square = (SLOTS, SLOTS)
    earlier = lax.broadcasted_iota(jnp.int32, square, 0) < lax.broadcasted_iota(jnp.int32, square, 1)
    rank = dot(hot.astype(BF16), jnp.where(earlier, 1.0, 0.0).astype(BF16)).astype(jnp.int32)
    number = wide(jnp.sum(hot, axis=1, keepdims=True)).astype(jnp.int32)
    padded = ((number + (QUAD - 1)) >> 2) << 2
    place = jnp.full((1, SLOTS), -1, jnp.int32)
    quad_rho = jnp.full((1, SLOTS), DEAD, jnp.int32)
    first = jnp.zeros((1, SLOTS), jnp.int32)
    for rho in range(PEERS):
        place = jnp.where(far_rho == rho, rank[rho : rho + 1] + first, place)
        last = first + padded[rho : rho + 1]
        quad_rho = jnp.where((lane * QUAD >= first) & (lane * QUAD < last), rho, quad_rho)
        first = last
    column = jnp.transpose(jnp.broadcast_to(place.astype(F32), square))
    spots = lax.broadcasted_iota(jnp.int32, square, 1).astype(F32)
    hits = jnp.concatenate([jnp.where(column == spots + shift, 1.0, 0.0).astype(BF16) for shift in (0.0, float(SLOTS))], axis=1)
    codes = jnp.where(row16 == 0, wide(lane), jnp.where(row16 == 1, wide(far_row), 1)).astype(F32).astype(BF16)
    found = dot(codes, hits)
    entry = jnp.where(found[2:3] > 0.5, found[0:1] + 256.0 * found[1:2], 256.0 * CL).astype(jnp.int32)
    wanted = jnp.sum(jnp.where(row16 + WANTED == wide(lane), wide(wanted), 0.0), axis=0, keepdims=True).astype(jnp.int32)
    draft[0:1, 0:SLOTS] = near_row + 8 * near_rho
    draft[1:2, :] = entry
    numbers = jnp.where(lane == COUNTS, (few[0, 0] + (STEP - 1)) // STEP, jnp.where(lane < COUNTS, quad_rho, wanted))
    numbers = jnp.where(lane == COUNTS + 1, (few[0, 1] + (CHUNK - 1)) // CHUNK, numbers)
    steps = (first + (2 * GROUPS * QUAD - 1)) >> (GROUPS.bit_length() + 2)
    draft[2:3, 0:SLOTS] = jnp.where(lane == COUNTS + 2, steps, numbers)


def place_out(rho):
    if rho == 11:
        return 3, 6
    if rho < 6:
        return 3, rho ^ 1
    k, same = divmod(rho - 6, 2)
    return k, 3 * same


def place_in(rho):
    if rho == 11:
        return 4, 6
    if rho < 6:
        return rho // 2, rho % 2
    return 3, rho - 6


def back_first(
    me, near_rows, near_cols, far_rows, far_cols, counts, both, near, left, right,
    m1, m2, m3, give, draft, near_held, left_held, right_held,
    own, acc, lists, few, plan, near_sem, left_sem, right_sem, list_sem,
):
    blocks = Blocks(plan, near_held, left_held, right_held, ((near, near_sem), (left, left_sem), (right, right_sem)))
    copies = [pltpu.make_async_copy(counts, few, list_sem.at[4])]
    for index, source in enumerate((near_rows, near_cols, far_rows, far_cols)):
        copies.append(pltpu.make_async_copy(source, lists.at[pl.ds(index, 1)], list_sem.at[index]))
    for copy in copies:
        copy.start()
    blocks.start()
    for cluster in range(CL):
        own[cluster] = both[0, :, cluster * B : (cluster + 1) * B]
    own[CL] = jnp.zeros((RHS, B), BF16)
    draft[...] = jnp.zeros_like(draft)
    copies[0].wait()
    near_steps = (few[0, 0] + (STEP - 1)) // STEP
    blocks.start_rest(near_steps * (STEP // CHUNK), (few[0, 1] + (CHUNK - 1)) // CHUNK)
    for copy in copies[1:]:
        copy.wait()
    make_plan(me[0], lists, few, draft)
    copy = pltpu.make_async_copy(draft, plan, list_sem.at[5])
    copy.start()
    acc[...] = jnp.zeros_like(acc)
    copy.wait()
    back_products(blocks, own, acc)
    outs = (m1, m2, m3, give)
    for rho in range(PEERS):
        message, index = place_out(rho)
        outs[message][index, 0:RHS], power = coded(acc[rho])
        half = lax.broadcasted_iota(jnp.int32, (EXTRA, B), 0) < EXTRA // 2
        outs[message][index, RHS:] = jnp.where(half, power, plan[2, WANTED + rho]).astype(jnp.int16)


def forward_first(
    draft, both, h1, h2, h3, post, diag, near, left, right,
    out,
    fetched, turned, acc, acc_turned, plan, sem,
):
    copy = pltpu.make_async_copy(draft, plan, sem)
    copy.start()
    fetched[DEAD] = jnp.zeros((RHS, B), BF16)
    acc[CL] = jnp.zeros((RHS, B), F32)
    for cluster in range(CL):
        acc[cluster] = dot_t(both[0, :, cluster * B : (cluster + 1) * B], diag[cluster])
    copy.wait()
    halo = (h1, h2, h3)
    for rho in range(PEERS):
        lanes = pl.ds(pl.multiple_of(plan[2, WANTED + rho] * B, B), B)
        if rho == 11:
            fetched[rho] = both[1, :, lanes]
        elif rho < 6:
            fetched[rho] = halo[rho // 2][rho % 2, :, lanes]
        else:
            k, same = divmod(rho - 6, 2)
            fetched[rho] = post[2 * k + (1 - same if k < 2 else 0), :, lanes]
    forward_products(Blocks(plan, near, left, right), fetched, turned, acc, acc_turned)
    out[...] = acc[0:CL]


STRIP = 16


def coded(block):
    top = jnp.maximum(jnp.max(jnp.abs(block), axis=0, keepdims=True), TINY)
    power = jnp.ceil(jnp.log(top * (1.0 / LEVELS)) * (1.0 / LN2) + 1e-3)
    scaled = block * jnp.exp(power * -LN2)
    return jnp.floor(scaled + 0.5).astype(jnp.int32).astype(jnp.int16), power.astype(jnp.int32)


def image_first(
    partial, r1, r2, r3, post, got,
    image, rounded, marked, m1, m2, m3, give,
    draft, wanted, sem,
):
    ins = (r1, r2, r3, post, got)
    places = [place_in(rho) for rho in range(PEERS)]
    extras = [ins[message][index, RHS:].astype(jnp.int32) for message, index in places]
    units = [jnp.exp(extra[0:1].astype(F32) * LN2) for extra in extras]
    marks = [extra[EXTRA // 2 : EXTRA // 2 + 1] for extra in extras]
    lane = lax.broadcasted_iota(jnp.int32, (1, SLOTS), 1)
    packed = jnp.zeros((1, SLOTS), jnp.int32)
    for rho, mark in enumerate(marks):
        packed = jnp.where(lane == rho, mark[:, 0:SLOTS], packed)
        marked[rho : rho + 1] = mark
    draft[...] = packed
    copy = pltpu.make_async_copy(draft, wanted, sem)
    copy.start()
    for first in range(0, RHS, STRIP):
        rows = slice(first, first + STRIP)
        totals = [partial[cluster, rows] for cluster in range(CL)]
        for (message, index), mark, unit in zip(places, marks, units):
            block = ins[message][index, rows].astype(jnp.int32).astype(F32) * unit
            mark = jnp.broadcast_to(mark, (STRIP, B))
            for cluster in range(CL):
                totals[cluster] += jnp.where(mark == cluster, block, 0.0)
        for cluster in range(CL):
            image[rows, cluster * B : (cluster + 1) * B] = totals[cluster]
            rounded[cluster, rows] = totals[cluster].astype(BF16)
    copy.wait()
    outs = (m1, m2, m3, give)
    for rho in range(PEERS):
        message, index = place_out(rho)
        outs[message][index] = rounded[wanted[0, rho]]


def back_second(
    draft, rounded, near, left, right,
    m1, m2, m3, give,
    own, acc, plan, sem,
):
    copy = pltpu.make_async_copy(draft, plan, sem)
    copy.start()
    own[0:CL] = rounded[...]
    own[CL] = jnp.zeros((RHS, B), BF16)
    acc[...] = jnp.zeros_like(acc)
    copy.wait()
    back_products(Blocks(plan, near, left, right), own, acc)
    outs = (m1, m2, m3, give)
    for rho in range(PEERS):
        message, index = place_out(rho)
        outs[message][index] = acc[rho].astype(BF16)


def forward_second(
    draft, own, r1, r2, r3, post, got, diag, near, left, right,
    out,
    fetched, turned, acc, acc_turned, plan, sem,
):
    copy = pltpu.make_async_copy(draft, plan, sem)
    copy.start()
    ins = (r1, r2, r3, post, got)
    for rho in range(PEERS):
        message, index = place_in(rho)
        fetched[rho] = ins[message][index]
    fetched[DEAD] = jnp.zeros((RHS, B), BF16)
    acc[CL] = jnp.zeros((RHS, B), F32)
    for cluster in range(CL):
        acc[cluster] = dot_t(own[cluster], diag[cluster])
    copy.wait()
    forward_products(Blocks(plan, near, left, right), fetched, turned, acc, acc_turned)
    out[...] = acc[0:CL]


def image_second(partial, marked, r1, r2, r3, post, got, image, acc, sem):
    ins = (r1, r2, r3, post, got)
    places = [place_in(rho) for rho in range(PEERS)]
    marks = [marked[rho : rho + 1] for rho in range(PEERS)]
    copies = []
    for first in range(0, RHS, STRIP):
        rows = slice(first, first + STRIP)
        totals = [partial[cluster, rows] for cluster in range(CL)]
        for (message, index), mark in zip(places, marks):
            block = ins[message][index, rows].astype(F32)
            mark = jnp.broadcast_to(mark, (STRIP, B))
            for cluster in range(CL):
                totals[cluster] += jnp.where(mark == cluster, block, 0.0)
        for cluster in range(CL):
            acc[rows, cluster * B : (cluster + 1) * B] = totals[cluster]
        copies.append(pltpu.make_async_copy(acc.at[rows], image.at[rows], sem.at[first // STRIP]))
        copies[-1].start()
    for copy in copies:
        copy.wait()


SMEM = pl.BlockSpec(memory_space=pltpu.SMEM)
VMEM = pl.BlockSpec(memory_space=pltpu.VMEM)
ANY = pl.BlockSpec(memory_space=pl.ANY)
HBM = pl.BlockSpec(memory_space=pltpu.HBM)


def call(kernel, name, outs, out_specs, in_specs, scratch):
    return pl.pallas_call(
        kernel,
        name=name,
        out_shape=outs,
        in_specs=in_specs,
        out_specs=out_specs,
        scratch_shapes=scratch,
        compiler_params=pltpu.CompilerParams(vmem_limit_bytes=VMEM_BYTES),
        cost_estimate=pl.CostEstimate(flops=2 * 10**9, bytes_accessed=22 * 10**6, transcendentals=0),
    )


def shaped(shape, dtype):
    return jax.ShapeDtypeStruct(shape, dtype)


def message_shapes(rows, dtype, given=7, third=3):
    return [shaped((n, rows, B), dtype) for n in (4, 4, third, given)]


def stage(source, target, sem):
    copy = pltpu.make_async_copy(source, target.at[0], sem)
    copy.start()
    copy.wait()


def staged(vectors):
    return call(stage, "staged", shaped((2, *vectors.shape), BF16), VMEM, [HBM], [pltpu.SemaphoreType.DMA])(vectors)


def k1(*args):
    held = [pltpu.VMEM(shape, BF16) for shape in ((SLOTS, B, B), (SLOTS, K, B), (SLOTS, K, B))]
    return call(
        back_first, "transposed_products",
        message_shapes(RHS + EXTRA, jnp.int16, 11) + [shaped(PLAN, jnp.int32)] + held,
        [VMEM] * 8,
        [SMEM] + [HBM] * 5 + [VMEM] + [HBM] * 3,
        [
            pltpu.VMEM((CL + 1, RHS, B), BF16),
            pltpu.VMEM((PEERS + 1, RHS, B), F32),
            pltpu.VMEM((8, SLOTS), jnp.int32),
            pltpu.SMEM((1, 2), jnp.int32),
            pltpu.SMEM(PLAN, jnp.int32),
        ]
        + [pltpu.SemaphoreType.DMA((n,)) for n in (CHUNKS, CHUNKS, CHUNKS, 6)],
    )(*args)


def plan_scratch():
    return [pltpu.SMEM(PLAN, jnp.int32), pltpu.SemaphoreType.DMA]


def forward_scratch():
    return [
        pltpu.VMEM((PEERS + 1, RHS, B), BF16),
        pltpu.VMEM((PEERS + 1, B, RHS), BF16),
        pltpu.VMEM((CL + 1, RHS, B), F32),
        pltpu.VMEM((CL + 1, B, RHS), F32),
    ] + plan_scratch()


def k2(*args):
    return call(
        forward_first, "forward_products",
        shaped((CL, RHS, B), F32), VMEM,
        [VMEM] * 10,
        forward_scratch(),
    )(*args)


def k3(*args):
    return call(
        image_first, "first_image",
        [
            pltpu.VMEM((RHS, CL * B), F32),
            shaped((CL, RHS, B), BF16),
            shaped((16, B), jnp.int32),
        ]
        + message_shapes(RHS, BF16, third=4),
        [VMEM] * 7,
        [VMEM] * 6,
        [pltpu.VMEM((1, SLOTS), jnp.int32), pltpu.SMEM((1, SLOTS), jnp.int32), pltpu.SemaphoreType.DMA],
    )(*args)


def k4(*args):
    return call(
        back_second, "second_transposed_products",
        message_shapes(RHS, BF16),
        [VMEM] * 4,
        [VMEM] * 5,
        [pltpu.VMEM((CL + 1, RHS, B), BF16), pltpu.VMEM((PEERS + 1, RHS, B), F32)] + plan_scratch(),
    )(*args)


def k5(*args):
    return call(
        forward_second, "second_forward_products",
        shaped((CL, RHS, B), F32), VMEM,
        [VMEM] * 11,
        forward_scratch(),
    )(*args)


def k6(*args):
    return call(
        image_second, "second_image",
        shaped((RHS, CL * B), F32), HBM,
        [VMEM] * 7,
        [pltpu.VMEM((RHS, CL * B), F32), pltpu.SemaphoreType.DMA((RHS // STRIP,))],
    )(*args)


def carriers(size, k):
    pairs = []
    for chip in range(size // 2):
        for core in range(2):
            step = k if core == 0 else -k
            pairs.append((2 * chip + core, (2 * (chip + step) + core) % size))
    return pairs


def per_device(
    vectors, diag_blocks, near_blocks, near_rows, near_cols, far_left, far_right, far_rows, far_cols, counts
):
    size = lax.axis_size("rows")
    me = lax.axis_index("rows").reshape(1)

    def swap(block):
        return lax.ppermute(block, "rows", [(i, i ^ 1) for i in range(size)])

    def carry(block, k):
        return lax.ppermute(block, "rows", carriers(size, k))

    def carried(messages):
        second, first, third = [carry(messages[k - 1], k) for k in (2, 1, 3)]
        return [first, second, third]

    def exchange(m1, m2, m3, give):
        got = swap(give)
        messages = []
        for k, message in enumerate((m1, m2, m3)):
            messages.append(lax.dynamic_update_slice(message, got[2 * k : 2 * k + 2], (1, 0, 0)))
        return carried(messages) + [got, messages]

    def passed_on(r1, r2, r3):
        return swap(jnp.concatenate([r1[2:4], r2[2:4], r3[2:3]]))

    def in_hbm(x):
        return pltpu.with_memory_space_constraint(x, pltpu.HBM)

    lists = [in_hbm(x.reshape(1, SLOTS)) for x in (near_rows, near_cols, far_rows, far_cols)]
    sib = swap(vectors)
    both = lax.dynamic_update_slice(staged(in_hbm(vectors)), sib[None], (1, 0, 0))
    halo = carried([both] * 3)
    m1, m2, m3, give, plan, *held = k1(
        me, *lists, in_hbm(counts), both, in_hbm(near_blocks), in_hbm(far_left), in_hbm(far_right)
    )
    far_halo, halo_1, halo_3, m1 = lax.optimization_barrier((halo[1], halo[0], halo[2], m1))
    halo = (halo_1, far_halo, halo_3)
    r1, r2, r3, got, messages = exchange(m1, m2, m3, give)
    halo_post = swap(jnp.concatenate([halo[0], halo[1], halo[2][1:]]))
    halo_post, messages = lax.optimization_barrier((halo_post, messages))
    partial = k2(plan, both, *halo, halo_post, diag_blocks, *held)
    partial, r2, r1, r3 = lax.optimization_barrier((partial, r2, r1, r3))
    post = passed_on(r1, r2, r3)
    first_image, rounded, marked, m1, m2, m3, give = k3(partial, r1, r2, r3, post, got)
    f1, f2, f3, f_got, messages = exchange(m1, m2, m3, give)
    rounded, messages = lax.optimization_barrier((rounded, messages))
    m1, m2, m3, give = k4(plan, rounded, *held)
    f2, f1, f3, m1 = lax.optimization_barrier((f2, f1, f3, m1))
    r1, r2, r3, got, messages = exchange(m1, m2, m3, give)
    f_post = passed_on(f1, f2, f3)
    f_post, messages = lax.optimization_barrier((f_post, messages))
    partial = k5(plan, rounded, f1, f2, f3, f_post, f_got, diag_blocks, *held)
    partial, r2, r1, r3 = lax.optimization_barrier((partial, r2, r1, r3))
    post = passed_on(r1, r2, r3)
    return first_image, k6(partial, marked, r1, r2, r3, post, got)


def solution(mesh):
    return jax.shard_map(
        per_device,
        mesh=mesh,
        in_specs=(
            P(None, "rows"),
            P("rows", None, None),
            P("rows", None, None),
            P("rows"),
            P("rows"),
            P("rows", None, None),
            P("rows", None, None),
            P("rows"),
            P("rows"),
            P("rows", None),
        ),
        out_specs=(P(None, "rows"), P(None, "rows")),
        check_vma=False,
    )
```

```python
import functools

import jax
import jax.numpy as jnp
from jax import lax
from jax.experimental import pallas as pl
from jax.experimental.pallas import tpu as pltpu
from jax.sharding import PartitionSpec as P

RHS, B, K = 64, 256, 32
CL, SLOTS, CHUNK = 4, 128, 16
CHUNKS = SLOTS // CHUNK
GROUP = B // K
HALF = B // 2
PEERS = 12
DEAD = 12
EXTRA = 16
LEVELS = 32766.0
TINY = 2.0**-100
LN2 = 0.6931471805599453
QUAD = 4
VMEM_BYTES = 16 * 2**20
F32, BF16 = jnp.float32, jnp.bfloat16


def dot(x, y):
    return lax.dot_general(x, y, (((1,), (0,)), ((), ())), preferred_element_type=F32)


def dot_t(x, y):
    return lax.dot_general(x, y, (((1,), (1,)), ((), ())), preferred_element_type=F32)


def peer_number(delta, core):
    kappa, other = delta // 2 - 3, delta % 2
    step = kappa * (1 - 2 * core)
    same = int(other != core)
    if step == 0:
        return 11 if same else DEAD
    if step < 0:
        return 2 * (-step - 1) + same
    return 6 + 2 * (step - 1) + same if step < 3 or not same else DEAD


PLAN = (4, 2 * SLOTS)
COUNTS, WANTED = 64, 80
STEP = 32
GROUPS = 4


class Blocks:
    def __init__(self, plan, near, left, right, sources=None):
        self.plan, self.near, self.left, self.right = plan, near, left, right
        self.sources = sources

    def copy(self, which, chunk):
        source, sem = self.sources[which]
        place = pl.ds(chunk * CHUNK, CHUNK)
        target = (self.near, self.left, self.right)[which]
        return pltpu.make_async_copy(source.at[place], target.at[place], sem.at[chunk])

    def start(self):
        for which in (1, 2, 0):
            self.copy(which, 0).start()

    def start_rest(self, near_chunks, far_chunks):
        def far_start(chunk, carry):
            self.copy(1, chunk).start()
            self.copy(2, chunk).start()
            return carry

        def near_start(chunk, carry):
            self.copy(0, chunk).start()
            return carry

        lax.fori_loop(1, far_chunks, far_start, 0)
        lax.fori_loop(1, near_chunks, near_start, 0)

    def far_loop(self, body):
        def arrived(chunk, carry):
            self.copy(1, chunk).wait()
            self.copy(2, chunk).wait()
            return carry

        if self.sources is not None:
            lax.fori_loop(0, self.plan[2, COUNTS + 1], arrived, 0)

        def step(index, carry):
            groups = []
            for part in range(GROUPS):
                first = index * GROUPS + part
                entries = [self.plan[1, first * GROUP + k] for k in range(GROUP)]
                slots = [entry & 255 for entry in entries]
                left = jnp.concatenate([self.left[slot] for slot in slots], axis=0)
                right = jnp.concatenate([self.right[slot] for slot in slots], axis=0)
                lane = lax.broadcasted_iota(jnp.int32, (1, B), 1) // K
                rows = jnp.zeros((1, B), jnp.int32)
                for k in range(GROUP):
                    rows = jnp.where(lane == k, entries[k] >> 8, rows)
                rows = jnp.broadcast_to(rows, (RHS, B))
                groups.append((left, right, rows, [self.plan[2, 2 * first + half] for half in (0, 1)]))
            body(groups)
            return carry

        lax.fori_loop(0, self.plan[2, COUNTS + 2], step, 0)

    def near_loop(self, body):
        size = STEP if self.sources is None else CHUNK

        def step(index, carry):
            if self.sources is not None:
                self.copy(0, index).wait()
            for part in range(size):
                slot = index * size + part
                code = self.plan[0, slot]
                body(part, code & 7, code >> 3, self.near[slot])
            return carry

        lax.fori_loop(0, self.plan[2, COUNTS] * (STEP // size), step, 0)


def halves(x, axis):
    return (x[:HALF], x[HALF:]) if axis == 0 else (x[:, :HALF], x[:, HALF:])


def back_products(blocks, own, acc):
    def far(groups):
        coefs = []
        for left, right, rows, partners in groups:
            every = dot_t(own[0:CL].reshape(CL * RHS, B), left)
            coef = jnp.zeros((RHS, B), F32)
            for cluster in range(CL):
                coef = jnp.where(rows == cluster, every[cluster * RHS : (cluster + 1) * RHS], coef)
            coefs.append(coef.astype(BF16))
        terms = []
        for coef, (left, right, rows, partners) in zip(coefs, groups):
            for part, block, partner in zip(halves(coef, 1), halves(right, 0), partners):
                terms.append((partner, dot(part, block)))
        for partner, term in terms:
            acc[partner] += term

    def near(part, row, partner, block):
        acc[partner] += dot(own[row], block)

    blocks.far_loop(far)
    blocks.near_loop(near)


def forward_products(blocks, fetched, turned, acc, acc_turned):
    turned[DEAD] = jnp.zeros((B, RHS), BF16)
    for partner in range(PEERS):
        turned[partner] = fetched[partner].T
    acc_turned[...] = jnp.zeros_like(acc_turned)

    def far(groups):
        spreads = []
        for left, right, rows, partners in groups:
            coef = [dot_t(fetched[partner], block) for partner, block in zip(partners, halves(right, 0))]
            coef = jnp.concatenate(coef, axis=1).astype(BF16).astype(F32)
            spread = [jnp.where(rows == cluster, coef, 0.0).astype(BF16) for cluster in range(CL)]
            spreads.append(jnp.concatenate(spread, axis=0))
        terms = [dot(spread, group[0]) for spread, group in zip(spreads, groups)]
        total = terms[0]
        for term in terms[1:]:
            total += term
        acc[0:CL] += total.reshape(CL, RHS, B)

    def near(part, row, partner, block):
        if part % 2 == 0:
            acc[row] += dot_t(fetched[partner], block)
        else:
            acc_turned[row] += dot(block, turned[partner])

    blocks.far_loop(far)
    blocks.near_loop(near)
    for cluster in range(CL):
        acc[cluster] += acc_turned[cluster].T


def make_plan(me, lists, few, draft):
    core = me % 2
    base = me - core - 6
    lane = lax.broadcasted_iota(jnp.int32, (1, SLOTS), 1)
    row16 = lax.broadcasted_iota(jnp.int32, (16, SLOTS), 0)
    kinds = []
    for kind in (0, 1):
        rows, cols = lists[2 * kind : 2 * kind + 1, :], lists[2 * kind + 1 : 2 * kind + 2, :]
        live = lane < few[0, kind]
        delta = ((cols >> 2) - base) & 15
        partner = jnp.full((1, SLOTS), DEAD, jnp.int32)
        for value in range(14):
            pair = [peer_number(value, a) for a in (0, 1)]
            partner = jnp.where(delta == value, jnp.where(core == 0, pair[0], pair[1]), partner)
        partner = jnp.where(live, partner, DEAD)
        kinds.append((jnp.where(live, rows & (CL - 1), CL), partner, cols & (CL - 1)))
    (near_row, near_rho, near_part), (far_row, far_rho, far_part) = kinds
    wide = lambda x: jnp.broadcast_to(x, (16, SLOTS))
    hot = row16 == wide(far_rho)
    wanted = jnp.maximum(
        jnp.where(row16 == wide(near_rho), wide(near_part).astype(F32), 0.0),
        jnp.where(hot, wide(far_part).astype(F32), 0.0),
    )
    wanted = jnp.max(wanted, axis=1, keepdims=True)
    hot = jnp.where(hot, 1.0, 0.0)
    square = (SLOTS, SLOTS)
    earlier = lax.broadcasted_iota(jnp.int32, square, 0) < lax.broadcasted_iota(jnp.int32, square, 1)
    rank = dot(hot.astype(BF16), jnp.where(earlier, 1.0, 0.0).astype(BF16)).astype(jnp.int32)
    number = wide(jnp.sum(hot, axis=1, keepdims=True)).astype(jnp.int32)
    padded = ((number + (QUAD - 1)) >> 2) << 2
    place = jnp.full((1, SLOTS), -1, jnp.int32)
    quad_rho = jnp.full((1, SLOTS), DEAD, jnp.int32)
    first = jnp.zeros((1, SLOTS), jnp.int32)
    for rho in range(PEERS):
        place = jnp.where(far_rho == rho, rank[rho : rho + 1] + first, place)
        last = first + padded[rho : rho + 1]
        quad_rho = jnp.where((lane * QUAD >= first) & (lane * QUAD < last), rho, quad_rho)
        first = last
    column = jnp.transpose(jnp.broadcast_to(place.astype(F32), square))
    spots = lax.broadcasted_iota(jnp.int32, square, 1).astype(F32)
    hits = jnp.concatenate([jnp.where(column == spots + shift, 1.0, 0.0).astype(BF16) for shift in (0.0, float(SLOTS))], axis=1)
    codes = jnp.where(row16 == 0, wide(lane), jnp.where(row16 == 1, wide(far_row), 1)).astype(F32).astype(BF16)
    found = dot(codes, hits)
    entry = jnp.where(found[2:3] > 0.5, found[0:1] + 256.0 * found[1:2], 256.0 * CL).astype(jnp.int32)
    wanted = jnp.sum(jnp.where(row16 + WANTED == wide(lane), wide(wanted), 0.0), axis=0, keepdims=True).astype(jnp.int32)
    draft[0:1, 0:SLOTS] = near_row + 8 * near_rho
    draft[1:2, :] = entry
    numbers = jnp.where(lane == COUNTS, (few[0, 0] + (STEP - 1)) // STEP, jnp.where(lane < COUNTS, quad_rho, wanted))
    numbers = jnp.where(lane == COUNTS + 1, (few[0, 1] + (CHUNK - 1)) // CHUNK, numbers)
    steps = (first + (2 * GROUPS * QUAD - 1)) >> (GROUPS.bit_length() + 2)
    draft[2:3, 0:SLOTS] = jnp.where(lane == COUNTS + 2, steps, numbers)


def place_out(rho):
    if rho == 11:
        return 3, 6
    if rho < 6:
        return 3, rho ^ 1
    k, same = divmod(rho - 6, 2)
    return k, 3 * same


def place_in(rho):
    if rho == 11:
        return 4, 6
    if rho < 6:
        return rho // 2, rho % 2
    return 3, rho - 6


def back_first(
    me, near_rows, near_cols, far_rows, far_cols, counts, both, near, left, right,
    m1, m2, m3, give, draft, near_held, left_held, right_held,
    own, acc, lists, few, plan, near_sem, left_sem, right_sem, list_sem,
):
    blocks = Blocks(plan, near_held, left_held, right_held, ((near, near_sem), (left, left_sem), (right, right_sem)))
    copies = [pltpu.make_async_copy(counts, few, list_sem.at[4])]
    for index, source in enumerate((near_rows, near_cols, far_rows, far_cols)):
        copies.append(pltpu.make_async_copy(source, lists.at[pl.ds(index, 1)], list_sem.at[index]))
    for copy in copies:
        copy.start()
    blocks.start()
    for cluster in range(CL):
        own[cluster] = both[0, :, cluster * B : (cluster + 1) * B]
    own[CL] = jnp.zeros((RHS, B), BF16)
    draft[...] = jnp.zeros_like(draft)
    copies[0].wait()
    near_steps = (few[0, 0] + (STEP - 1)) // STEP
    blocks.start_rest(near_steps * (STEP // CHUNK), (few[0, 1] + (CHUNK - 1)) // CHUNK)
    for copy in copies[1:]:
        copy.wait()
    make_plan(me[0], lists, few, draft)
    copy = pltpu.make_async_copy(draft, plan, list_sem.at[5])
    copy.start()
    acc[...] = jnp.zeros_like(acc)
    copy.wait()
    back_products(blocks, own, acc)
    outs = (m1, m2, m3, give)
    for rho in range(PEERS):
        message, index = place_out(rho)
        outs[message][index, 0:RHS], power = coded(acc[rho])
        half = lax.broadcasted_iota(jnp.int32, (EXTRA, B), 0) < EXTRA // 2
        outs[message][index, RHS:] = jnp.where(half, power, plan[2, WANTED + rho]).astype(jnp.int16)


def forward_first(
    draft, both, h1, h2, h3, post, diag, near, left, right,
    out,
    fetched, turned, acc, acc_turned, plan, sem,
):
    copy = pltpu.make_async_copy(draft, plan, sem)
    copy.start()
    fetched[DEAD] = jnp.zeros((RHS, B), BF16)
    acc[CL] = jnp.zeros((RHS, B), F32)
    for cluster in range(CL):
        acc[cluster] = dot_t(both[0, :, cluster * B : (cluster + 1) * B], diag[cluster])
    copy.wait()
    halo = (h1, h2, h3)
    for rho in range(PEERS):
        lanes = pl.ds(pl.multiple_of(plan[2, WANTED + rho] * B, B), B)
        if rho == 11:
            fetched[rho] = both[1, :, lanes]
        elif rho < 6:
            fetched[rho] = halo[rho // 2][rho % 2, :, lanes]
        else:
            k, same = divmod(rho - 6, 2)
            fetched[rho] = post[2 * k + (1 - same if k < 2 else 0), :, lanes]
    forward_products(Blocks(plan, near, left, right), fetched, turned, acc, acc_turned)
    out[...] = acc[0:CL]


STRIP = 16


def coded(block):
    top = jnp.maximum(jnp.max(jnp.abs(block), axis=0, keepdims=True), TINY)
    power = jnp.ceil(jnp.log(top * (1.0 / LEVELS)) * (1.0 / LN2) + 1e-3)
    scaled = block * jnp.exp(power * -LN2)
    return jnp.floor(scaled + 0.5).astype(jnp.int32).astype(jnp.int16), power.astype(jnp.int32)


def image_first(
    partial, r1, r2, r3, post, got,
    image, rounded, marked, m1, m2, m3, give,
    draft, wanted, sem,
):
    ins = (r1, r2, r3, post, got)
    places = [place_in(rho) for rho in range(PEERS)]
    extras = [ins[message][index, RHS:].astype(jnp.int32) for message, index in places]
    units = [jnp.exp(extra[0:1].astype(F32) * LN2) for extra in extras]
    marks = [extra[EXTRA // 2 : EXTRA // 2 + 1] for extra in extras]
    lane = lax.broadcasted_iota(jnp.int32, (1, SLOTS), 1)
    packed = jnp.zeros((1, SLOTS), jnp.int32)
    for rho, mark in enumerate(marks):
        packed = jnp.where(lane == rho, mark[:, 0:SLOTS], packed)
        marked[rho : rho + 1] = mark
    draft[...] = packed
    copy = pltpu.make_async_copy(draft, wanted, sem)
    copy.start()
    for first in range(0, RHS, STRIP):
        rows = slice(first, first + STRIP)
        totals = [partial[cluster, rows] for cluster in range(CL)]
        for (message, index), mark, unit in zip(places, marks, units):
            block = ins[message][index, rows].astype(jnp.int32).astype(F32) * unit
            mark = jnp.broadcast_to(mark, (STRIP, B))
            for cluster in range(CL):
                totals[cluster] += jnp.where(mark == cluster, block, 0.0)
        for cluster in range(CL):
            image[rows, cluster * B : (cluster + 1) * B] = totals[cluster]
            rounded[cluster, rows] = totals[cluster].astype(BF16)
    copy.wait()
    outs = (m1, m2, m3, give)
    for rho in range(PEERS):
        message, index = place_out(rho)
        outs[message][index] = rounded[wanted[0, rho]]


def back_second(
    draft, rounded, near, left, right,
    m1, m2, m3, give,
    own, acc, plan, sem,
):
    copy = pltpu.make_async_copy(draft, plan, sem)
    copy.start()
    own[0:CL] = rounded[...]
    own[CL] = jnp.zeros((RHS, B), BF16)
    acc[...] = jnp.zeros_like(acc)
    copy.wait()
    back_products(Blocks(plan, near, left, right), own, acc)
    outs = (m1, m2, m3, give)
    for rho in range(PEERS):
        message, index = place_out(rho)
        outs[message][index] = acc[rho].astype(BF16)


def forward_second(
    draft, own, r1, r2, r3, post, got, diag, near, left, right,
    out,
    fetched, turned, acc, acc_turned, plan, sem,
):
    copy = pltpu.make_async_copy(draft, plan, sem)
    copy.start()
    ins = (r1, r2, r3, post, got)
    for rho in range(PEERS):
        message, index = place_in(rho)
        fetched[rho] = ins[message][index]
    fetched[DEAD] = jnp.zeros((RHS, B), BF16)
    acc[CL] = jnp.zeros((RHS, B), F32)
    for cluster in range(CL):
        acc[cluster] = dot_t(own[cluster], diag[cluster])
    copy.wait()
    forward_products(Blocks(plan, near, left, right), fetched, turned, acc, acc_turned)
    out[...] = acc[0:CL]


def image_second(partial, marked, r1, r2, r3, post, got, image, acc, sem):
    ins = (r1, r2, r3, post, got)
    places = [place_in(rho) for rho in range(PEERS)]
    marks = [marked[rho : rho + 1] for rho in range(PEERS)]
    copies = []
    for first in range(0, RHS, STRIP):
        rows = slice(first, first + STRIP)
        totals = [partial[cluster, rows] for cluster in range(CL)]
        for (message, index), mark in zip(places, marks):
            block = ins[message][index, rows].astype(F32)
            mark = jnp.broadcast_to(mark, (STRIP, B))
            for cluster in range(CL):
                totals[cluster] += jnp.where(mark == cluster, block, 0.0)
        for cluster in range(CL):
            acc[rows, cluster * B : (cluster + 1) * B] = totals[cluster]
        copies.append(pltpu.make_async_copy(acc.at[rows], image.at[rows], sem.at[first // STRIP]))
        copies[-1].start()
    for copy in copies:
        copy.wait()


SMEM = pl.BlockSpec(memory_space=pltpu.SMEM)
VMEM = pl.BlockSpec(memory_space=pltpu.VMEM)
ANY = pl.BlockSpec(memory_space=pl.ANY)
HBM = pl.BlockSpec(memory_space=pltpu.HBM)


def call(kernel, name, outs, out_specs, in_specs, scratch):
    return pl.pallas_call(
        kernel,
        name=name,
        out_shape=outs,
        in_specs=in_specs,
        out_specs=out_specs,
        scratch_shapes=scratch,
        compiler_params=pltpu.CompilerParams(vmem_limit_bytes=VMEM_BYTES),
        cost_estimate=pl.CostEstimate(flops=2 * 10**9, bytes_accessed=22 * 10**6, transcendentals=0),
    )


def shaped(shape, dtype):
    return jax.ShapeDtypeStruct(shape, dtype)


def message_shapes(rows, dtype, given=7, third=3):
    return [shaped((n, rows, B), dtype) for n in (4, 4, third, given)]


def stage(source, target, sem):
    copy = pltpu.make_async_copy(source, target.at[0], sem)
    copy.start()
    copy.wait()


def staged(vectors):
    return call(stage, "staged", shaped((2, *vectors.shape), BF16), VMEM, [HBM], [pltpu.SemaphoreType.DMA])(vectors)


def k1(*args):
    held = [pltpu.VMEM(shape, BF16) for shape in ((SLOTS, B, B), (SLOTS, K, B), (SLOTS, K, B))]
    return call(
        back_first, "transposed_products",
        message_shapes(RHS + EXTRA, jnp.int16, 11) + [shaped(PLAN, jnp.int32)] + held,
        [VMEM] * 8,
        [SMEM] + [HBM] * 5 + [VMEM] + [HBM] * 3,
        [
            pltpu.VMEM((CL + 1, RHS, B), BF16),
            pltpu.VMEM((PEERS + 1, RHS, B), F32),
            pltpu.VMEM((8, SLOTS), jnp.int32),
            pltpu.SMEM((1, 2), jnp.int32),
            pltpu.SMEM(PLAN, jnp.int32),
        ]
        + [pltpu.SemaphoreType.DMA((n,)) for n in (CHUNKS, CHUNKS, CHUNKS, 6)],
    )(*args)


def plan_scratch():
    return [pltpu.SMEM(PLAN, jnp.int32), pltpu.SemaphoreType.DMA]


def forward_scratch():
    return [
        pltpu.VMEM((PEERS + 1, RHS, B), BF16),
        pltpu.VMEM((PEERS + 1, B, RHS), BF16),
        pltpu.VMEM((CL + 1, RHS, B), F32),
        pltpu.VMEM((CL + 1, B, RHS), F32),
    ] + plan_scratch()


def k2(*args):
    return call(
        forward_first, "forward_products",
        shaped((CL, RHS, B), F32), VMEM,
        [VMEM] * 10,
        forward_scratch(),
    )(*args)


def k3(*args):
    return call(
        image_first, "first_image",
        [
            pltpu.VMEM((RHS, CL * B), F32),
            shaped((CL, RHS, B), BF16),
            shaped((16, B), jnp.int32),
        ]
        + message_shapes(RHS, BF16, third=4),
        [VMEM] * 7,
        [VMEM] * 6,
        [pltpu.VMEM((1, SLOTS), jnp.int32), pltpu.SMEM((1, SLOTS), jnp.int32), pltpu.SemaphoreType.DMA],
    )(*args)


def k4(*args):
    return call(
        back_second, "second_transposed_products",
        message_shapes(RHS, BF16),
        [VMEM] * 4,
        [VMEM] * 5,
        [pltpu.VMEM((CL + 1, RHS, B), BF16), pltpu.VMEM((PEERS + 1, RHS, B), F32)] + plan_scratch(),
    )(*args)


def k5(*args):
    return call(
        forward_second, "second_forward_products",
        shaped((CL, RHS, B), F32), VMEM,
        [VMEM] * 11,
        forward_scratch(),
    )(*args)


def k6(*args):
    return call(
        image_second, "second_image",
        shaped((RHS, CL * B), F32), HBM,
        [VMEM] * 7,
        [pltpu.VMEM((RHS, CL * B), F32), pltpu.SemaphoreType.DMA((RHS // STRIP,))],
    )(*args)


def carriers(size, k):
    pairs = []
    for chip in range(size // 2):
        for core in range(2):
            step = k if core == 0 else -k
            pairs.append((2 * chip + core, (2 * (chip + step) + core) % size))
    return pairs


def per_device(
    vectors, diag_blocks, near_blocks, near_rows, near_cols, far_left, far_right, far_rows, far_cols, counts
):
    size = lax.axis_size("rows")
    me = lax.axis_index("rows").reshape(1)

    def swap(block):
        return lax.ppermute(block, "rows", [(i, i ^ 1) for i in range(size)])

    def carry(block, k):
        return lax.ppermute(block, "rows", carriers(size, k))

    def carried(messages):
        second, first, third = [carry(messages[k - 1], k) for k in (2, 1, 3)]
        return [first, second, third]

    def exchange(m1, m2, m3, give):
        got = swap(give)
        messages = []
        for k, message in enumerate((m1, m2, m3)):
            messages.append(lax.dynamic_update_slice(message, got[2 * k : 2 * k + 2], (1, 0, 0)))
        return carried(messages) + [got, messages]

    def passed_on(r1, r2, r3):
        return swap(jnp.concatenate([r1[2:4], r2[2:4], r3[2:3]]))

    def in_hbm(x):
        return pltpu.with_memory_space_constraint(x, pltpu.HBM)

    lists = [in_hbm(x.reshape(1, SLOTS)) for x in (near_rows, near_cols, far_rows, far_cols)]
    sib = swap(vectors)
    both = lax.dynamic_update_slice(staged(in_hbm(vectors)), sib[None], (1, 0, 0))
    halo = carried([both] * 3)
    m1, m2, m3, give, plan, *held = k1(
        me, *lists, in_hbm(counts), both, in_hbm(near_blocks), in_hbm(far_left), in_hbm(far_right)
    )
    far_halo, halo_3, halo_1, m1 = lax.optimization_barrier((halo[1], halo[2], halo[0], m1))
    halo = (halo_1, far_halo, halo_3)
    r1, r2, r3, got, messages = exchange(m1, m2, m3, give)
    halo_post = swap(jnp.concatenate([halo[0], halo[1], halo[2][1:]]))
    halo_post, messages = lax.optimization_barrier((halo_post, messages))
    partial = k2(plan, both, *halo, halo_post, diag_blocks, *held)
    partial, r2, r3, r1 = lax.optimization_barrier((partial, r2, r3, r1))
    post = passed_on(r1, r2, r3)
    first_image, rounded, marked, m1, m2, m3, give = k3(partial, r1, r2, r3, post, got)
    f1, f2, f3, f_got, messages = exchange(m1, m2, m3, give)
    rounded, messages = lax.optimization_barrier((rounded, messages))
    m1, m2, m3, give = k4(plan, rounded, *held)
    f2, f3, f1, m1 = lax.optimization_barrier((f2, f3, f1, m1))
    r1, r2, r3, got, messages = exchange(m1, m2, m3, give)
    f_post = passed_on(f1, f2, f3)
    f_post, messages = lax.optimization_barrier((f_post, messages))
    partial = k5(plan, rounded, f1, f2, f3, f_post, f_got, diag_blocks, *held)
    partial, r2, r3, r1 = lax.optimization_barrier((partial, r2, r3, r1))
    post = passed_on(r1, r2, r3)
    return first_image, k6(partial, marked, r1, r2, r3, post, got)


def solution(mesh):
    return jax.shard_map(
        per_device,
        mesh=mesh,
        in_specs=(
            P(None, "rows"),
            P("rows", None, None),
            P("rows", None, None),
            P("rows"),
            P("rows"),
            P("rows", None, None),
            P("rows", None, None),
            P("rows"),
            P("rows"),
            P("rows", None),
        ),
        out_specs=(P(None, "rows"), P(None, "rows")),
        check_vma=False,
    )
```
